128 devices in a mesh: gx: 8 (over y, core), gy: 4 (over x), gz: 4 (over z).
Axes of the slice: x: 4, y: 4, z: 4, core: 2. Of those that a mesh axis runs over, the one named last changes fastest.
Arguments:
- velocity: float32 [128, 1024, 512], P('gx', 'gy', 'gz'), may hold values from -6 to 6
Outputs:
- detail_one: float32 [7, 64, 512, 256], P(None, 'gx', 'gy', 'gz')
- detail_two: float32 [7, 32, 256, 128], P(None, 'gx', 'gy', 'gz')
- detail_three: float32 [7, 16, 128, 64], P(None, 'gx', 'gy', 'gz')
- coarse_band: float32 [16, 128, 64], P('gx', 'gy', 'gz')
The draws below stay inside these ranges and needn't reach their ends.
All inputs are finite; a program needn't handle non-finite values.
Results may differ from the reference program's by a relative error of at most 0.000022.
Values sent between devices are 32-bit elements; how exact they have to be, the bound alone decides.
A program may use at most 64 MiB of HBM per device.

```python
import math
import jax
import jax.numpy as jnp
from jax import lax

NX = 128
NY = 1024
NZ = 512


def block_scale(key, extent, shards, low, largest):
    factor_of, own = 1.0, jax.random.fold_in(key, 6)
    for position, blocks in shards:
        steps = jnp.exp(jax.random.uniform(jax.random.fold_in(own, position), (blocks,), jnp.float32, low / len(shards), largest / len(shards)))
        factor_of = factor_of * jnp.repeat(steps, extent[position] // blocks).reshape([-1 if axis == position else 1 for axis in range(len(extent))])
    return factor_of


def bell_draw(stream_key, shape, deviation, bound, shards=(), kind=jnp.bfloat16):
    factor_of = block_scale(stream_key, shape, shards, -0.22, 0.18) if shards else 1.0
    drawn = jax.random.normal(stream_key, shape, jnp.float32) * deviation * factor_of
    return jnp.minimum(jnp.maximum(drawn, -bound), bound).astype(kind)


def setup_inputs(seed: int = 0) -> dict:
    streams_of = jax.random.split(jax.random.key(seed), 2)
    velocity = bell_draw(streams_of[0], (NX, NY, NZ), 1.0, 6.0, ((0, 8), (1, 4), (2, 4)), jnp.float32)
    return dict(velocity=velocity)


lift_alpha = -1.586134342059924
lift_beta = -0.052980118572961
lift_gamma = 0.882911075530934
lift_delta = 0.443506852043971
scale_low = math.sqrt(2.0) / 1.230174104914001
scale_high = 1.230174104914001 / math.sqrt(2.0)

def take_range(volume, start, stop, axis_dim):
    return lax.slice_in_dim(volume, start, stop, axis=axis_dim)

def split_parity(volume, axis_dim):
    half_len = volume.shape[axis_dim] // 2
    paired = volume.reshape(volume.shape[:axis_dim] + (half_len, 2) + volume.shape[axis_dim + 1:])
    return (lax.index_in_dim(paired, 0, axis_dim + 1, keepdims=False), lax.index_in_dim(paired, 1, axis_dim + 1, keepdims=False))

def ahead_of(evens, axis_dim, periodic):
    length = evens.shape[axis_dim]
    if periodic:
        tail_row = take_range(evens, 0, 1, axis_dim)
    else:
        tail_row = take_range(evens, length - 1, length, axis_dim)
    return jnp.concatenate([take_range(evens, 1, length, axis_dim), tail_row], axis=axis_dim)

def behind_of(odds, axis_dim, periodic):
    length = odds.shape[axis_dim]
    if periodic:
        head_row = take_range(odds, length - 1, length, axis_dim)
    else:
        head_row = take_range(odds, 0, 1, axis_dim)
    return jnp.concatenate([head_row, take_range(odds, 0, length - 1, axis_dim)], axis=axis_dim)

def lift_whole(volume, axis_dim, periodic):
    evens, odds = split_parity(volume, axis_dim)
    odds = odds + lift_alpha * (evens + ahead_of(evens, axis_dim, periodic))
    evens = evens + lift_beta * (behind_of(odds, axis_dim, periodic) + odds)
    odds = odds + lift_gamma * (evens + ahead_of(evens, axis_dim, periodic))
    evens = evens + lift_delta * (behind_of(odds, axis_dim, periodic) + odds)
    return (evens * scale_low, odds * scale_high)

def stack_bands(lowpass, highpass):
    band_count = lowpass.shape[0]
    return jnp.stack([lowpass, highpass], axis=1).reshape((2 * band_count,) + lowpass.shape[1:])

def reference(velocity):
    approx = velocity
    outputs = []
    for level_no in range(3):
        bands = approx[None]
        for axis_dim, periodic in ((1, True), (2, True), (3, False)):
            bands = stack_bands(*lift_whole(bands, axis_dim, periodic))
        outputs.append(bands[1:])
        approx = bands[0]
    return (outputs[0], outputs[1], outputs[2], approx)
```

```python
import math

import jax
import jax.numpy as jnp
import numpy as np
from jax import lax
from jax.experimental import pallas as pl
from jax.experimental.pallas import tpu as pltpu
from jax.sharding import PartitionSpec as P

ALPHA = -1.586134342059924
BETA = -0.052980118572961
GAMMA = 0.882911075530934
DELTA = 0.443506852043971
SCALE_LOW = math.sqrt(2.0) / 1.230174104914001
SCALE_HIGH = 1.230174104914001 / math.sqrt(2.0)


def lift_matrix(rows, edges):
    s, d = rows[0::2], rows[1::2]
    none = np.zeros_like(s[:1])
    if edges == "periodic":
        d = d + ALPHA * (s + np.roll(s, -1, 0))
        s = s + BETA * (np.roll(d, 1, 0) + d)
        d = d + GAMMA * (s + np.roll(s, -1, 0))
        s = s + DELTA * (np.roll(d, 1, 0) + d)
        return s, d
    start, end = edges
    up = lambda v, last: np.concatenate([v[1:], last])
    down = lambda v, first: np.concatenate([first, v[:-1]])
    d1 = d + ALPHA * (s + up(s, s[-1:] if end else none))
    before1 = d1[:1] if start else ALPHA * s[:1]
    s1 = s + BETA * (down(d1, before1) + d1)
    d2 = d1 + GAMMA * (s1 + up(s1, s1[-1:] if end else BETA * d1[-1:]))
    before2 = d2[:1] if start else before1 + GAMMA * (BETA * before1 + s1[:1])
    return s1 + DELTA * (down(d2, before2) + d2), d2


def path_matrix(rows, level, edges):
    for _ in range(level):
        rows, high = lift_matrix(rows, edges)
    return np.concatenate([rows, high])


def outgoing(n):
    rows, left, right = np.eye(n), [], []
    for _ in range(3):
        s, d = rows[0::2], rows[1::2]
        left += [s[0], s[0] + BETA * (d[0] + ALPHA * (s[0] + s[1]))]
        right += [d[-1] + ALPHA * s[-1], s[-1] + BETA * (d[-2] + ALPHA * (s[-2] + s[-1]))]
        rows = lift_matrix(rows, (False, False))[0]
    return np.stack(left), np.stack(right)


def line_blocks(n, level):
    m = n >> level
    rows = np.eye(5 * n)
    for _ in range(level):
        rows, high = lift_matrix(rows, "periodic")
    whole = np.concatenate([rows[2 * m : 3 * m], high[2 * m : 3 * m]])
    return [whole[:, k * n : (k + 1) * n] for k in range(5)]


def solved(target, basis):
    u = np.linalg.lstsq(basis.T, target.T, rcond=None)[0].T
    assert np.abs(u @ basis - target).max() < 1e-9
    return np.where(np.abs(u) < 1e-10, 0.0, u)


def block_plan(n, level):
    left, right = outgoing(n)
    left, right = left[: 2 * level], right[: 2 * level]
    blocks = line_blocks(n, level)
    alone = path_matrix(np.eye(n), level, (False, False))
    from_left = solved(blocks[1], right)
    from_right = solved(blocks[3], left)
    own = solved(blocks[2] - alone, np.concatenate([left, right]))
    return dict(left=left, right=right, alone=alone, from_left=from_left, from_right=from_right, own_left=own[:, : 2 * level], own_right=own[:, 2 * level :])


def mirror_plan(n, level, plan):
    out = []
    m = n >> level
    for start in (True, False):
        rows = np.eye(4 * n)
        for _ in range(level):
            rows, high = lift_matrix(rows, (True, True))
        at = 0 if start else 3
        whole = np.concatenate([rows[at * m : (at + 1) * m], high[at * m : (at + 1) * m]])
        whole = whole[:, at * n : (at + 1) * n]
        rest = whole - plan["alone"] - plan["own_left"] @ plan["left"] - plan["own_right"] @ plan["right"]
        u = plan["from_left"] if start else plan["from_right"]
        g = np.linalg.lstsq(u, rest, rcond=None)[0]
        assert np.abs(u @ g - rest).max() < 1e-9
        out.append(np.where(np.abs(g) < 1e-10, 0.0, g))
    return out


MESH = pl.DeviceIdType.MESH
SIZES = {"gx": 8, "gy": 4, "gz": 4}
NX, NY, NZ = 16, 256, 128
F32 = jnp.float32


def rounded(matrix):
    return [[float(np.float32(c)) if abs(c) > 1e-10 else 0.0 for c in row] for row in matrix]


def fir(weights, rows):
    total = None
    for weight, row in zip(weights, rows):
        if weight == 0.0:
            continue
        term = row() if callable(row) else row
        term = term if weight == 1.0 else weight * term
        total = term if total is None else total + term
    return total


def lift_list(s, d, up, down, first, last):
    before1 = ALPHA * first(s)
    d1 = [b + ALPHA * (a + c) for a, b, c in zip(s, d, up(s, None))]
    s1 = [a + BETA * (b + c) for a, b, c in zip(s, d1, down(d1, before1))]
    d2 = [b + GAMMA * (a + c) for a, b, c in zip(s1, d1, up(s1, BETA * last(d1)))]
    before2 = before1 + GAMMA * (BETA * before1 + first(s1))
    s2 = [a + DELTA * (b + c) for a, b, c in zip(s1, d2, down(d2, before2))]
    return s2, d2


def lift_rows(src, base, n, dst, to, keep_high=True):
    k = n // 16
    s = [src[pl.ds(base + 16 * i, 8, stride=2), :] for i in range(k)]
    d = [src[pl.ds(base + 16 * i + 1, 8, stride=2), :] for i in range(k)]
    sub = lax.broadcasted_iota(jnp.int32, (8, 128), 0)
    top, bottom = sub == 0, sub == 7

    def up(v, fill):
        r = [pltpu.roll(x, 7, 0) for x in v]
        fill = jnp.zeros((8, 128), F32) if fill is None else fill
        return [jnp.where(bottom, r[i + 1] if i + 1 < k else fill, r[i]) for i in range(k)]

    def down(v, fill):
        r = [pltpu.roll(x, 1, 0) for x in v]
        return [jnp.where(top, r[i - 1] if i else fill, r[i]) for i in range(k)]

    low, high = lift_list(s, d, up, down, lambda v: v[0], lambda v: v[-1])
    for i in range(k):
        dst[pl.ds(to + 8 * i, 8), :] = low[i]
        if keep_high:
            dst[pl.ds(to + 8 * (k + i), 8), :] = high[i]


def lift_major(rows):
    low, high = lift_list(
        rows[0::2],
        rows[1::2],
        lambda v, fill: v[1:] + [jnp.zeros_like(v[0]) if fill is None else fill],
        lambda v, fill: [fill] + v[:-1],
        lambda v: v[0],
        lambda v: v[-1],
    )
    return low + high


class Side:
    def __init__(self, plan):
        self.groups = {}
        for source in ("from_left", "from_right", "own_left", "own_right"):
            u = plan[source]
            for g in range(u.shape[0] // 8):
                for f in range(u.shape[1]):
                    column = u[8 * g : 8 * g + 8, f]
                    if np.abs(column).max() > 1e-10:
                        self.groups.setdefault(g, []).append((source, f, column))


PLANS = {n: [block_plan(n, level) for level in (1, 2, 3)] for n in (NY, NZ)}
SIDES = {n: [Side(plan) for plan in PLANS[n]] for n in (NY, NZ)}
MIRRORS = [mirror_plan(NZ, level, PLANS[NZ][level - 1]) for level in (1, 2, 3)]
SEND_LEFT = {n: rounded(PLANS[n][2]["left"]) for n in (NY, NZ)}
SEND_RIGHT = {n: rounded(PLANS[n][2]["right"]) for n in (NY, NZ)}
SCALES = [(SCALE_LOW**level, SCALE_LOW ** (level - 1) * SCALE_HIGH) for level in (1, 2, 3)]


def factored(matrix):
    u, size, v = np.linalg.svd(matrix, full_matrices=False)
    rank = int((size > 1e-9).sum())
    return rounded(u[:, :rank] * size[:rank]), rounded(v[:rank])


X_ONE = block_plan(NX, 1)
X_ONE_LEFT, X_ONE_RIGHT = rounded(X_ONE["left"]), rounded(X_ONE["right"])
X_ONE_FROM_LEFT, X_ONE_FROM_RIGHT = rounded(X_ONE["from_left"]), rounded(X_ONE["from_right"])
X_TWO_BLOCKS = line_blocks(NX, 2)
X_TWO_FROM_LEFT, X_TWO_RIGHT = factored(X_TWO_BLOCKS[1])
X_TWO_FROM_RIGHT, X_TWO_LEFT = factored(X_TWO_BLOCKS[3])
X_TWO_OWN = rounded(X_TWO_BLOCKS[2])
X_THREE = [rounded(block) for block in line_blocks(NX, 3)]
N_TWO = len(X_TWO_RIGHT)

Y_ROWS = 6 * NX
Z_TWO, Z_THREE, Z_ROWS = 4 * NX, 8 * NX, 8 * NX + 6 * (NX // 2)
X23_ROWS = N_TWO * 64 + 64


def neighbour(axis, step):
    size = SIZES[axis]
    place = {name: lax.axis_index(name) for name in SIZES}
    place[axis] = lax.rem(place[axis] + (step + size), size)
    return tuple(place[name] for name in ("gx", "gy", "gz"))


def build_table(table, sides):
    sub = lax.broadcasted_iota(jnp.int32, (8, 128), 0)
    found = []
    at = 0
    for side in sides:
        places = {}
        for g, terms in side.groups.items():
            for source, f, column in terms:
                value = jnp.zeros((8, 128), F32)
                for i in range(8):
                    if abs(column[i]) > 1e-10:
                        value = jnp.where(sub == i, float(np.float32(column[i])), value)
                table[pl.ds(at, 8), :] = value
                places[g, source, f] = at
                at += 8
        found.append(places)
    return found


def table_rows(sides):
    return 8 * sum(len(terms) for side in sides for terms in side.groups.values())


def correct(ref, base, side, places, table, rows_of):
    for g, terms in side.groups.items():
        value = ref[pl.ds(base + 8 * g, 8), :]
        for source, f, _ in terms:
            value = value + table[pl.ds(places[g, source, f], 8), :] * rows_of(source, f)
        ref[pl.ds(base + 8 * g, 8), :] = value


def kernel(
    vel, out1, out2, out3, out4,
    v, y1, y2, y3, z1, z2, z3, w1, w2, w3, t2, t3, t4, ytab, ztab,
    ysl, ysr, yrl, yrr, zsl, zsr, zrl, zrr, zml, zmr,
    x1sl, x1sr, x1rl, x1rr, x23sl, x23sr, x23rl, x23rr, x3sl, x3sr, x3rl, x3rr,
    load_sem, send_sems, recv_sems,
):
    load = pltpu.make_async_copy(vel, v, load_sem)
    load.start()
    near = {
        "yl": neighbour("gy", -1), "yr": neighbour("gy", 1), "zl": neighbour("gz", -1), "zr": neighbour("gz", 1),
        "xl": neighbour("gx", -1), "xr": neighbour("gx", 1), "xll": neighbour("gx", -2), "xrr": neighbour("gx", 2),
    }
    barrier = pltpu.get_barrier_semaphore()
    for device in near.values():
        pl.semaphore_signal(barrier, inc=1, device_id=device, device_id_type=MESH)
    y_places = build_table(ytab, SIDES[NY])
    z_places = build_table(ztab, SIDES[NZ])

    def remote(index, src, dst, to):
        return pltpu.make_async_remote_copy(
            src_ref=src,
            dst_ref=dst,
            send_sem=send_sems.at[index],
            recv_sem=recv_sems.at[index],
            device_id=near[to],
            device_id_type=MESH,
        )

    load.wait()

    for h in range(2):
        head = [v[pl.ds(h * 8 * NY + k, 8, stride=NY), :] for k in range(21)]
        tail = [v[pl.ds(h * 8 * NY + k, 8, stride=NY), :] for k in range(NY - 28, NY)]
        for f in range(6):
            ysl[pl.ds(f * NX + 8 * h, 8), :] = fir(SEND_LEFT[NY][f][:21], head)
            ysr[pl.ds(f * NX + 8 * h, 8), :] = fir(SEND_RIGHT[NY][f][-28:], tail)
    pl.semaphore_wait(barrier, len(near))
    y_left = remote(0, ysl, yrr, "yl")
    y_right = remote(1, ysr, yrl, "yr")
    y_left.start()
    y_right.start()

    def lift_y(x, c):
        lift_rows(v, x * NY, NY, y1, x * NY)
        lift_rows(y1, x * NY, NY // 2, y2, x * (NY // 2))
        lift_rows(y2, x * (NY // 2), NY // 4, y3, x * (NY // 4))
        return c

    lax.fori_loop(0, NX, lift_y, 0)
    y_left.wait()
    y_right.wait()

    def finish_y(x, c):
        def rows_of(source, f):
            ref = {"from_left": yrl, "from_right": yrr, "own_left": ysl, "own_right": ysr}[source]
            return ref[pl.ds(f * NX + x, 1), :]

        for level, ref in enumerate((y1, y2, y3)):
            correct(ref, x * (NY >> level), SIDES[NY][level], y_places[level], ytab, rows_of)
        for t in range(2):
            z1[pl.ds(x * 256 + 128 * t, 128), :] = y1[pl.ds(x * NY + 128 * t, 128), :].T
        z2[pl.ds(x * 128, 128), :] = y2[pl.ds(x * 128, 128), :].T
        return c

    lax.fori_loop(0, NX, finish_y, 0)

    def turn_three(p, c):
        z3[pl.ds(p * 128, 128), :] = y3[pl.ds(p * 128, 128), :].T
        return c

    lax.fori_loop(0, NX // 2, turn_three, 0)

    def z_sums(level, load_row, store):
        left, right = SEND_LEFT[NZ][: 2 * level], SEND_RIGHT[NZ][: 2 * level]
        start, end = (rounded(m) for m in MIRRORS[level - 1])
        rows = {}

        def row(k):
            if k not in rows:
                rows[k] = load_row(k)
            return rows[k]

        for f in range(2 * level):
            for ref, weights in ((zsl, left), (zsr, right), (zml, start), (zmr, end)):
                ks = [k for k in range(NZ) if weights[f][k] != 0.0]
                store(ref, f, fir([weights[f][k] for k in ks], [row(k) for k in ks]))

    for h in range(2):
        for t in range(2):

            def store_one(ref, f, value, h=h, t=t):
                ref[pl.ds((f * 2 + t) * NX + 8 * h, 8), :] = value

            z_sums(1, lambda k, h=h, t=t: z1[pl.ds(h * 8 * 256 + t * 128 + k, 8, stride=256), :], store_one)

        def store_two(ref, f, value, h=h):
            ref[pl.ds(Z_TWO + f * NX + 8 * h, 8), :] = value

        z_sums(2, lambda k, h=h: z2[pl.ds(h * 8 * 128 + k, 8, stride=128), :], store_two)

    def store_three(ref, f, value):
        ref[pl.ds(Z_THREE + f * (NX // 2), 8), :] = value

    z_sums(3, lambda k: z3[pl.ds(k, 8, stride=128), :], store_three)
    z_left = remote(2, zsl, zrr, "zl")
    z_right = remote(3, zsr, zrl, "zr")
    z_left.start()
    z_right.start()

    def lift_z1(i, c):
        lift_rows(z1, i * NZ, NZ, w1, i * NZ)
        return c

    def lift_z2(x, c):
        lift_rows(z2, x * NZ, NZ, t2, x * 64, keep_high=False)
        lift_rows(t2, x * 64, 64, w2, x * 64)
        return c

    def lift_z3(p, c):
        lift_rows(z3, p * NZ, NZ, t3, p * 64, keep_high=False)
        lift_rows(t3, p * 64, 64, t4, p * 32, keep_high=False)
        lift_rows(t4, p * 32, 32, w3, p * 32)
        return c

    lax.fori_loop(0, 2 * NX, lift_z1, 0)
    lax.fori_loop(0, NX, lift_z2, 0)
    lax.fori_loop(0, NX // 2, lift_z3, 0)
    z_left.wait()
    z_right.wait()
    gz = lax.axis_index("gz")

    @pl.when(gz == 0)
    def _():
        zrl[...] = zml[...]

    @pl.when(gz == SIZES["gz"] - 1)
    def _():
        zrr[...] = zmr[...]

    z_refs = {"from_left": zrl, "from_right": zrr, "own_left": zsl, "own_right": zsr}

    def finish_z2(x, c):
        correct(w2, x * 64, SIDES[NZ][1], z_places[1], ztab, lambda s, f: z_refs[s][pl.ds(Z_TWO + f * NX + x, 1), :])
        return c

    def finish_z3(p, c):
        correct(w3, p * 32, SIDES[NZ][2], z_places[2], ztab, lambda s, f: z_refs[s][pl.ds(Z_THREE + f * 8 + p, 1), :])
        return c

    def finish_z1(x, c):
        for t in range(2):
            correct(
                w1, x * 256 + 128 * t, SIDES[NZ][0], z_places[0], ztab,
                lambda s, f, t=t: z_refs[s][pl.ds((f * 2 + t) * NX + x, 1), :],
            )
        return c

    lax.fori_loop(0, NX, finish_z2, 0)
    lax.fori_loop(0, NX // 2, finish_z3, 0)

    lane = lax.broadcasted_iota(jnp.int32, (8, 128), 1)
    low_lanes = lane < 64

    def sums_two(g, c):
        rows = [w2[pl.ds(x * 64 + 8 * g, 8), :] for x in range(NX)]
        for f in range(N_TWO):
            x23sl[pl.ds(f * 64 + 8 * g, 8), :] = fir(X_TWO_LEFT[f], rows)
            x23sr[pl.ds(f * 64 + 8 * g, 8), :] = fir(X_TWO_RIGHT[f], rows)
        return c

    def paired(weights, rows):
        total = jnp.zeros((8, 128), F32)
        for p in range(NX // 2):
            if weights[2 * p] == 0.0 and weights[2 * p + 1] == 0.0:
                continue
            total = total + jnp.where(low_lanes, weights[2 * p], weights[2 * p + 1]) * rows[p]
        return total + pltpu.roll(total, 64, 1)

    def sums_three(matrix, rows):
        return [
            jnp.where(low_lanes, paired(matrix[2 * h], rows), paired(matrix[2 * h + 1], rows)) for h in range(2)
        ]

    def send_three(g, c):
        rows = [w3[pl.ds(p * 32 + 8 * g, 8), :] for p in range(NX // 2)]
        for ref, block, at in ((x23sr, 1, N_TWO * 64), (x23sl, 3, N_TWO * 64), (x3sr, 0, 0), (x3sl, 4, 0)):
            for h, value in enumerate(sums_three(X_THREE[block], rows)):
                ref[pl.ds(at + 32 * h + 8 * g, 8), :] = value
        return c

    lax.fori_loop(0, 8, sums_two, 0)
    lax.fori_loop(0, 4, send_three, 0)
    x23_left = remote(4, x23sl, x23rr, "xl")
    x23_right = remote(5, x23sr, x23rl, "xr")
    x3_left = remote(6, x3sl, x3rr, "xll")
    x3_right = remote(7, x3sr, x3rl, "xrr")
    for copy in (x23_left, x23_right, x3_left, x3_right):
        copy.start()
    lax.fori_loop(0, NX, finish_z1, 0)

    def sums_one(g, c):
        rows = [w1[pl.ds(x * 256 + 8 * g, 8), :] for x in range(NX)]
        for f in range(2):
            x1sl[pl.ds(f * 256 + 8 * g, 8), :] = fir(X_ONE_LEFT[f], rows)
            x1sr[pl.ds(f * 256 + 8 * g, 8), :] = fir(X_ONE_RIGHT[f], rows)
        return c

    lax.fori_loop(0, 32, sums_one, 0)
    x1_left = remote(8, x1sl, x1rr, "xl")
    x1_right = remote(9, x1sr, x1rl, "xr")
    x1_left.start()
    x1_right.start()

    for copy in (x23_left, x23_right, x3_left, x3_right):
        copy.wait()

    def out_three(g, hz):
        rows = [w3[pl.ds(p * 32 + 8 * g, 8), :] for p in range(NX // 2)]
        own = sums_three(X_THREE[2], rows)
        high_y = (lane % 64) >= 32
        for hx in range(2):
            value = own[hx]
            for ref, at in ((x23rl, N_TWO * 64), (x23rr, N_TWO * 64), (x3rl, 0), (x3rr, 0)):
                value = value + ref[pl.ds(at + 32 * hx + 8 * g, 8), :]
            scale = SCALES[2][hx] * SCALES[2][hz]
            value = value * jnp.where(high_y, scale * SCALES[2][1], scale * SCALES[2][0])
            for q in range(4):
                i, hy = divmod(q, 2)
                band = 4 * hx + 2 * hy + hz
                row = 16 * i + 8 * (g % 2)
                piece = value[:, 32 * q : 32 * q + 32]
                if band:
                    out3[pl.ds((band - 1) * 32 + row, 8), :] = piece
                else:
                    out4[pl.ds(row, 8), :] = piece

    for g in range(4):
        out_three(g, g // 2)

    def out_two(g, hz):
        rows = [w2[pl.ds(x * 64 + 8 * g, 8), :] for x in range(NX)]
        left = [x23rl[pl.ds(f * 64 + 8 * g, 8), :] for f in range(N_TWO)]
        right = [x23rr[pl.ds(f * 64 + 8 * g, 8), :] for f in range(N_TWO)]
        for i in range(8):
            hx = i // 4
            value = fir(X_TWO_OWN[i] + X_TWO_FROM_LEFT[i] + X_TWO_FROM_RIGHT[i], rows + left + right)
            scale = SCALES[1][hx] * SCALES[1][hz]
            value = value * jnp.where(low_lanes, scale * SCALES[1][0], scale * SCALES[1][1])
            for hy in range(2):
                band = 4 * hx + 2 * hy + hz
                if band:
                    at = (band - 1) * 128 + (i % 4) * 32 + 8 * (g % 4)
                    out2[pl.ds(at, 8), :] = value[:, 64 * hy : 64 * hy + 64]

    for g in range(8):
        out_two(g, g // 4)

    x1_left.wait()
    x1_right.wait()

    for hy in range(2):
        for hz in range(2):

            def out_one(g, c, hy=hy, hz=hz):
                row = 128 * hy + 64 * hz + 8 * g
                rows = [w1[pl.ds(x * 256 + row, 8), :] for x in range(NX)]
                left = [x1rl[pl.ds(f * 256 + row, 8), :] for f in range(2)]
                right = [x1rr[pl.ds(f * 256 + row, 8), :] for f in range(2)]
                for i, value in enumerate(lift_major(rows)):
                    hx = i // 8
                    band = 4 * hx + 2 * hy + hz
                    if not band:
                        continue
                    value = fir([1.0] + X_ONE_FROM_LEFT[i] + X_ONE_FROM_RIGHT[i], [value] + left + right)
                    value = value * (SCALES[0][hx] * SCALES[0][hy] * SCALES[0][hz])
                    out1[pl.ds((band - 1) * 512 + (i % 8) * 64 + 8 * g, 8), :] = value
                return c

            lax.fori_loop(0, 8, out_one, 0)


def rows_of_scratch():
    rows = [16 * NY, 16 * NY, 16 * NY // 2, 16 * NY // 4]
    rows += [32 * NZ, 16 * NZ, 8 * NZ]
    rows += [32 * NZ, 16 * 64, 8 * 32]
    rows += [16 * 64, 8 * 64, 8 * 32]
    rows += [table_rows(SIDES[NY]), table_rows(SIDES[NZ])]
    rows += [Y_ROWS] * 4 + [Z_ROWS] * 6 + [512] * 4 + [X23_ROWS] * 4 + [64] * 4
    return rows


def shards(velocity):
    shapes = [(7 * 8 * 64, 128), (7 * 4 * 32, 64), (7 * 2 * 16, 32), (2 * 16, 32)]
    out1, out2, out3, out4 = pl.pallas_call(
        kernel,
        out_shape=[jax.ShapeDtypeStruct(shape, F32) for shape in shapes],
        in_specs=[pl.BlockSpec(memory_space=pl.ANY)],
        out_specs=[pl.BlockSpec(memory_space=pltpu.VMEM)] * 4,
        scratch_shapes=[pltpu.VMEM((rows, 128), F32) for rows in rows_of_scratch()]
        + [pltpu.SemaphoreType.DMA, pltpu.SemaphoreType.DMA((10,)), pltpu.SemaphoreType.DMA((10,))],
        compiler_params=pltpu.CompilerParams(collective_id=0, has_side_effects=True, vmem_limit_bytes=40 * 2**20),
    )(velocity.reshape(NX * NY, NZ))
    return (
        out1.reshape(7, 8, 64, 128).transpose(0, 1, 3, 2),
        out2.reshape(7, 4, 32, 64).transpose(0, 1, 3, 2),
        out3.reshape(7, 2, 16, 32).transpose(0, 1, 3, 2),
        out4.reshape(2, 16, 32).transpose(0, 2, 1),
    )


def solution(mesh):
    return jax.shard_map(
        shards,
        mesh=mesh,
        in_specs=(P("gx", "gy", "gz"),),
        out_specs=(
            P(None, "gx", "gy", "gz"),
            P(None, "gx", "gy", "gz"),
            P(None, "gx", "gy", "gz"),
            P("gx", "gy", "gz"),
        ),
        check_vma=False,
    )
```

```python
import math

import jax
import jax.numpy as jnp
import ml_dtypes
import numpy as np
from jax import lax
from jax.experimental import pallas as pl
from jax.experimental.pallas import tpu as pltpu
from jax.sharding import PartitionSpec as P

ALPHA = -1.586134342059924
BETA = -0.052980118572961
GAMMA = 0.882911075530934
DELTA = 0.443506852043971
SCALE_LOW = math.sqrt(2.0) / 1.230174104914001
SCALE_HIGH = 1.230174104914001 / math.sqrt(2.0)


def lift_matrix(rows, edges):
    s, d = rows[0::2], rows[1::2]
    none = np.zeros_like(s[:1])
    if edges == "periodic":
        d = d + ALPHA * (s + np.roll(s, -1, 0))
        s = s + BETA * (np.roll(d, 1, 0) + d)
        d = d + GAMMA * (s + np.roll(s, -1, 0))
        s = s + DELTA * (np.roll(d, 1, 0) + d)
        return s, d
    start, end = edges
    up = lambda v, last: np.concatenate([v[1:], last])
    down = lambda v, first: np.concatenate([first, v[:-1]])
    d1 = d + ALPHA * (s + up(s, s[-1:] if end else none))
    before1 = d1[:1] if start else ALPHA * s[:1]
    s1 = s + BETA * (down(d1, before1) + d1)
    d2 = d1 + GAMMA * (s1 + up(s1, s1[-1:] if end else BETA * d1[-1:]))
    before2 = d2[:1] if start else before1 + GAMMA * (BETA * before1 + s1[:1])
    return s1 + DELTA * (down(d2, before2) + d2), d2


def path_matrix(rows, level, edges):
    for _ in range(level):
        rows, high = lift_matrix(rows, edges)
    return np.concatenate([rows, high])


def outgoing(n):
    rows, left, right = np.eye(n), [], []
    for _ in range(3):
        s, d = rows[0::2], rows[1::2]
        left += [s[0], s[0] + BETA * (d[0] + ALPHA * (s[0] + s[1]))]
        right += [d[-1] + ALPHA * s[-1], s[-1] + BETA * (d[-2] + ALPHA * (s[-2] + s[-1]))]
        rows = lift_matrix(rows, (False, False))[0]
    return np.stack(left), np.stack(right)


def line_blocks(n, level):
    m = n >> level
    rows = np.eye(5 * n)
    for _ in range(level):
        rows, high = lift_matrix(rows, "periodic")
    whole = np.concatenate([rows[2 * m : 3 * m], high[2 * m : 3 * m]])
    return [whole[:, k * n : (k + 1) * n] for k in range(5)]


def solved(target, basis):
    u = np.linalg.lstsq(basis.T, target.T, rcond=None)[0].T
    assert np.abs(u @ basis - target).max() < 1e-9
    return np.where(np.abs(u) < 1e-10, 0.0, u)


def block_plan(n, level):
    left, right = outgoing(n)
    left, right = left[: 2 * level], right[: 2 * level]
    blocks = line_blocks(n, level)
    alone = path_matrix(np.eye(n), level, (False, False))
    from_left = solved(blocks[1], right)
    from_right = solved(blocks[3], left)
    own = solved(blocks[2] - alone, np.concatenate([left, right]))
    return dict(left=left, right=right, alone=alone, from_left=from_left, from_right=from_right, own_left=own[:, : 2 * level], own_right=own[:, 2 * level :])


def mirror_plan(n, plans):
    out = []
    for start in (True, False):
        uses, rests = [], []
        for level, plan in enumerate(plans, 1):
            m = n >> level
            rows = np.eye(4 * n)
            for _ in range(level):
                rows, high = lift_matrix(rows, (True, True))
            at = 0 if start else 3
            whole = np.concatenate([rows[at * m : (at + 1) * m], high[at * m : (at + 1) * m]])
            whole = whole[:, at * n : (at + 1) * n]
            rests.append(whole - plan["alone"] - plan["own_left"] @ plan["left"] - plan["own_right"] @ plan["right"])
            u = plan["from_left"] if start else plan["from_right"]
            uses.append(np.pad(u, ((0, 0), (0, 6 - u.shape[1]))))
        use, rest = np.concatenate(uses), np.concatenate(rests)
        g = np.linalg.lstsq(use, rest, rcond=None)[0]
        assert np.abs(use @ g - rest).max() < 1e-9
        out.append(np.where(np.abs(g) < 1e-10, 0.0, g))
    return out


MESH = pl.DeviceIdType.MESH
SIZES = {"gx": 8, "gy": 4, "gz": 4}
NX, NY, NZ = 16, 256, 128
F32 = jnp.float32


def rounded(matrix):
    return [[float(np.float32(c)) if abs(c) > 1e-10 else 0.0 for c in row] for row in matrix]


def fir(weights, rows):
    total = None
    for weight, row in zip(weights, rows):
        if weight == 0.0:
            continue
        term = row() if callable(row) else row
        term = term if weight == 1.0 else weight * term
        total = term if total is None else total + term
    return total


def lift_list(s, d, up, down, first, last):
    before1 = ALPHA * first(s)
    d1 = [b + ALPHA * (a + c) for a, b, c in zip(s, d, up(s, None))]
    s1 = [a + BETA * (b + c) for a, b, c in zip(s, d1, down(d1, before1))]
    d2 = [b + GAMMA * (a + c) for a, b, c in zip(s1, d1, up(s1, BETA * last(d1)))]
    before2 = before1 + GAMMA * (BETA * before1 + first(s1))
    s2 = [a + DELTA * (b + c) for a, b, c in zip(s1, d2, down(d2, before2))]
    return s2, d2


def lift_rows(src, base, n, dst, to, keep_high=True):
    k = n // 16
    s = [src[pl.ds(base + 16 * i, 8, stride=2), :] for i in range(k)]
    d = [src[pl.ds(base + 16 * i + 1, 8, stride=2), :] for i in range(k)]
    sub = lax.broadcasted_iota(jnp.int32, (8, 128), 0)
    top, bottom = sub == 0, sub == 7

    def up(v, fill):
        r = [pltpu.roll(x, 7, 0) for x in v]
        fill = jnp.zeros((8, 128), F32) if fill is None else fill
        return [jnp.where(bottom, r[i + 1] if i + 1 < k else fill, r[i]) for i in range(k)]

    def down(v, fill):
        r = [pltpu.roll(x, 1, 0) for x in v]
        return [jnp.where(top, r[i - 1] if i else fill, r[i]) for i in range(k)]

    low, high = lift_list(s, d, up, down, lambda v: v[0], lambda v: v[-1])
    for i in range(k):
        dst[pl.ds(to + 8 * i, 8), :] = low[i]
        if keep_high:
            dst[pl.ds(to + 8 * (k + i), 8), :] = high[i]


def lift_major(rows):
    low, high = lift_list(
        rows[0::2],
        rows[1::2],
        lambda v, fill: v[1:] + [jnp.zeros_like(v[0]) if fill is None else fill],
        lambda v, fill: [fill] + v[:-1],
        lambda v: v[0],
        lambda v: v[-1],
    )
    return low + high


class Side:
    def __init__(self, plan):
        self.groups = {}
        for source in ("from_left", "from_right", "own_left", "own_right"):
            u = plan[source]
            for g in range(u.shape[0] // 8):
                for f in range(u.shape[1]):
                    column = u[8 * g : 8 * g + 8, f]
                    if np.abs(column).max() > 1e-10:
                        self.groups.setdefault(g, []).append((source, f, column))


PLANS = {n: [block_plan(n, level) for level in (1, 2, 3)] for n in (NY, NZ)}
SIDES = {n: [Side(plan) for plan in PLANS[n]] for n in (NY, NZ)}
MIRRORS = mirror_plan(NZ, PLANS[NZ])
SEND_LEFT = {n: rounded(PLANS[n][2]["left"]) for n in (NY, NZ)}
SEND_RIGHT = {n: rounded(PLANS[n][2]["right"]) for n in (NY, NZ)}
SCALES = [(SCALE_LOW**level, SCALE_LOW ** (level - 1) * SCALE_HIGH) for level in (1, 2, 3)]


def factored(matrix):
    u, size, v = np.linalg.svd(matrix, full_matrices=False)
    rank = int((size > 1e-9).sum())
    return rounded(u[:, :rank] * size[:rank]), rounded(v[:rank])


X_ONE = block_plan(NX, 1)
X_ONE_LEFT, X_ONE_RIGHT = rounded(X_ONE["left"]), rounded(X_ONE["right"])
X_ONE_FROM_LEFT, X_ONE_FROM_RIGHT = rounded(X_ONE["from_left"]), rounded(X_ONE["from_right"])
X_TWO_BLOCKS = line_blocks(NX, 2)
X_TWO_FROM_LEFT, X_TWO_RIGHT = factored(X_TWO_BLOCKS[1])
X_TWO_FROM_RIGHT, X_TWO_LEFT = factored(X_TWO_BLOCKS[3])
X_TWO_OWN = rounded(X_TWO_BLOCKS[2])
X_THREE = [rounded(block) for block in line_blocks(NX, 3)]
N_TWO = len(X_TWO_RIGHT)

Y_ROWS = 6 * NX
Z_TWO, Z_THREE, Z_ROWS = 4 * NX, 8 * NX, 8 * NX + 6 * (NX // 2)
X23_ROWS = N_TWO * 64 + 64


def neighbour(axis, step):
    size = SIZES[axis]
    place = {name: lax.axis_index(name) for name in SIZES}
    place[axis] = lax.rem(place[axis] + (step + size), size)
    return tuple(place[name] for name in ("gx", "gy", "gz"))


def build_table(table, sides):
    sub = lax.broadcasted_iota(jnp.int32, (8, 128), 0)
    found = []
    at = 0
    for side in sides:
        places = {}
        for g, terms in side.groups.items():
            for source, f, column in terms:
                value = jnp.zeros((8, 128), F32)
                for i in range(8):
                    if abs(column[i]) > 1e-10:
                        value = jnp.where(sub == i, float(np.float32(column[i])), value)
                table[pl.ds(at, 8), :] = value
                places[g, source, f] = at
                at += 8
        found.append(places)
    return found


def table_rows(sides):
    return 8 * sum(len(terms) for side in sides for terms in side.groups.values())


def correct(ref, base, side, places, table, refs, row):
    for g, terms in side.groups.items():
        terms = [(source, f) for source, f, _ in terms if source in refs]
        if not terms:
            continue
        value = ref[pl.ds(base + 8 * g, 8), :]
        for source, f in terms:
            value = value + table[pl.ds(places[g, source, f], 8), :] * refs[source][pl.ds(row(f), 1), :]
        ref[pl.ds(base + 8 * g, 8), :] = value


def parts_of(value):
    rest, parts = np.asarray(value, np.float32), []
    for _ in range(3):
        part = rest.astype(ml_dtypes.bfloat16)
        parts.append(part)
        rest = rest - part.astype(np.float32)
    return parts


def spread(level):
    plan = PLANS[NY][level - 1]
    left, right = plan["from_left"].T, plan["from_right"].T
    if level == 3:
        blocks = []
        for u in (left, right):
            block = np.zeros((8, NX, 128))
            block[:6, 0::2, :64] = u[:, None, :]
            block[:6, 1::2, 64:] = u[:, None, :]
            blocks.append(block.reshape(128, 128))
        matrix = np.concatenate(blocks)
    else:
        matrix = np.repeat(np.concatenate([left, right]), NX, axis=0)
    one, two, three = parts_of(matrix)
    return np.concatenate([one, two, three, one, two, one])


SPREADS = [spread(level) for level in (1, 2, 3)]
Z_SENDS = np.zeros((32, NZ), np.float32)
for _at, _rows in enumerate((PLANS[NZ][2]["left"], PLANS[NZ][2]["right"], *MIRRORS)):
    Z_SENDS[8 * _at : 8 * _at + 6] = _rows


def split(value):
    one = value.astype(jnp.bfloat16).astype(F32)
    two = (value - one).astype(jnp.bfloat16).astype(F32)
    return one, two, value - one - two


def lanes_of(shape):
    return lax.broadcasted_iota(jnp.int32, shape, 1)


def slots(level, left, right):
    lane = lanes_of(left.shape)
    turn = lambda value, by: pltpu.roll(value, by, 1)
    if level == 1:
        one, two, three = split(jnp.where(lane < 32, left, jnp.where(lane < 64, turn(right, 32), 0.0)))
        return [one + turn(one, 64), one + turn(two, 64), two + turn(three, 64)]
    if level == 2:
        one, two, three = split(jnp.where(lane < 64, left, turn(right, 64)))
        return [one, one, one, two, two, three]
    one, two, three = zip(split(left), split(right))
    return [*one, *one, *one, *two, *two, *three]


def expand(level, arrays, keep, spread_ref):
    factor = jnp.concatenate([jnp.where(keep, a, 0.0).astype(jnp.bfloat16) for a in arrays], axis=1)
    return jnp.dot(factor, spread_ref[...], preferred_element_type=F32)


def kernel(
    vel, spread1_hbm, spread2_hbm, spread3_hbm, sends_hbm,
    w1, w2, w3, x1rl, x1rr, x23rl, x23rr, x3rl, x3rr,
    v, y1, y2, y3, z1, z2, z3, t2, t3, t4, ytab, ztab,
    ysl, ysr, yrl, yrr, zsl, zsr, zrl, zrr, zml, zmr,
    htl, htr, g1, g2, g3, u2, u3, p1, p2, p3, zlsl, zlsr, zlrl, zlrr, zlml, zlmr,
    x1sl, x1sr, x23sl, x23sr, x3sl, x3sr, xesl, xesr, xerl, xerr,
    spread1, spread2, spread3, sends,
    load_sems, send_sems, recv_sems,
):
    loads = [
        pltpu.make_async_copy(src, dst, load_sems.at[i])
        for i, (src, dst) in enumerate(
            ((vel, v), (sends_hbm, sends), (spread1_hbm, spread1), (spread2_hbm, spread2), (spread3_hbm, spread3))
        )
    ]
    for load in loads:
        load.start()
    near = {
        "yl": neighbour("gy", -1), "yr": neighbour("gy", 1), "zl": neighbour("gz", -1), "zr": neighbour("gz", 1),
        "xl": neighbour("gx", -1), "xr": neighbour("gx", 1), "xll": neighbour("gx", -2), "xrr": neighbour("gx", 2),
    }
    barrier = pltpu.get_barrier_semaphore()
    for device in near.values():
        pl.semaphore_signal(barrier, inc=1, device_id=device, device_id_type=MESH)
    y_places = build_table(ytab, SIDES[NY])
    z_places = build_table(ztab, SIDES[NZ])
    for ref in (yrl, yrr):
        ref[pl.ds(Y_ROWS, 32), :] = jnp.zeros((32, 128), F32)

    def remote(index, src, dst, to):
        return pltpu.make_async_remote_copy(
            src_ref=src,
            dst_ref=dst,
            send_sem=send_sems.at[index],
            recv_sem=recv_sems.at[index],
            device_id=near[to],
            device_id_type=MESH,
        )

    loads[0].wait()

    for h in range(2):
        head = [v[pl.ds(h * 8 * NY + k, 8, stride=NY), :] for k in range(21)]
        tail = [v[pl.ds(h * 8 * NY + k, 8, stride=NY), :] for k in range(NY - 28, NY)]
        for f in range(6):
            ysl[pl.ds(f * NX + 8 * h, 8), :] = fir(SEND_LEFT[NY][f][:21], head)
            ysr[pl.ds(f * NX + 8 * h, 8), :] = fir(SEND_RIGHT[NY][f][-28:], tail)

    def lift_y(x, c):
        lift_rows(v, x * NY, NY, y1, x * NY)
        lift_rows(y1, x * NY, NY // 2, y2, x * (NY // 2))
        lift_rows(y2, x * (NY // 2), NY // 4, y3, x * (NY // 4))
        own = {"own_left": ysl, "own_right": ysr}
        for level, ref in ((1, y2), (2, y3)):
            correct(ref, x * (NY >> level), SIDES[NY][level], y_places[level], ytab, own, lambda f: f * NX + x)
        return c

    lax.fori_loop(0, NX, lift_y, 0)
    pl.semaphore_wait(barrier, len(near))
    y_left = remote(0, ysl, yrr.at[pl.ds(0, Y_ROWS)], "yl")
    y_right = remote(1, ysr, yrl.at[pl.ds(0, Y_ROWS)], "yr")
    y_left.start()
    y_right.start()

    def turn(x, c):
        for t in range(2):
            z1[pl.ds(x * 256 + 128 * t, 128), :] = y1[pl.ds(x * NY + 128 * t, 128), :].T
        z2[pl.ds(x * 128, 128), :] = y2[pl.ds(x * 128, 128), :].T
        return c

    def turn_three(p, c):
        z3[pl.ds(p * 128, 128), :] = y3[pl.ds(p * 128, 128), :].T
        return c

    lax.fori_loop(0, NX, turn, 0, unroll=2)
    lax.fori_loop(0, NX // 2, turn_three, 0, unroll=2)

    def z_sums(level, load_row, store):
        rows = {}

        def row(k):
            if k not in rows:
                rows[k] = load_row(k)
            return rows[k]

        for f in range(2 * level):
            for at, ref in enumerate((zsl, zsr, zml, zmr)):
                weights = [float(c) for c in Z_SENDS[8 * at + f]]
                ks = [k for k in range(NZ) if weights[k] != 0.0]
                store(ref, f, fir([weights[k] for k in ks], [row(k) for k in ks]))

    for h in range(2):
        for t in range(2):

            def store_one(ref, f, value, h=h, t=t):
                ref[pl.ds((f * 2 + t) * NX + 8 * h, 8), :] = value

            z_sums(1, lambda k, h=h, t=t: z1[pl.ds(h * 8 * 256 + t * 128 + k, 8, stride=256), :], store_one)

        def store_two(ref, f, value, h=h):
            ref[pl.ds(Z_TWO + f * NX + 8 * h, 8), :] = value

        z_sums(2, lambda k, h=h: z2[pl.ds(h * 8 * 128 + k, 8, stride=128), :], store_two)

    def store_three(ref, f, value):
        ref[pl.ds(Z_THREE + f * (NX // 2), 8), :] = value

    z_sums(3, lambda k: z3[pl.ds(k, 8, stride=128), :], store_three)
    z_left = remote(2, zsl, zrr, "zl")
    z_right = remote(3, zsr, zrl, "zr")
    z_left.start()
    z_right.start()

    row_one = lambda x, t: lambda f: (f * 2 + t) * NX + x
    row_two = lambda x: lambda f: Z_TWO + f * NX + x
    row_three = lambda p: lambda f: Z_THREE + f * (NX // 2) + p
    z_own = {"own_left": zsl, "own_right": zsr}

    def lift_z2(x, c):
        lift_rows(z2, x * NZ, NZ, t2, x * 64, keep_high=False)
        lift_rows(t2, x * 64, 64, w2, x * 64)
        correct(w2, x * 64, SIDES[NZ][1], z_places[1], ztab, z_own, row_two(x))
        return c

    def lift_z3(p, c):
        lift_rows(z3, p * NZ, NZ, t3, p * 64, keep_high=False)
        lift_rows(t3, p * 64, 64, t4, p * 32, keep_high=False)
        lift_rows(t4, p * 32, 32, w3, p * 32)
        correct(w3, p * 32, SIDES[NZ][2], z_places[2], ztab, z_own, row_three(p))
        return c

    def lift_z1(i, c):
        lift_rows(z1, i * NZ, NZ, w1, i * NZ)
        return c

    lax.fori_loop(0, NX // 2, lift_z3, 0)
    lax.fori_loop(0, NX, lift_z2, 0)

    y_left.wait()
    y_right.wait()
    for load in loads[1:]:
        load.wait()
    htl[...] = yrl[...].T
    htr[...] = yrr[...].T
    for at, ref in ((0, htl), (8, htr)):
        sums = jnp.dot(sends[...], ref[...], precision=lax.Precision.HIGHEST, preferred_element_type=F32)
        for i, out in enumerate((zlsl, zlsr, zlml, zlmr)):
            out[pl.ds(at, 8), :] = sums[8 * i : 8 * i + 8]
    zl_left = remote(4, zlsl, zlrr, "zl")
    zl_right = remote(5, zlsr, zlrl, "zr")
    zl_left.start()
    zl_right.start()

    for i, ref in enumerate((htl, htr)):
        lift_rows(ref, 0, 128, g1, 128 * i)
        lift_rows(g1, 128 * i, 64, u2, 64 * i)
        lift_rows(u2, 64 * i, 32, u3, 32 * i)
    for i in range(2):
        own = {"own_left": zlsl, "own_right": zlsr}
        g2[pl.ds(64 * i, 64), :] = u2[pl.ds(64 * i, 64), :]
        g3[pl.ds(32 * i, 32), :] = u3[pl.ds(32 * i, 32), :]
        correct(g2, 64 * i, SIDES[NZ][1], z_places[1], ztab, own, lambda f, i=i: 8 * i + f)
        correct(g3, 32 * i, SIDES[NZ][2], z_places[2], ztab, own, lambda f, i=i: 8 * i + f)
    for level, g, p, n in ((1, g1, p1, 128), (2, g2, p2, 64), (3, g3, p3, 32)):
        for i, value in enumerate(slots(level, g[pl.ds(0, n), :], g[pl.ds(n, n), :])):
            p[pl.ds(n * i, n), :] = value

    lax.fori_loop(0, 2 * NX, lift_z1, 0)

    def spread_one(x, c):
        keep = (lanes_of((128, 128)) & 15) == x
        value = expand(1, [p1[pl.ds(128 * i, 128), :] for i in range(3)], keep, spread1)
        for t in range(2):
            at = pl.ds(x * 256 + 128 * t, 128)
            w1[at, :] = w1[at, :] + value[:, 128 * t : 128 * t + 128]
        return c

    def spread_two(x, c):
        keep = (lanes_of((64, 128)) & 15) == x
        at = pl.ds(x * 64, 64)
        w2[at, :] = w2[at, :] + expand(2, [p2[pl.ds(64 * i, 64), :] for i in range(6)], keep, spread2)
        return c

    def spread_three(p, c):
        keep = ((lanes_of((32, 128)) & 15) >> 1) == p
        at = pl.ds(p * 32, 32)
        w3[at, :] = w3[at, :] + expand(3, [p3[pl.ds(32 * i, 32), :] for i in range(12)], keep, spread3)
        return c

    lax.fori_loop(0, NX, spread_one, 0)

    def sums_one(g, c):
        rows = [w1[pl.ds(x * 256 + 8 * g, 8), :] for x in (0, 1, 2, 12, 13, 14, 15)]
        for f in range(2):
            x1sl[pl.ds(f * 256 + 8 * g, 8), :] = fir(X_ONE_LEFT[f][:3], rows[:3])
            x1sr[pl.ds(f * 256 + 8 * g, 8), :] = fir(X_ONE_RIGHT[f][12:], rows[3:])
        return c

    lax.fori_loop(0, 32, sums_one, 0, unroll=4)
    x1_left = remote(6, x1sl, x1rr, "xl")
    x1_right = remote(7, x1sr, x1rl, "xr")
    x1_left.start()
    x1_right.start()
    lax.fori_loop(0, NX // 2, spread_three, 0)
    lax.fori_loop(0, NX, spread_two, 0)

    for copy in (z_left, z_right, zl_left, zl_right):
        copy.wait()
    gz = lax.axis_index("gz")

    @pl.when(gz == 0)
    def _():
        zrl[...] = zml[...]
        zlrl[...] = zlml[...]

    @pl.when(gz == SIZES["gz"] - 1)
    def _():
        zrr[...] = zmr[...]
        zlrr[...] = zlmr[...]

    lane, sub = lanes_of((16, 128)), lax.broadcasted_iota(jnp.int32, (16, 128), 0)
    for late, ref in ((zlrl, zrl), (zlrr, zrr)):
        left, right = late[pl.ds(0, 8), :], late[pl.ds(8, 8), :]
        for level, spread_ref, count in ((3, spread3, 8), (2, spread2, NX), (1, spread1, NX)):
            arrays = slots(level, left, right)
            if level == 3:
                keep = ((lane[:8] & 15) >> 1) == sub[:8]
            else:
                keep = (lane & 15) == sub
            tall = [
                jnp.concatenate([jnp.where(keep, a[f : f + 1], 0.0) for f in range(2 * level)], axis=0) for a in arrays
            ]
            value = expand(level, tall, jnp.full(tall[0].shape, True), spread_ref)
            for f in range(2 * level):
                piece = value[f * count : f * count + count]
                if level == 1:
                    for t in range(2):
                        at = pl.ds((f * 2 + t) * NX, NX)
                        ref[at, :] = ref[at, :] + piece[:, 128 * t : 128 * t + 128]
                else:
                    at = pl.ds((Z_TWO if level == 2 else Z_THREE) + f * count, count)
                    ref[at, :] = ref[at, :] + piece

    for side, ref in enumerate((zrl, zrr)):
        for f in range(2):
            for t in range(2):
                rows = [ref[pl.ds((f * 2 + t) * NX + x, 1), :] for x in (0, 1, 2, 12, 13, 14, 15)]
                for xf in range(2):
                    at = pl.ds((xf * 2 + t) * 4 + side * 2 + f, 1)
                    xesl[at, :] = fir(X_ONE_LEFT[xf][:3], rows[:3])
                    xesr[at, :] = fir(X_ONE_RIGHT[xf][12:], rows[3:])
    xe_left = remote(8, xesl, xerr, "xl")
    xe_right = remote(9, xesr, xerl, "xr")
    xe_left.start()
    xe_right.start()

    z_past = {"from_left": zrl, "from_right": zrr}

    def finish_z2(x, c):
        correct(w2, x * 64, SIDES[NZ][1], z_places[1], ztab, z_past, row_two(x))
        return c

    def finish_z3(p, c):
        correct(w3, p * 32, SIDES[NZ][2], z_places[2], ztab, z_past, row_three(p))
        return c

    def finish_z1(x, c):
        for t in range(2):
            correct(w1, x * 256 + 128 * t, SIDES[NZ][0], z_places[0], ztab, z_past, row_one(x, t))
        return c

    lax.fori_loop(0, NX // 2, finish_z3, 0)
    lax.fori_loop(0, NX, finish_z2, 0)

    def sums_two(g, c):
        rows = [w2[pl.ds(x * 64 + 8 * g, 8), :] for x in range(NX)]
        for f in range(N_TWO):
            x23sl[pl.ds(f * 64 + 8 * g, 8), :] = fir(X_TWO_LEFT[f], rows)
            x23sr[pl.ds(f * 64 + 8 * g, 8), :] = fir(X_TWO_RIGHT[f], rows)
        return c

    def send_three(g, c):
        rows = [w3[pl.ds(p * 32 + 8 * g, 8), :] for p in range(NX // 2)]
        for ref, block, at in ((x23sr, 1, N_TWO * 64), (x23sl, 3, N_TWO * 64), (x3sr, 0, 0), (x3sl, 4, 0)):
            for h, value in enumerate(sums_three(X_THREE[block], rows)):
                ref[pl.ds(at + 32 * h + 8 * g, 8), :] = value
        return c

    lax.fori_loop(0, 8, sums_two, 0)
    lax.fori_loop(0, 4, send_three, 0)
    x23_left = remote(10, x23sl, x23rr, "xl")
    x23_right = remote(11, x23sr, x23rl, "xr")
    x3_left = remote(12, x3sl, x3rr, "xll")
    x3_right = remote(13, x3sr, x3rl, "xrr")
    for copy in (x23_left, x23_right, x3_left, x3_right):
        copy.start()
    lax.fori_loop(0, NX, finish_z1, 0)
    for copy in (x1_left, x1_right, xe_left, xe_right):
        copy.wait()
    for xf in range(2):
        for t in range(2):
            for ref, ends in ((x1rl, xerl), (x1rr, xerr)):
                at = (xf * 2 + t) * 4
                refs = {"from_left": ends.at[pl.ds(at, 2)], "from_right": ends.at[pl.ds(at + 2, 2)]}
                correct(ref, xf * 256 + 128 * t, SIDES[NZ][0], z_places[0], ztab, refs, lambda f: f)
    for copy in (x23_left, x23_right, x3_left, x3_right):
        copy.wait()


def paired(weights, rows):
    low_lanes = lanes_of((8, 128)) < 64
    total = jnp.zeros((8, 128), F32)
    for p in range(NX // 2):
        if weights[2 * p] == 0.0 and weights[2 * p + 1] == 0.0:
            continue
        total = total + jnp.where(low_lanes, weights[2 * p], weights[2 * p + 1]) * rows[p]
    return total + pltpu.roll(total, 64, 1)


def sums_three(matrix, rows):
    low_lanes = lanes_of((8, 128)) < 64
    return [jnp.where(low_lanes, paired(matrix[2 * h], rows), paired(matrix[2 * h + 1], rows)) for h in range(2)]


def finish(w1, w2, w3, x1rl, x1rr, x23rl, x23rr, x3rl, x3rr, out1, out2, out3, out4, o1, o2, o3, o4, sems):
    lane = lanes_of((8, 128))
    low_lanes = lane < 64
    copies = []

    def send(src, dst):
        copy = pltpu.make_async_copy(src, dst, sems.at[len(copies)])
        copy.start()
        copies.append(copy)

    for hy in range(2):
        for hz in range(2):

            def out_one(g, c, hy=hy, hz=hz):
                row = 128 * hy + 64 * hz + 8 * g
                rows = [w1[pl.ds(x * 256 + row, 8), :] for x in range(NX)]
                left = [x1rl[pl.ds(f * 256 + row, 8), :] for f in range(2)]
                right = [x1rr[pl.ds(f * 256 + row, 8), :] for f in range(2)]
                for i, value in enumerate(lift_major(rows)):
                    hx = i // 8
                    band = 4 * hx + 2 * hy + hz
                    if not band:
                        continue
                    value = fir([1.0] + X_ONE_FROM_LEFT[i] + X_ONE_FROM_RIGHT[i], [value] + left + right)
                    value = value * (SCALES[0][hx] * SCALES[0][hy] * SCALES[0][hz])
                    o1[pl.ds((band - 1) * 512 + (i % 8) * 64 + 8 * g, 8), :] = value
                return c

            lax.fori_loop(0, 8, out_one, 0)
            for hx in range(2):
                band = 4 * hx + 2 * hy + hz
                if band:
                    at = pl.ds((band - 1) * 512, 512)
                    send(o1.at[at], out1.at[at])

    def out_two(g, hz):
        rows = [w2[pl.ds(x * 64 + 8 * g, 8), :] for x in range(NX)]
        left = [x23rl[pl.ds(f * 64 + 8 * g, 8), :] for f in range(N_TWO)]
        right = [x23rr[pl.ds(f * 64 + 8 * g, 8), :] for f in range(N_TWO)]
        for i in range(8):
            hx = i // 4
            value = fir(X_TWO_OWN[i] + X_TWO_FROM_LEFT[i] + X_TWO_FROM_RIGHT[i], rows + left + right)
            scale = SCALES[1][hx] * SCALES[1][hz]
            value = value * jnp.where(low_lanes, scale * SCALES[1][0], scale * SCALES[1][1])
            for hy in range(2):
                band = 4 * hx + 2 * hy + hz
                if band:
                    at = (band - 1) * 128 + (i % 4) * 32 + 8 * (g % 4)
                    o2[pl.ds(at, 8), :] = value[:, 64 * hy : 64 * hy + 64]

    for g in range(8):
        out_two(g, g // 4)
    send(o2, out2)

    def out_three(g, hz):
        rows = [w3[pl.ds(p * 32 + 8 * g, 8), :] for p in range(NX // 2)]
        own = sums_three(X_THREE[2], rows)
        high_y = (lane & 63) >= 32
        for hx in range(2):
            value = own[hx]
            for ref, at in ((x23rl, N_TWO * 64), (x23rr, N_TWO * 64), (x3rl, 0), (x3rr, 0)):
                value = value + ref[pl.ds(at + 32 * hx + 8 * g, 8), :]
            scale = SCALES[2][hx] * SCALES[2][hz]
            value = value * jnp.where(high_y, scale * SCALES[2][1], scale * SCALES[2][0])
            for q in range(4):
                i, hy = divmod(q, 2)
                band = 4 * hx + 2 * hy + hz
                row = 16 * i + 8 * (g % 2)
                piece = value[:, 32 * q : 32 * q + 32]
                if band:
                    o3[pl.ds((band - 1) * 32 + row, 8), :] = piece
                else:
                    o4[pl.ds(row, 8), :] = piece

    for g in range(4):
        out_three(g, g // 2)
    send(o3, out3)
    send(o4, out4)
    for copy in copies:
        copy.wait()


def shards(velocity):
    vmem, hbm = pl.BlockSpec(memory_space=pltpu.VMEM), pl.BlockSpec(memory_space=pltpu.HBM)
    wide = lambda rows: pltpu.VMEM((rows, 128), F32)
    results = [32 * NZ, 16 * 64, 8 * 32, 512, 512, X23_ROWS, X23_ROWS, 64, 64]
    scratch = [16 * NY, 16 * NY, 16 * NY // 2, 16 * NY // 4]
    scratch += [32 * NZ, 16 * NZ, 8 * NZ]
    scratch += [16 * 64, 8 * 64, 8 * 32]
    scratch += [table_rows(SIDES[NY]), table_rows(SIDES[NZ])]
    scratch += [Y_ROWS] * 2 + [128] * 2 + [Z_ROWS] * 6
    scratch += [128, 128, 256, 128, 64, 128, 64, 3 * 128, 6 * 64, 12 * 32] + [16] * 6
    scratch += [512] * 2 + [X23_ROWS] * 2 + [64] * 2 + [16] * 4
    operands = [velocity.reshape(NX * NY, NZ), *[jnp.asarray(matrix) for matrix in SPREADS], jnp.asarray(Z_SENDS)]
    got = pl.pallas_call(
        kernel,
        out_shape=[jax.ShapeDtypeStruct((rows, 128), F32) for rows in results],
        in_specs=[hbm] * 5,
        out_specs=[vmem] * len(results),
        scratch_shapes=[wide(rows) for rows in scratch]
        + [pltpu.VMEM(matrix.shape, jnp.bfloat16) for matrix in SPREADS]
        + [wide(32)]
        + [pltpu.SemaphoreType.DMA((5,)), pltpu.SemaphoreType.DMA((14,)), pltpu.SemaphoreType.DMA((14,))],
        compiler_params=pltpu.CompilerParams(collective_id=0, has_side_effects=True, vmem_limit_bytes=28 * 2**20),
    )(*[pltpu.with_memory_space_constraint(a, pltpu.HBM) for a in operands])
    shapes = [(7 * 8 * 64, 128), (7 * 4 * 32, 64), (7 * 2 * 16, 32), (2 * 16, 32)]
    out1, out2, out3, out4 = pl.pallas_call(
        finish,
        out_shape=[jax.ShapeDtypeStruct(shape, F32) for shape in shapes],
        in_specs=[vmem] * len(results),
        out_specs=[hbm] * 4,
        scratch_shapes=[pltpu.VMEM(shape, F32) for shape in shapes] + [pltpu.SemaphoreType.DMA((10,))],
        compiler_params=pltpu.CompilerParams(vmem_limit_bytes=16 * 2**20),
    )(*got)
    return (
        out1.reshape(7, 8, 64, 128).transpose(0, 1, 3, 2),
        out2.reshape(7, 4, 32, 64).transpose(0, 1, 3, 2),
        out3.reshape(7, 2, 16, 32).transpose(0, 1, 3, 2),
        out4.reshape(2, 16, 32).transpose(0, 2, 1),
    )


def solution(mesh):
    return jax.shard_map(
        shards,
        mesh=mesh,
        in_specs=(P("gx", "gy", "gz"),),
        out_specs=(
            P(None, "gx", "gy", "gz"),
            P(None, "gx", "gy", "gz"),
            P(None, "gx", "gy", "gz"),
            P("gx", "gy", "gz"),
        ),
        check_vma=False,
    )
```

```python
import math

import jax
import jax.numpy as jnp
import ml_dtypes
import numpy as np
from jax import lax
from jax.experimental import pallas as pl
from jax.experimental.pallas import tpu as pltpu
from jax.sharding import PartitionSpec as P

ALPHA = -1.586134342059924
BETA = -0.052980118572961
GAMMA = 0.882911075530934
DELTA = 0.443506852043971
SCALE_LOW = math.sqrt(2.0) / 1.230174104914001
SCALE_HIGH = 1.230174104914001 / math.sqrt(2.0)


def lift_matrix(rows, edges):
    s, d = rows[0::2], rows[1::2]
    none = np.zeros_like(s[:1])
    if edges == "periodic":
        d = d + ALPHA * (s + np.roll(s, -1, 0))
        s = s + BETA * (np.roll(d, 1, 0) + d)
        d = d + GAMMA * (s + np.roll(s, -1, 0))
        s = s + DELTA * (np.roll(d, 1, 0) + d)
        return s, d
    start, end = edges
    up = lambda v, last: np.concatenate([v[1:], last])
    down = lambda v, first: np.concatenate([first, v[:-1]])
    d1 = d + ALPHA * (s + up(s, s[-1:] if end else none))
    before1 = d1[:1] if start else ALPHA * s[:1]
    s1 = s + BETA * (down(d1, before1) + d1)
    d2 = d1 + GAMMA * (s1 + up(s1, s1[-1:] if end else BETA * d1[-1:]))
    before2 = d2[:1] if start else before1 + GAMMA * (BETA * before1 + s1[:1])
    return s1 + DELTA * (down(d2, before2) + d2), d2


def path_matrix(rows, level, edges):
    for _ in range(level):
        rows, high = lift_matrix(rows, edges)
    return np.concatenate([rows, high])


def outgoing(n):
    rows, left, right = np.eye(n), [], []
    for _ in range(3):
        s, d = rows[0::2], rows[1::2]
        left += [s[0], s[0] + BETA * (d[0] + ALPHA * (s[0] + s[1]))]
        right += [d[-1] + ALPHA * s[-1], s[-1] + BETA * (d[-2] + ALPHA * (s[-2] + s[-1]))]
        rows = lift_matrix(rows, (False, False))[0]
    return np.stack(left), np.stack(right)


def line_blocks(n, level):
    m = n >> level
    rows = np.eye(5 * n)
    for _ in range(level):
        rows, high = lift_matrix(rows, "periodic")
    whole = np.concatenate([rows[2 * m : 3 * m], high[2 * m : 3 * m]])
    return [whole[:, k * n : (k + 1) * n] for k in range(5)]


def solved(target, basis):
    u = np.linalg.lstsq(basis.T, target.T, rcond=None)[0].T
    assert np.abs(u @ basis - target).max() < 1e-9
    return np.where(np.abs(u) < 1e-10, 0.0, u)


def block_plan(n, level):
    left, right = outgoing(n)
    left, right = left[: 2 * level], right[: 2 * level]
    blocks = line_blocks(n, level)
    alone = path_matrix(np.eye(n), level, (False, False))
    from_left = solved(blocks[1], right)
    from_right = solved(blocks[3], left)
    own = solved(blocks[2] - alone, np.concatenate([left, right]))
    return dict(left=left, right=right, alone=alone, from_left=from_left, from_right=from_right, own_left=own[:, : 2 * level], own_right=own[:, 2 * level :])


def mirror_plan(n, plans):
    out = []
    for start in (True, False):
        uses, rests = [], []
        for level, plan in enumerate(plans, 1):
            m = n >> level
            rows = np.eye(4 * n)
            for _ in range(level):
                rows, high = lift_matrix(rows, (True, True))
            at = 0 if start else 3
            whole = np.concatenate([rows[at * m : (at + 1) * m], high[at * m : (at + 1) * m]])
            whole = whole[:, at * n : (at + 1) * n]
            rests.append(whole - plan["alone"] - plan["own_left"] @ plan["left"] - plan["own_right"] @ plan["right"])
            u = plan["from_left"] if start else plan["from_right"]
            uses.append(np.pad(u, ((0, 0), (0, 6 - u.shape[1]))))
        use, rest = np.concatenate(uses), np.concatenate(rests)
        g = np.linalg.lstsq(use, rest, rcond=None)[0]
        assert np.abs(use @ g - rest).max() < 1e-9
        out.append(np.where(np.abs(g) < 1e-10, 0.0, g))
    return out


MESH = pl.DeviceIdType.MESH
SIZES = {"gx": 8, "gy": 4, "gz": 4}
NX, NY, NZ = 16, 256, 128
F32 = jnp.float32


def rounded(matrix):
    return [[float(np.float32(c)) if abs(c) > 1e-10 else 0.0 for c in row] for row in matrix]


def fir(weights, rows):
    total = None
    for weight, row in zip(weights, rows):
        if weight == 0.0:
            continue
        term = row() if callable(row) else row
        term = term if weight == 1.0 else weight * term
        total = term if total is None else total + term
    return total


def lift_list(s, d, up, down, first, last):
    before1 = ALPHA * first(s)
    d1 = [b + ALPHA * (a + c) for a, b, c in zip(s, d, up(s, None))]
    s1 = [a + BETA * (b + c) for a, b, c in zip(s, d1, down(d1, before1))]
    d2 = [b + GAMMA * (a + c) for a, b, c in zip(s1, d1, up(s1, BETA * last(d1)))]
    before2 = before1 + GAMMA * (BETA * before1 + first(s1))
    s2 = [a + DELTA * (b + c) for a, b, c in zip(s1, d2, down(d2, before2))]
    return s2, d2


def lift_rows(src, base, n, dst, to, keep_high=True):
    k = n // 16
    s = [src[pl.ds(base + 16 * i, 8, stride=2), :] for i in range(k)]
    d = [src[pl.ds(base + 16 * i + 1, 8, stride=2), :] for i in range(k)]
    sub = lax.broadcasted_iota(jnp.int32, (8, 128), 0)
    top, bottom = sub == 0, sub == 7

    def up(v, fill):
        r = [pltpu.roll(x, 7, 0) for x in v]
        fill = jnp.zeros((8, 128), F32) if fill is None else fill
        return [jnp.where(bottom, r[i + 1] if i + 1 < k else fill, r[i]) for i in range(k)]

    def down(v, fill):
        r = [pltpu.roll(x, 1, 0) for x in v]
        return [jnp.where(top, r[i - 1] if i else fill, r[i]) for i in range(k)]

    low, high = lift_list(s, d, up, down, lambda v: v[0], lambda v: v[-1])
    for i in range(k):
        dst[pl.ds(to + 8 * i, 8), :] = low[i]
        if keep_high:
            dst[pl.ds(to + 8 * (k + i), 8), :] = high[i]


def lift_major(rows):
    low, high = lift_list(
        rows[0::2],
        rows[1::2],
        lambda v, fill: v[1:] + [jnp.zeros_like(v[0]) if fill is None else fill],
        lambda v, fill: [fill] + v[:-1],
        lambda v: v[0],
        lambda v: v[-1],
    )
    return low + high


class Side:
    def __init__(self, plan):
        self.groups = {}
        for source in ("from_left", "from_right", "own_left", "own_right"):
            u = plan[source]
            for g in range(u.shape[0] // 8):
                for f in range(u.shape[1]):
                    column = u[8 * g : 8 * g + 8, f]
                    if np.abs(column).max() > 1e-10:
                        self.groups.setdefault(g, []).append((source, f, column))


PLANS = {n: [block_plan(n, level) for level in (1, 2, 3)] for n in (NY, NZ)}
SIDES = {n: [Side(plan) for plan in PLANS[n]] for n in (NY, NZ)}
MIRRORS = mirror_plan(NZ, PLANS[NZ])
SEND_LEFT = {n: rounded(PLANS[n][2]["left"]) for n in (NY, NZ)}
SEND_RIGHT = {n: rounded(PLANS[n][2]["right"]) for n in (NY, NZ)}
SCALES = [(SCALE_LOW**level, SCALE_LOW ** (level - 1) * SCALE_HIGH) for level in (1, 2, 3)]


def factored(matrix):
    u, size, v = np.linalg.svd(matrix, full_matrices=False)
    rank = int((size > 1e-9).sum())
    return rounded(u[:, :rank] * size[:rank]), rounded(v[:rank])


X_ONE = block_plan(NX, 1)
X_ONE_LEFT, X_ONE_RIGHT = rounded(X_ONE["left"]), rounded(X_ONE["right"])
X_ONE_FROM_LEFT, X_ONE_FROM_RIGHT = rounded(X_ONE["from_left"]), rounded(X_ONE["from_right"])
X_TWO_BLOCKS = line_blocks(NX, 2)
X_TWO_FROM_LEFT, X_TWO_RIGHT = factored(X_TWO_BLOCKS[1])
X_TWO_FROM_RIGHT, X_TWO_LEFT = factored(X_TWO_BLOCKS[3])
X_TWO_OWN = rounded(X_TWO_BLOCKS[2])
X_THREE = [rounded(block) for block in line_blocks(NX, 3)]
N_TWO = len(X_TWO_RIGHT)

Y_ROWS = 6 * NX
Z_TWO, Z_THREE, Z_ROWS = 4 * NX, 8 * NX, 8 * NX + 6 * (NX // 2)
X23_ROWS = N_TWO * 64 + 64


def neighbour(axis, step):
    size = SIZES[axis]
    place = {name: lax.axis_index(name) for name in SIZES}
    place[axis] = lax.rem(place[axis] + (step + size), size)
    return tuple(place[name] for name in ("gx", "gy", "gz"))


def build_table(table, sides):
    sub = lax.broadcasted_iota(jnp.int32, (8, 128), 0)
    found = []
    at = 0
    for side in sides:
        places = {}
        for g, terms in side.groups.items():
            for source, f, column in terms:
                value = jnp.zeros((8, 128), F32)
                for i in range(8):
                    if abs(column[i]) > 1e-10:
                        value = jnp.where(sub == i, float(np.float32(column[i])), value)
                table[pl.ds(at, 8), :] = value
                places[g, source, f] = at
                at += 8
        found.append(places)
    return found


def table_rows(sides):
    return 8 * sum(len(terms) for side in sides for terms in side.groups.values())


def correct(ref, base, side, places, table, refs, row):
    for g, terms in side.groups.items():
        terms = [(source, f) for source, f, _ in terms if source in refs]
        if not terms:
            continue
        value = ref[pl.ds(base + 8 * g, 8), :]
        for source, f in terms:
            value = value + table[pl.ds(places[g, source, f], 8), :] * refs[source][pl.ds(row(f), 1), :]
        ref[pl.ds(base + 8 * g, 8), :] = value


def parts_of(value):
    rest, parts = np.asarray(value, np.float32), []
    for _ in range(3):
        part = rest.astype(ml_dtypes.bfloat16)
        parts.append(part)
        rest = rest - part.astype(np.float32)
    return parts


def spread(level):
    plan = PLANS[NY][level - 1]
    left, right = plan["from_left"].T, plan["from_right"].T
    if level == 3:
        blocks = []
        for u in (left, right):
            block = np.zeros((8, NX, 128))
            block[:6, 0::2, :64] = u[:, None, :]
            block[:6, 1::2, 64:] = u[:, None, :]
            blocks.append(block.reshape(128, 128))
        matrix = np.concatenate(blocks)
    else:
        matrix = np.repeat(np.concatenate([left, right]), NX, axis=0)
    one, two, three = parts_of(matrix)
    return np.concatenate([one, two, three, one, two, one])


SPREADS = [spread(level) for level in (1, 2, 3)]
Z_SENDS = np.zeros((32, NZ), np.float32)
for _at, _rows in enumerate((PLANS[NZ][2]["left"], PLANS[NZ][2]["right"], *MIRRORS)):
    Z_SENDS[8 * _at : 8 * _at + 6] = _rows


def split(value):
    one = value.astype(jnp.bfloat16).astype(F32)
    two = (value - one).astype(jnp.bfloat16).astype(F32)
    return one, two, value - one - two


def lanes_of(shape):
    return lax.broadcasted_iota(jnp.int32, shape, 1)


def slots(level, left, right):
    lane = lanes_of(left.shape)
    turn = lambda value, by: pltpu.roll(value, by, 1)
    if level == 1:
        one, two, three = split(jnp.where(lane < 32, left, jnp.where(lane < 64, turn(right, 32), 0.0)))
        return [one + turn(one, 64), one + turn(two, 64), two + turn(three, 64)]
    if level == 2:
        one, two, three = split(jnp.where(lane < 64, left, turn(right, 64)))
        return [one, one, one, two, two, three]
    one, two, three = zip(split(left), split(right))
    return [*one, *one, *one, *two, *two, *three]


def expand(level, arrays, keep, spread_ref):
    factor = jnp.concatenate([jnp.where(keep, a, 0.0).astype(jnp.bfloat16) for a in arrays], axis=1)
    return jnp.dot(factor, spread_ref[...], preferred_element_type=F32)


def kernel(
    vel, spread1_hbm, spread2_hbm, spread3_hbm, sends_hbm,
    w1, w2, w3, x1rl, x1rr, x23rl, x23rr, x3rl, x3rr,
    v, y1, y2, y3, z1, z2, z3, t2, t3, t4, ytab, ztab,
    ysl, ysr, yrl, yrr, zsl, zsr, zrl, zrr, zml, zmr,
    htl, htr, g1, g2, g3, u2, u3, p1, p2, p3, zlsl, zlsr, zlrl, zlrr, zlml, zlmr,
    x1sl, x1sr, x23sl, x23sr, x3sl, x3sr, xesl, xesr, xerl, xerr,
    spread1, spread2, spread3, sends,
    load_sems, send_sems, recv_sems,
):
    loads = [
        pltpu.make_async_copy(src, dst, load_sems.at[i])
        for i, (src, dst) in enumerate(
            ((vel, v), (sends_hbm, sends), (spread1_hbm, spread1), (spread2_hbm, spread2), (spread3_hbm, spread3))
        )
    ]
    for load in loads:
        load.start()
    near = {
        "yl": neighbour("gy", -1), "yr": neighbour("gy", 1), "zl": neighbour("gz", -1), "zr": neighbour("gz", 1),
        "xl": neighbour("gx", -1), "xr": neighbour("gx", 1), "xll": neighbour("gx", -2), "xrr": neighbour("gx", 2),
    }
    barrier = pltpu.get_barrier_semaphore()
    for device in near.values():
        pl.semaphore_signal(barrier, inc=1, device_id=device, device_id_type=MESH)
    y_places = build_table(ytab, SIDES[NY])
    z_places = build_table(ztab, SIDES[NZ])
    for ref in (yrl, yrr):
        ref[pl.ds(Y_ROWS, 32), :] = jnp.zeros((32, 128), F32)

    def remote(index, src, dst, to):
        return pltpu.make_async_remote_copy(
            src_ref=src,
            dst_ref=dst,
            send_sem=send_sems.at[index],
            recv_sem=recv_sems.at[index],
            device_id=near[to],
            device_id_type=MESH,
        )

    loads[0].wait()

    for h in range(2):
        head = [v[pl.ds(h * 8 * NY + k, 8, stride=NY), :] for k in range(21)]
        tail = [v[pl.ds(h * 8 * NY + k, 8, stride=NY), :] for k in range(NY - 28, NY)]
        for f in range(6):
            ysl[pl.ds(f * NX + 8 * h, 8), :] = fir(SEND_LEFT[NY][f][:21], head)
            ysr[pl.ds(f * NX + 8 * h, 8), :] = fir(SEND_RIGHT[NY][f][-28:], tail)

    def lift_y(x, c):
        lift_rows(v, x * NY, NY, y1, x * NY)
        lift_rows(y1, x * NY, NY // 2, y2, x * (NY // 2))
        lift_rows(y2, x * (NY // 2), NY // 4, y3, x * (NY // 4))
        own = {"own_left": ysl, "own_right": ysr}
        for level, ref in ((1, y2), (2, y3)):
            correct(ref, x * (NY >> level), SIDES[NY][level], y_places[level], ytab, own, lambda f: f * NX + x)
        return c

    lax.fori_loop(0, NX, lift_y, 0, unroll=2)
    pl.semaphore_wait(barrier, len(near))
    y_left = remote(0, ysl, yrr.at[pl.ds(0, Y_ROWS)], "yl")
    y_right = remote(1, ysr, yrl.at[pl.ds(0, Y_ROWS)], "yr")
    y_left.start()
    y_right.start()

    def turn(x, c):
        for t in range(2):
            z1[pl.ds(x * 256 + 128 * t, 128), :] = y1[pl.ds(x * NY + 128 * t, 128), :].T
        z2[pl.ds(x * 128, 128), :] = y2[pl.ds(x * 128, 128), :].T
        return c

    def turn_three(p, c):
        z3[pl.ds(p * 128, 128), :] = y3[pl.ds(p * 128, 128), :].T
        return c

    lax.fori_loop(0, NX, turn, 0, unroll=4)
    lax.fori_loop(0, NX // 2, turn_three, 0, unroll=8)

    def z_sums(level, load_row, store):
        rows = {}

        def row(k):
            if k not in rows:
                rows[k] = load_row(k)
            return rows[k]

        for f in range(2 * level):
            for at, ref in enumerate((zsl, zsr, zml, zmr)):
                weights = [float(c) for c in Z_SENDS[8 * at + f]]
                ks = [k for k in range(NZ) if weights[k] != 0.0]
                store(ref, f, fir([weights[k] for k in ks], [row(k) for k in ks]))

    for h in range(2):
        for t in range(2):

            def store_one(ref, f, value, h=h, t=t):
                ref[pl.ds((f * 2 + t) * NX + 8 * h, 8), :] = value

            z_sums(1, lambda k, h=h, t=t: z1[pl.ds(h * 8 * 256 + t * 128 + k, 8, stride=256), :], store_one)

        def store_two(ref, f, value, h=h):
            ref[pl.ds(Z_TWO + f * NX + 8 * h, 8), :] = value

        z_sums(2, lambda k, h=h: z2[pl.ds(h * 8 * 128 + k, 8, stride=128), :], store_two)

    def store_three(ref, f, value):
        ref[pl.ds(Z_THREE + f * (NX // 2), 8), :] = value

    z_sums(3, lambda k: z3[pl.ds(k, 8, stride=128), :], store_three)
    z_left = remote(2, zsl, zrr, "zl")
    z_right = remote(3, zsr, zrl, "zr")
    z_left.start()
    z_right.start()

    row_one = lambda x, t: lambda f: (f * 2 + t) * NX + x
    row_two = lambda x: lambda f: Z_TWO + f * NX + x
    row_three = lambda p: lambda f: Z_THREE + f * (NX // 2) + p
    z_own = {"own_left": zsl, "own_right": zsr}

    def lift_z2(x, c):
        lift_rows(z2, x * NZ, NZ, t2, x * 64, keep_high=False)
        lift_rows(t2, x * 64, 64, w2, x * 64)
        correct(w2, x * 64, SIDES[NZ][1], z_places[1], ztab, z_own, row_two(x))
        return c

    def lift_z3(p, c):
        lift_rows(z3, p * NZ, NZ, t3, p * 64, keep_high=False)
        lift_rows(t3, p * 64, 64, t4, p * 32, keep_high=False)
        lift_rows(t4, p * 32, 32, w3, p * 32)
        correct(w3, p * 32, SIDES[NZ][2], z_places[2], ztab, z_own, row_three(p))
        return c

    def lift_z1(i, c):
        lift_rows(z1, i * NZ, NZ, w1, i * NZ)
        return c

    lax.fori_loop(0, NX // 2, lift_z3, 0, unroll=4)
    lax.fori_loop(0, NX, lift_z2, 0, unroll=4)

    y_left.wait()
    y_right.wait()
    for load in loads[1:]:
        load.wait()
    htl[...] = yrl[...].T
    htr[...] = yrr[...].T
    for at, ref in ((0, htl), (8, htr)):
        sums = jnp.dot(sends[...], ref[...], precision=lax.Precision.HIGHEST, preferred_element_type=F32)
        for i, out in enumerate((zlsl, zlsr, zlml, zlmr)):
            out[pl.ds(at, 8), :] = sums[8 * i : 8 * i + 8]
    zl_left = remote(4, zlsl, zlrr, "zl")
    zl_right = remote(5, zlsr, zlrl, "zr")
    zl_left.start()
    zl_right.start()

    for i, ref in enumerate((htl, htr)):
        lift_rows(ref, 0, 128, g1, 128 * i)
        lift_rows(g1, 128 * i, 64, u2, 64 * i)
        lift_rows(u2, 64 * i, 32, u3, 32 * i)
    for i in range(2):
        own = {"own_left": zlsl, "own_right": zlsr}
        g2[pl.ds(64 * i, 64), :] = u2[pl.ds(64 * i, 64), :]
        g3[pl.ds(32 * i, 32), :] = u3[pl.ds(32 * i, 32), :]
        correct(g2, 64 * i, SIDES[NZ][1], z_places[1], ztab, own, lambda f, i=i: 8 * i + f)
        correct(g3, 32 * i, SIDES[NZ][2], z_places[2], ztab, own, lambda f, i=i: 8 * i + f)
    for level, g, p, n in ((1, g1, p1, 128), (2, g2, p2, 64), (3, g3, p3, 32)):
        for i, value in enumerate(slots(level, g[pl.ds(0, n), :], g[pl.ds(n, n), :])):
            p[pl.ds(n * i, n), :] = value

    lax.fori_loop(0, 2 * NX, lift_z1, 0, unroll=4)

    def spread_one(x, c):
        keep = (lanes_of((128, 128)) & 15) == x
        value = expand(1, [p1[pl.ds(128 * i, 128), :] for i in range(3)], keep, spread1)
        for t in range(2):
            at = pl.ds(x * 256 + 128 * t, 128)
            w1[at, :] = w1[at, :] + value[:, 128 * t : 128 * t + 128]
        return c

    def spread_two(x, c):
        keep = (lanes_of((64, 128)) & 15) == x
        at = pl.ds(x * 64, 64)
        w2[at, :] = w2[at, :] + expand(2, [p2[pl.ds(64 * i, 64), :] for i in range(6)], keep, spread2)
        return c

    def spread_three(p, c):
        keep = ((lanes_of((32, 128)) & 15) >> 1) == p
        at = pl.ds(p * 32, 32)
        w3[at, :] = w3[at, :] + expand(3, [p3[pl.ds(32 * i, 32), :] for i in range(12)], keep, spread3)
        return c

    lax.fori_loop(0, NX, spread_one, 0, unroll=4)

    def sums_one(g, c):
        rows = [w1[pl.ds(x * 256 + 8 * g, 8), :] for x in (0, 1, 2, 12, 13, 14, 15)]
        for f in range(2):
            x1sl[pl.ds(f * 256 + 8 * g, 8), :] = fir(X_ONE_LEFT[f][:3], rows[:3])
            x1sr[pl.ds(f * 256 + 8 * g, 8), :] = fir(X_ONE_RIGHT[f][12:], rows[3:])
        return c

    lax.fori_loop(0, 32, sums_one, 0, unroll=4)
    x1_left = remote(6, x1sl, x1rr, "xl")
    x1_right = remote(7, x1sr, x1rl, "xr")
    x1_left.start()
    x1_right.start()
    lax.fori_loop(0, NX // 2, spread_three, 0, unroll=8)
    lax.fori_loop(0, NX, spread_two, 0, unroll=8)

    for copy in (z_left, z_right, zl_left, zl_right):
        copy.wait()
    gz = lax.axis_index("gz")

    @pl.when(gz == 0)
    def _():
        zrl[...] = zml[...]
        zlrl[...] = zlml[...]

    @pl.when(gz == SIZES["gz"] - 1)
    def _():
        zrr[...] = zmr[...]
        zlrr[...] = zlmr[...]

    lane, sub = lanes_of((16, 128)), lax.broadcasted_iota(jnp.int32, (16, 128), 0)
    for late, ref in ((zlrl, zrl), (zlrr, zrr)):
        left, right = late[pl.ds(0, 8), :], late[pl.ds(8, 8), :]
        for level, spread_ref, count in ((3, spread3, 8), (2, spread2, NX), (1, spread1, NX)):
            arrays = slots(level, left, right)
            if level == 3:
                keep = ((lane[:8] & 15) >> 1) == sub[:8]
            else:
                keep = (lane & 15) == sub
            tall = [
                jnp.concatenate([jnp.where(keep, a[f : f + 1], 0.0) for f in range(2 * level)], axis=0) for a in arrays
            ]
            value = expand(level, tall, jnp.full(tall[0].shape, True), spread_ref)
            for f in range(2 * level):
                piece = value[f * count : f * count + count]
                if level == 1:
                    for t in range(2):
                        at = pl.ds((f * 2 + t) * NX, NX)
                        ref[at, :] = ref[at, :] + piece[:, 128 * t : 128 * t + 128]
                else:
                    at = pl.ds((Z_TWO if level == 2 else Z_THREE) + f * count, count)
                    ref[at, :] = ref[at, :] + piece

    for side, ref in enumerate((zrl, zrr)):
        for f in range(2):
            for t in range(2):
                rows = [ref[pl.ds((f * 2 + t) * NX + x, 1), :] for x in (0, 1, 2, 12, 13, 14, 15)]
                for xf in range(2):
                    at = pl.ds((xf * 2 + t) * 4 + side * 2 + f, 1)
                    xesl[at, :] = fir(X_ONE_LEFT[xf][:3], rows[:3])
                    xesr[at, :] = fir(X_ONE_RIGHT[xf][12:], rows[3:])
    xe_left = remote(8, xesl, xerr, "xl")
    xe_right = remote(9, xesr, xerl, "xr")
    xe_left.start()
    xe_right.start()

    z_past = {"from_left": zrl, "from_right": zrr}

    def finish_z2(x, c):
        correct(w2, x * 64, SIDES[NZ][1], z_places[1], ztab, z_past, row_two(x))
        return c

    def finish_z3(p, c):
        correct(w3, p * 32, SIDES[NZ][2], z_places[2], ztab, z_past, row_three(p))
        return c

    def finish_z1(x, c):
        for t in range(2):
            correct(w1, x * 256 + 128 * t, SIDES[NZ][0], z_places[0], ztab, z_past, row_one(x, t))
        return c

    lax.fori_loop(0, NX // 2, finish_z3, 0, unroll=2)
    lax.fori_loop(0, NX, finish_z2, 0, unroll=4)

    def sums_two(g, c):
        rows = [w2[pl.ds(x * 64 + 8 * g, 8), :] for x in range(NX)]
        for f in range(N_TWO):
            x23sl[pl.ds(f * 64 + 8 * g, 8), :] = fir(X_TWO_LEFT[f], rows)
            x23sr[pl.ds(f * 64 + 8 * g, 8), :] = fir(X_TWO_RIGHT[f], rows)
        return c

    def send_three(g, c):
        rows = [w3[pl.ds(p * 32 + 8 * g, 8), :] for p in range(NX // 2)]
        for ref, block, at in ((x23sr, 1, N_TWO * 64), (x23sl, 3, N_TWO * 64), (x3sr, 0, 0), (x3sl, 4, 0)):
            for h, value in enumerate(sums_three(X_THREE[block], rows)):
                ref[pl.ds(at + 32 * h + 8 * g, 8), :] = value
        return c

    lax.fori_loop(0, 8, sums_two, 0)
    lax.fori_loop(0, 4, send_three, 0, unroll=2)
    x23_left = remote(10, x23sl, x23rr, "xl")
    x23_right = remote(11, x23sr, x23rl, "xr")
    x3_left = remote(12, x3sl, x3rr, "xll")
    x3_right = remote(13, x3sr, x3rl, "xrr")
    for copy in (x23_left, x23_right, x3_left, x3_right):
        copy.start()
    lax.fori_loop(0, NX, finish_z1, 0)
    for copy in (x1_left, x1_right, xe_left, xe_right):
        copy.wait()
    for xf in range(2):
        for t in range(2):
            for ref, ends in ((x1rl, xerl), (x1rr, xerr)):
                at = (xf * 2 + t) * 4
                refs = {"from_left": ends.at[pl.ds(at, 2)], "from_right": ends.at[pl.ds(at + 2, 2)]}
                correct(ref, xf * 256 + 128 * t, SIDES[NZ][0], z_places[0], ztab, refs, lambda f: f)
    for copy in (x23_left, x23_right, x3_left, x3_right):
        copy.wait()


def paired(weights, rows):
    low_lanes = lanes_of((8, 128)) < 64
    total = jnp.zeros((8, 128), F32)
    for p in range(NX // 2):
        if weights[2 * p] == 0.0 and weights[2 * p + 1] == 0.0:
            continue
        total = total + jnp.where(low_lanes, weights[2 * p], weights[2 * p + 1]) * rows[p]
    return total + pltpu.roll(total, 64, 1)


def sums_three(matrix, rows):
    low_lanes = lanes_of((8, 128)) < 64
    return [jnp.where(low_lanes, paired(matrix[2 * h], rows), paired(matrix[2 * h + 1], rows)) for h in range(2)]


def finish(w1, w2, w3, x1rl, x1rr, x23rl, x23rr, x3rl, x3rr, out1, out2, out3, out4, o1, o2, o3, o4, sems):
    lane = lanes_of((8, 128))
    low_lanes = lane < 64
    copies = []

    def send(src, dst):
        copy = pltpu.make_async_copy(src, dst, sems.at[len(copies)])
        copy.start()
        copies.append(copy)

    for hy in range(2):
        for hz in range(2):

            def out_one(g, c, hy=hy, hz=hz):
                row = 128 * hy + 64 * hz + 8 * g
                rows = [w1[pl.ds(x * 256 + row, 8), :] for x in range(NX)]
                left = [x1rl[pl.ds(f * 256 + row, 8), :] for f in range(2)]
                right = [x1rr[pl.ds(f * 256 + row, 8), :] for f in range(2)]
                for i, value in enumerate(lift_major(rows)):
                    hx = i // 8
                    band = 4 * hx + 2 * hy + hz
                    if not band:
                        continue
                    value = fir([1.0] + X_ONE_FROM_LEFT[i] + X_ONE_FROM_RIGHT[i], [value] + left + right)
                    value = value * (SCALES[0][hx] * SCALES[0][hy] * SCALES[0][hz])
                    o1[pl.ds((band - 1) * 512 + (i % 8) * 64 + 8 * g, 8), :] = value
                return c

            lax.fori_loop(0, 8, out_one, 0)
            for hx in range(2):
                band = 4 * hx + 2 * hy + hz
                if band:
                    at = pl.ds((band - 1) * 512, 512)
                    send(o1.at[at], out1.at[at])

    def out_two(g, hz):
        rows = [w2[pl.ds(x * 64 + 8 * g, 8), :] for x in range(NX)]
        left = [x23rl[pl.ds(f * 64 + 8 * g, 8), :] for f in range(N_TWO)]
        right = [x23rr[pl.ds(f * 64 + 8 * g, 8), :] for f in range(N_TWO)]
        for i in range(8):
            hx = i // 4
            value = fir(X_TWO_OWN[i] + X_TWO_FROM_LEFT[i] + X_TWO_FROM_RIGHT[i], rows + left + right)
            scale = SCALES[1][hx] * SCALES[1][hz]
            value = value * jnp.where(low_lanes, scale * SCALES[1][0], scale * SCALES[1][1])
            for hy in range(2):
                band = 4 * hx + 2 * hy + hz
                if band:
                    at = (band - 1) * 128 + (i % 4) * 32 + 8 * (g % 4)
                    o2[pl.ds(at, 8), :] = value[:, 64 * hy : 64 * hy + 64]

    for g in range(8):
        out_two(g, g // 4)
    send(o2, out2)

    def out_three(g, hz):
        rows = [w3[pl.ds(p * 32 + 8 * g, 8), :] for p in range(NX // 2)]
        own = sums_three(X_THREE[2], rows)
        high_y = (lane & 63) >= 32
        for hx in range(2):
            value = own[hx]
            for ref, at in ((x23rl, N_TWO * 64), (x23rr, N_TWO * 64), (x3rl, 0), (x3rr, 0)):
                value = value + ref[pl.ds(at + 32 * hx + 8 * g, 8), :]
            scale = SCALES[2][hx] * SCALES[2][hz]
            value = value * jnp.where(high_y, scale * SCALES[2][1], scale * SCALES[2][0])
            for q in range(4):
                i, hy = divmod(q, 2)
                band = 4 * hx + 2 * hy + hz
                row = 16 * i + 8 * (g % 2)
                piece = value[:, 32 * q : 32 * q + 32]
                if band:
                    o3[pl.ds((band - 1) * 32 + row, 8), :] = piece
                else:
                    o4[pl.ds(row, 8), :] = piece

    for g in range(4):
        out_three(g, g // 2)
    send(o3, out3)
    send(o4, out4)
    for copy in copies:
        copy.wait()


def shards(velocity):
    vmem, hbm = pl.BlockSpec(memory_space=pltpu.VMEM), pl.BlockSpec(memory_space=pltpu.HBM)
    wide = lambda rows: pltpu.VMEM((rows, 128), F32)
    results = [32 * NZ, 16 * 64, 8 * 32, 512, 512, X23_ROWS, X23_ROWS, 64, 64]
    scratch = [16 * NY, 16 * NY, 16 * NY // 2, 16 * NY // 4]
    scratch += [32 * NZ, 16 * NZ, 8 * NZ]
    scratch += [16 * 64, 8 * 64, 8 * 32]
    scratch += [table_rows(SIDES[NY]), table_rows(SIDES[NZ])]
    scratch += [Y_ROWS] * 2 + [128] * 2 + [Z_ROWS] * 6
    scratch += [128, 128, 256, 128, 64, 128, 64, 3 * 128, 6 * 64, 12 * 32] + [16] * 6
    scratch += [512] * 2 + [X23_ROWS] * 2 + [64] * 2 + [16] * 4
    operands = [velocity.reshape(NX * NY, NZ), *[jnp.asarray(matrix) for matrix in SPREADS], jnp.asarray(Z_SENDS)]
    got = pl.pallas_call(
        kernel,
        out_shape=[jax.ShapeDtypeStruct((rows, 128), F32) for rows in results],
        in_specs=[hbm] * 5,
        out_specs=[vmem] * len(results),
        scratch_shapes=[wide(rows) for rows in scratch]
        + [pltpu.VMEM(matrix.shape, jnp.bfloat16) for matrix in SPREADS]
        + [wide(32)]
        + [pltpu.SemaphoreType.DMA((5,)), pltpu.SemaphoreType.DMA((14,)), pltpu.SemaphoreType.DMA((14,))],
        compiler_params=pltpu.CompilerParams(collective_id=0, has_side_effects=True, vmem_limit_bytes=28 * 2**20),
    )(*[pltpu.with_memory_space_constraint(a, pltpu.HBM) for a in operands])
    shapes = [(7 * 8 * 64, 128), (7 * 4 * 32, 64), (7 * 2 * 16, 32), (2 * 16, 32)]
    out1, out2, out3, out4 = pl.pallas_call(
        finish,
        out_shape=[jax.ShapeDtypeStruct(shape, F32) for shape in shapes],
        in_specs=[vmem] * len(results),
        out_specs=[hbm] * 4,
        scratch_shapes=[pltpu.VMEM(shape, F32) for shape in shapes] + [pltpu.SemaphoreType.DMA((10,))],
        compiler_params=pltpu.CompilerParams(vmem_limit_bytes=16 * 2**20),
    )(*got)
    return (
        out1.reshape(7, 8, 64, 128).transpose(0, 1, 3, 2),
        out2.reshape(7, 4, 32, 64).transpose(0, 1, 3, 2),
        out3.reshape(7, 2, 16, 32).transpose(0, 1, 3, 2),
        out4.reshape(2, 16, 32).transpose(0, 2, 1),
    )


def solution(mesh):
    return jax.shard_map(
        shards,
        mesh=mesh,
        in_specs=(P("gx", "gy", "gz"),),
        out_specs=(
            P(None, "gx", "gy", "gz"),
            P(None, "gx", "gy", "gz"),
            P(None, "gx", "gy", "gz"),
            P("gx", "gy", "gz"),
        ),
        check_vma=False,
    )
```

```python
import math

import jax
import jax.numpy as jnp
import ml_dtypes
import numpy as np
from jax import lax
from jax.experimental import pallas as pl
from jax.experimental.pallas import tpu as pltpu
from jax.sharding import PartitionSpec as P

ALPHA = -1.586134342059924
BETA = -0.052980118572961
GAMMA = 0.882911075530934
DELTA = 0.443506852043971
SCALE_LOW = math.sqrt(2.0) / 1.230174104914001
SCALE_HIGH = 1.230174104914001 / math.sqrt(2.0)


def lift_matrix(rows, edges):
    s, d = rows[0::2], rows[1::2]
    none = np.zeros_like(s[:1])
    if edges == "periodic":
        d = d + ALPHA * (s + np.roll(s, -1, 0))
        s = s + BETA * (np.roll(d, 1, 0) + d)
        d = d + GAMMA * (s + np.roll(s, -1, 0))
        s = s + DELTA * (np.roll(d, 1, 0) + d)
        return s, d
    start, end = edges
    up = lambda v, last: np.concatenate([v[1:], last])
    down = lambda v, first: np.concatenate([first, v[:-1]])
    d1 = d + ALPHA * (s + up(s, s[-1:] if end else none))
    before1 = d1[:1] if start else ALPHA * s[:1]
    s1 = s + BETA * (down(d1, before1) + d1)
    d2 = d1 + GAMMA * (s1 + up(s1, s1[-1:] if end else BETA * d1[-1:]))
    before2 = d2[:1] if start else before1 + GAMMA * (BETA * before1 + s1[:1])
    return s1 + DELTA * (down(d2, before2) + d2), d2


def path_matrix(rows, level, edges):
    for _ in range(level):
        rows, high = lift_matrix(rows, edges)
    return np.concatenate([rows, high])


def outgoing(n):
    rows, left, right = np.eye(n), [], []
    for _ in range(3):
        s, d = rows[0::2], rows[1::2]
        left += [s[0], s[0] + BETA * (d[0] + ALPHA * (s[0] + s[1]))]
        right += [d[-1] + ALPHA * s[-1], s[-1] + BETA * (d[-2] + ALPHA * (s[-2] + s[-1]))]
        rows = lift_matrix(rows, (False, False))[0]
    return np.stack(left), np.stack(right)


def line_blocks(n, level):
    m = n >> level
    rows = np.eye(5 * n)
    for _ in range(level):
        rows, high = lift_matrix(rows, "periodic")
    whole = np.concatenate([rows[2 * m : 3 * m], high[2 * m : 3 * m]])
    return [whole[:, k * n : (k + 1) * n] for k in range(5)]


def solved(target, basis):
    u = np.linalg.lstsq(basis.T, target.T, rcond=None)[0].T
    assert np.abs(u @ basis - target).max() < 1e-9
    return np.where(np.abs(u) < 1e-10, 0.0, u)


def block_plan(n, level):
    left, right = outgoing(n)
    left, right = left[: 2 * level], right[: 2 * level]
    blocks = line_blocks(n, level)
    alone = path_matrix(np.eye(n), level, (False, False))
    from_left = solved(blocks[1], right)
    from_right = solved(blocks[3], left)
    own = solved(blocks[2] - alone, np.concatenate([left, right]))
    return dict(left=left, right=right, alone=alone, from_left=from_left, from_right=from_right, own_left=own[:, : 2 * level], own_right=own[:, 2 * level :])


def mirror_plan(n, plans):
    out = []
    for start in (True, False):
        uses, rests = [], []
        for level, plan in enumerate(plans, 1):
            m = n >> level
            rows = np.eye(4 * n)
            for _ in range(level):
                rows, high = lift_matrix(rows, (True, True))
            at = 0 if start else 3
            whole = np.concatenate([rows[at * m : (at + 1) * m], high[at * m : (at + 1) * m]])
            whole = whole[:, at * n : (at + 1) * n]
            rests.append(whole - plan["alone"] - plan["own_left"] @ plan["left"] - plan["own_right"] @ plan["right"])
            u = plan["from_left"] if start else plan["from_right"]
            uses.append(np.pad(u, ((0, 0), (0, 6 - u.shape[1]))))
        use, rest = np.concatenate(uses), np.concatenate(rests)
        g = np.linalg.lstsq(use, rest, rcond=None)[0]
        assert np.abs(use @ g - rest).max() < 1e-9
        out.append(np.where(np.abs(g) < 1e-10, 0.0, g))
    return out


MESH = pl.DeviceIdType.MESH
SIZES = {"gx": 8, "gy": 4, "gz": 4}
NX, NY, NZ = 16, 256, 128
F32 = jnp.float32


def rounded(matrix):
    return [[float(np.float32(c)) if abs(c) > 1e-10 else 0.0 for c in row] for row in matrix]


def fir(weights, rows):
    total = None
    for weight, row in zip(weights, rows):
        if weight == 0.0:
            continue
        term = row() if callable(row) else row
        term = term if weight == 1.0 else weight * term
        total = term if total is None else total + term
    return total


def lift_list(s, d, up, down, first, last):
    before1 = ALPHA * first(s)
    d1 = [b + ALPHA * (a + c) for a, b, c in zip(s, d, up(s, None))]
    s1 = [a + BETA * (b + c) for a, b, c in zip(s, d1, down(d1, before1))]
    d2 = [b + GAMMA * (a + c) for a, b, c in zip(s1, d1, up(s1, BETA * last(d1)))]
    before2 = before1 + GAMMA * (BETA * before1 + first(s1))
    s2 = [a + DELTA * (b + c) for a, b, c in zip(s1, d2, down(d2, before2))]
    return s2, d2


def lift_rows(src, base, n, dst, to, keep_high=True):
    k = n // 16
    s = [src[pl.ds(base + 16 * i, 8, stride=2), :] for i in range(k)]
    d = [src[pl.ds(base + 16 * i + 1, 8, stride=2), :] for i in range(k)]
    sub = lax.broadcasted_iota(jnp.int32, (8, 128), 0)
    top, bottom = sub == 0, sub == 7

    def up(v, fill):
        r = [pltpu.roll(x, 7, 0) for x in v]
        fill = jnp.zeros((8, 128), F32) if fill is None else fill
        return [jnp.where(bottom, r[i + 1] if i + 1 < k else fill, r[i]) for i in range(k)]

    def down(v, fill):
        r = [pltpu.roll(x, 1, 0) for x in v]
        return [jnp.where(top, r[i - 1] if i else fill, r[i]) for i in range(k)]

    low, high = lift_list(s, d, up, down, lambda v: v[0], lambda v: v[-1])
    for i in range(k):
        dst[pl.ds(to + 8 * i, 8), :] = low[i]
        if keep_high:
            dst[pl.ds(to + 8 * (k + i), 8), :] = high[i]


def lift_major(rows):
    low, high = lift_list(
        rows[0::2],
        rows[1::2],
        lambda v, fill: v[1:] + [jnp.zeros_like(v[0]) if fill is None else fill],
        lambda v, fill: [fill] + v[:-1],
        lambda v: v[0],
        lambda v: v[-1],
    )
    return low + high


class Side:
    def __init__(self, plan):
        self.groups = {}
        for source in ("from_left", "from_right", "own_left", "own_right"):
            u = plan[source]
            for g in range(u.shape[0] // 8):
                for f in range(u.shape[1]):
                    column = u[8 * g : 8 * g + 8, f]
                    if np.abs(column).max() > 1e-10:
                        self.groups.setdefault(g, []).append((source, f, column))


PLANS = {n: [block_plan(n, level) for level in (1, 2, 3)] for n in (NY, NZ)}
SIDES = {n: [Side(plan) for plan in PLANS[n]] for n in (NY, NZ)}
MIRRORS = mirror_plan(NZ, PLANS[NZ])
SEND_LEFT = {n: rounded(PLANS[n][2]["left"]) for n in (NY, NZ)}
SEND_RIGHT = {n: rounded(PLANS[n][2]["right"]) for n in (NY, NZ)}
SCALES = [(SCALE_LOW**level, SCALE_LOW ** (level - 1) * SCALE_HIGH) for level in (1, 2, 3)]


def factored(matrix):
    u, size, v = np.linalg.svd(matrix, full_matrices=False)
    rank = int((size > 1e-9).sum())
    return rounded(u[:, :rank] * size[:rank]), rounded(v[:rank])


X_ONE = block_plan(NX, 1)
X_ONE_LEFT, X_ONE_RIGHT = rounded(X_ONE["left"]), rounded(X_ONE["right"])
X_ONE_FROM_LEFT, X_ONE_FROM_RIGHT = rounded(X_ONE["from_left"]), rounded(X_ONE["from_right"])
X_TWO_BLOCKS = line_blocks(NX, 2)
X_TWO_FROM_LEFT, X_TWO_RIGHT = factored(X_TWO_BLOCKS[1])
X_TWO_FROM_RIGHT, X_TWO_LEFT = factored(X_TWO_BLOCKS[3])
X_TWO_OWN = rounded(X_TWO_BLOCKS[2])
X_THREE = [rounded(block) for block in line_blocks(NX, 3)]
N_TWO = len(X_TWO_RIGHT)

Y_ROWS = 6 * NX
Z_TWO, Z_THREE, Z_ROWS = 4 * NX, 8 * NX, 8 * NX + 6 * (NX // 2)
X23_ROWS = N_TWO * 64 + 64


def neighbour(axis, step):
    size = SIZES[axis]
    place = {name: lax.axis_index(name) for name in SIZES}
    place[axis] = lax.rem(place[axis] + (step + size), size)
    return tuple(place[name] for name in ("gx", "gy", "gz"))


def build_table(table, sides):
    sub = lax.broadcasted_iota(jnp.int32, (8, 128), 0)
    found = []
    at = 0
    for side in sides:
        places = {}
        for g, terms in side.groups.items():
            for source, f, column in terms:
                value = jnp.zeros((8, 128), F32)
                for i in range(8):
                    if abs(column[i]) > 1e-10:
                        value = jnp.where(sub == i, float(np.float32(column[i])), value)
                table[pl.ds(at, 8), :] = value
                places[g, source, f] = at
                at += 8
        found.append(places)
    return found


def table_rows(sides):
    return 8 * sum(len(terms) for side in sides for terms in side.groups.values())


def correct(ref, base, side, places, table, refs, row):
    for g, terms in side.groups.items():
        terms = [(source, f) for source, f, _ in terms if source in refs]
        if not terms:
            continue
        value = ref[pl.ds(base + 8 * g, 8), :]
        for source, f in terms:
            value = value + table[pl.ds(places[g, source, f], 8), :] * refs[source][pl.ds(row(f), 1), :]
        ref[pl.ds(base + 8 * g, 8), :] = value


def parts_of(value):
    rest, parts = np.asarray(value, np.float32), []
    for _ in range(3):
        part = rest.astype(ml_dtypes.bfloat16)
        parts.append(part)
        rest = rest - part.astype(np.float32)
    return parts


def spread(level):
    plan = PLANS[NY][level - 1]
    left, right = plan["from_left"].T, plan["from_right"].T
    if level == 3:
        blocks = []
        for u in (left, right):
            block = np.zeros((8, NX, 128))
            block[:6, 0::2, :64] = u[:, None, :]
            block[:6, 1::2, 64:] = u[:, None, :]
            blocks.append(block.reshape(128, 128))
        matrix = np.concatenate(blocks)
    else:
        matrix = np.repeat(np.concatenate([left, right]), NX, axis=0)
    one, two, three = parts_of(matrix)
    return np.concatenate([one, two, three, one, two, one])


SPREADS = [spread(level) for level in (1, 2, 3)]
Z_SENDS = np.zeros((40, NZ), np.float32)
for _at, _rows in enumerate((PLANS[NZ][2]["left"], PLANS[NZ][2]["right"], *MIRRORS)):
    Z_SENDS[8 * _at : 8 * _at + 6] = _rows
for _at, _rows in enumerate((X_ONE["left"], X_ONE["right"])):
    for _xf in range(2):
        for _f in range(2):
            Z_SENDS[32 + 4 * _at + 2 * _xf + _f, _f * NX : (_f + 1) * NX] = _rows[_xf]


def split(value):
    one = value.astype(jnp.bfloat16).astype(F32)
    two = (value - one).astype(jnp.bfloat16).astype(F32)
    return one, two, value - one - two


def lanes_of(shape):
    return lax.broadcasted_iota(jnp.int32, shape, 1)


def slots(level, left, right):
    lane = lanes_of(left.shape)
    turn = lambda value, by: pltpu.roll(value, by, 1)
    if level == 1:
        base = left if right is None else jnp.where(lane < 32, left, jnp.where(lane < 64, turn(right, 32), 0.0))
        one, two, three = split(base)
        return [one + turn(one, 64), one + turn(two, 64), two + turn(three, 64)]
    if level == 2:
        one, two, three = split(jnp.where(lane < 64, left, turn(right, 64)))
        return [one, one, one, two, two, three]
    one, two, three = zip(split(left), split(right))
    return [*one, *one, *one, *two, *two, *three]


def expand(level, arrays, keep, spread_ref):
    factor = jnp.concatenate([jnp.where(keep, a, 0.0).astype(jnp.bfloat16) for a in arrays], axis=1)
    return jnp.dot(factor, spread_ref[...], preferred_element_type=F32)


def kernel(
    vel, spread1_hbm, spread2_hbm, spread3_hbm, sends_hbm,
    o1, o2, o3, o4,
    w1, w2, w3, x1rl, x1rr, x23rl, x23rr, x3rl, x3rr, eg,
    v, y1, y2, y3, z1, z2, z3, t2, t3, t4, ytab, ztab,
    ysl, ysr, yrl, yrr, zsl, zsr, zrl, zrr, zml, zmr,
    htl, htr, g1, g2, g3, u2, u3, p1, p2, p3, zlsl, zlsr, zlrl, zlrr, zlml, zlmr,
    x1sl, x1sr, x23sl, x23sr, x3sl, x3sr, xesl, xesr, xerl, xerr,
    spread1, spread2, spread3, sends,
    load_sems, send_sems, recv_sems,
):
    loads = [
        pltpu.make_async_copy(src, dst, load_sems.at[i])
        for i, (src, dst) in enumerate(
            ((vel, v), (sends_hbm, sends), (spread1_hbm, spread1), (spread2_hbm, spread2), (spread3_hbm, spread3))
        )
    ]
    for load in loads:
        load.start()
    near = {
        "yl": neighbour("gy", -1), "yr": neighbour("gy", 1), "zl": neighbour("gz", -1), "zr": neighbour("gz", 1),
        "xl": neighbour("gx", -1), "xr": neighbour("gx", 1), "xll": neighbour("gx", -2), "xrr": neighbour("gx", 2),
    }
    barrier = pltpu.get_barrier_semaphore()
    for device in near.values():
        pl.semaphore_signal(barrier, inc=1, device_id=device, device_id_type=MESH)
    y_places = build_table(ytab, SIDES[NY])
    z_places = build_table(ztab, SIDES[NZ])
    for ref in (yrl, yrr):
        ref[pl.ds(Y_ROWS, 32), :] = jnp.zeros((32, 128), F32)
    eg[...] = jnp.zeros((128, 128), F32)

    def remote(index, src, dst, to):
        return pltpu.make_async_remote_copy(
            src_ref=src,
            dst_ref=dst,
            send_sem=send_sems.at[index],
            recv_sem=recv_sems.at[index],
            device_id=near[to],
            device_id_type=MESH,
        )

    loads[0].wait()

    for h in range(2):
        head = [v[pl.ds(h * 8 * NY + k, 8, stride=NY), :] for k in range(21)]
        tail = [v[pl.ds(h * 8 * NY + k, 8, stride=NY), :] for k in range(NY - 28, NY)]
        for f in range(6):
            ysl[pl.ds(f * NX + 8 * h, 8), :] = fir(SEND_LEFT[NY][f][:21], head)
            ysr[pl.ds(f * NX + 8 * h, 8), :] = fir(SEND_RIGHT[NY][f][-28:], tail)

    pl.semaphore_wait(barrier, len(near))
    y_left = remote(0, ysl, yrr.at[pl.ds(0, Y_ROWS)], "yl")
    y_right = remote(1, ysr, yrl.at[pl.ds(0, Y_ROWS)], "yr")
    y_left.start()
    y_right.start()

    def lift_y(x, c):
        lift_rows(v, x * NY, NY, y1, x * NY)
        lift_rows(y1, x * NY, NY // 2, y2, x * (NY // 2))
        lift_rows(y2, x * (NY // 2), NY // 4, y3, x * (NY // 4))
        own = {"own_left": ysl, "own_right": ysr}
        for level, ref in ((1, y2), (2, y3)):
            correct(ref, x * (NY >> level), SIDES[NY][level], y_places[level], ytab, own, lambda f: f * NX + x)
        return c

    lax.fori_loop(0, NX, lift_y, 0, unroll=2)
    def turn_one(x, c):
        for t in range(2):
            z1[pl.ds(x * 256 + 128 * t, 128), :] = y1[pl.ds(x * NY + 128 * t, 128), :].T
        return c

    def turn_two(x, c):
        z2[pl.ds(x * 128, 128), :] = y2[pl.ds(x * 128, 128), :].T
        return c

    def turn_three(p, c):
        z3[pl.ds(p * 128, 128), :] = y3[pl.ds(p * 128, 128), :].T
        return c

    def z_sums(level, load_row, store):
        rows = {}

        def row(k):
            if k not in rows:
                rows[k] = load_row(k)
            return rows[k]

        for f in range(2 * level):
            for at, ref in enumerate((zsl, zsr, zml, zmr)):
                weights = [float(c) for c in Z_SENDS[8 * at + f]]
                ks = [k for k in range(NZ) if weights[k] != 0.0]
                store(ref, f, fir([weights[k] for k in ks], [row(k) for k in ks]))

    lax.fori_loop(0, NX // 2, turn_three, 0, unroll=8)
    lax.fori_loop(0, NX, turn_two, 0, unroll=8)

    def store_three(ref, f, value):
        ref[pl.ds(Z_THREE + f * (NX // 2), 8), :] = value

    z_sums(3, lambda k: z3[pl.ds(k, 8, stride=128), :], store_three)
    for h in range(2):

        def store_two(ref, f, value, h=h):
            ref[pl.ds(Z_TWO + f * NX + 8 * h, 8), :] = value

        z_sums(2, lambda k, h=h: z2[pl.ds(h * 8 * 128 + k, 8, stride=128), :], store_two)
    deep = pl.ds(Z_TWO, Z_ROWS - Z_TWO)
    z_left = remote(2, zsl.at[deep], zrr.at[deep], "zl")
    z_right = remote(3, zsr.at[deep], zrl.at[deep], "zr")
    z_left.start()
    z_right.start()

    def lift_z1(i, c):
        lift_rows(z1, i * NZ, NZ, w1, i * NZ)
        return c

    lax.fori_loop(0, NX, turn_one, 0, unroll=4)
    lax.fori_loop(0, 2 * NX, lift_z1, 0, unroll=4)

    def sums_one(g, c):
        rows = [w1[pl.ds(x * 256 + 8 * g, 8), :] for x in (0, 1, 2, 12, 13, 14, 15)]
        for f in range(2):
            x1sl[pl.ds(f * 256 + 8 * g, 8), :] = fir(X_ONE_LEFT[f][:3], rows[:3])
            x1sr[pl.ds(f * 256 + 8 * g, 8), :] = fir(X_ONE_RIGHT[f][12:], rows[3:])
        return c

    lax.fori_loop(0, 32, sums_one, 0, unroll=4)
    x1_left = remote(6, x1sl, x1rr, "xl")
    x1_right = remote(7, x1sr, x1rl, "xr")
    x1_left.start()
    x1_right.start()
    for h in range(2):
        for t in range(2):

            def store_one(ref, f, value, h=h, t=t):
                ref[pl.ds((f * 2 + t) * NX + 8 * h, 8), :] = value

            z_sums(1, lambda k, h=h, t=t: z1[pl.ds(h * 8 * 256 + t * 128 + k, 8, stride=256), :], store_one)
    first = pl.ds(0, Z_TWO)
    z1_left = remote(14, zsl.at[first], zrr.at[first], "zl")
    z1_right = remote(15, zsr.at[first], zrl.at[first], "zr")
    z1_left.start()
    z1_right.start()

    row_one = lambda x, t: lambda f: (f * 2 + t) * NX + x
    row_two = lambda x: lambda f: Z_TWO + f * NX + x
    row_three = lambda p: lambda f: Z_THREE + f * (NX // 2) + p
    z_own = {"own_left": zsl, "own_right": zsr}

    def lift_z2(x, c):
        lift_rows(z2, x * NZ, NZ, t2, x * 64, keep_high=False)
        lift_rows(t2, x * 64, 64, w2, x * 64)
        correct(w2, x * 64, SIDES[NZ][1], z_places[1], ztab, z_own, row_two(x))
        return c

    def lift_z3(p, c):
        lift_rows(z3, p * NZ, NZ, t3, p * 64, keep_high=False)
        lift_rows(t3, p * 64, 64, t4, p * 32, keep_high=False)
        lift_rows(t4, p * 32, 32, w3, p * 32)
        correct(w3, p * 32, SIDES[NZ][2], z_places[2], ztab, z_own, row_three(p))
        return c

    y_left.wait()
    y_right.wait()
    for load in loads[1:]:
        load.wait()
    htl[...] = yrl[...].T
    htr[...] = yrr[...].T
    for at, ref in ((0, htl), (8, htr)):
        sums = jnp.dot(sends[pl.ds(0, 32), :], ref[...], precision=lax.Precision.HIGHEST, preferred_element_type=F32)
        for i, out in enumerate((zlsl, zlsr, zlml, zlmr)):
            out[pl.ds(at, 8), :] = sums[8 * i : 8 * i + 8]
    zl_left = remote(4, zlsl, zlrr, "zl")
    zl_right = remote(5, zlsr, zlrl, "zr")
    zl_left.start()
    zl_right.start()

    lax.fori_loop(0, NX // 2, lift_z3, 0, unroll=4)
    lax.fori_loop(0, NX, lift_z2, 0, unroll=4)

    for i, ref in enumerate((htl, htr)):
        lift_rows(ref, 0, 128, g1, 128 * i)
        lift_rows(g1, 128 * i, 64, u2, 64 * i)
        lift_rows(u2, 64 * i, 32, u3, 32 * i)
    for i in range(2):
        own = {"own_left": zlsl, "own_right": zlsr}
        g2[pl.ds(64 * i, 64), :] = u2[pl.ds(64 * i, 64), :]
        g3[pl.ds(32 * i, 32), :] = u3[pl.ds(32 * i, 32), :]
        correct(g2, 64 * i, SIDES[NZ][1], z_places[1], ztab, own, lambda f, i=i: 8 * i + f)
        correct(g3, 32 * i, SIDES[NZ][2], z_places[2], ztab, own, lambda f, i=i: 8 * i + f)
    for level, g, p, n in ((1, g1, p1, 128), (2, g2, p2, 64), (3, g3, p3, 32)):
        for i, value in enumerate(slots(level, g[pl.ds(0, n), :], g[pl.ds(n, n), :])):
            p[pl.ds(n * i, n), :] = value

    def spread_one(x, c):
        keep = (lanes_of((128, 128)) & 15) == x
        value = expand(1, [p1[pl.ds(128 * i, 128), :] for i in range(3)], keep, spread1)
        for t in range(2):
            at = pl.ds(x * 256 + 128 * t, 128)
            w1[at, :] = w1[at, :] + value[:, 128 * t : 128 * t + 128]
        return c

    def spread_two(x, c):
        keep = (lanes_of((64, 128)) & 15) == x
        at = pl.ds(x * 64, 64)
        w2[at, :] = w2[at, :] + expand(2, [p2[pl.ds(64 * i, 64), :] for i in range(6)], keep, spread2)
        return c

    def spread_three(p, c):
        keep = ((lanes_of((32, 128)) & 15) >> 1) == p
        at = pl.ds(p * 32, 32)
        w3[at, :] = w3[at, :] + expand(3, [p3[pl.ds(32 * i, 32), :] for i in range(12)], keep, spread3)
        return c

    lax.fori_loop(0, NX // 2, spread_three, 0, unroll=8)
    lax.fori_loop(0, NX, spread_two, 0, unroll=8)

    for copy in (z_left, z_right, z1_left, z1_right, zl_left, zl_right):
        copy.wait()
    gz = lax.axis_index("gz")

    @pl.when(gz == 0)
    def _():
        zrl[...] = zml[...]
        zlrl[...] = zlml[...]

    @pl.when(gz == SIZES["gz"] - 1)
    def _():
        zrr[...] = zmr[...]
        zlrr[...] = zlmr[...]

    lane, sub = lanes_of((16, 128)), lax.broadcasted_iota(jnp.int32, (16, 128), 0)
    for late, ref in ((zlrl, zrl), (zlrr, zrr)):
        left, right = late[pl.ds(0, 8), :], late[pl.ds(8, 8), :]
        for level, spread_ref, count in ((3, spread3, 8), (2, spread2, NX), (1, spread1, NX)):
            arrays = slots(level, left, right)
            if level == 3:
                keep = ((lane[:8] & 15) >> 1) == sub[:8]
            else:
                keep = (lane & 15) == sub
            tall = [
                jnp.concatenate([jnp.where(keep, a[f : f + 1], 0.0) for f in range(2 * level)], axis=0) for a in arrays
            ]
            value = expand(level, tall, jnp.full(tall[0].shape, True), spread_ref)
            for f in range(2 * level):
                piece = value[f * count : f * count + count]
                if level == 1:
                    for t in range(2):
                        at = pl.ds((f * 2 + t) * NX, NX)
                        ref[at, :] = ref[at, :] + piece[:, 128 * t : 128 * t + 128]
                else:
                    at = pl.ds((Z_TWO if level == 2 else Z_THREE) + f * count, count)
                    ref[at, :] = ref[at, :] + piece

    sums = lax.dot_general(
        sends[pl.ds(32, 8), :],
        g1[...],
        (((1,), (1,)), ((), ())),
        precision=lax.Precision.HIGHEST,
        preferred_element_type=F32,
    )
    for way, ref in enumerate((xesl, xesr)):
        for xf in range(2):
            for side in range(2):
                at = 4 * way + 2 * xf
                ref[pl.ds(16 + 4 * xf + 2 * side, 2), :] = sums[at : at + 2, 128 * side : 128 * side + 128]

    for side, ref in enumerate((zrl, zrr)):
        for f in range(2):
            for t in range(2):
                rows = [ref[pl.ds((f * 2 + t) * NX + x, 1), :] for x in (0, 1, 2, 12, 13, 14, 15)]
                for xf in range(2):
                    at = pl.ds((xf * 2 + t) * 4 + side * 2 + f, 1)
                    xesl[at, :] = fir(X_ONE_LEFT[xf][:3], rows[:3])
                    xesr[at, :] = fir(X_ONE_RIGHT[xf][12:], rows[3:])
    xe_left = remote(8, xesl, xerr, "xl")
    xe_right = remote(9, xesr, xerl, "xr")
    xe_left.start()
    xe_right.start()

    z_past = {"from_left": zrl, "from_right": zrr}

    def finish_z2(x, c):
        correct(w2, x * 64, SIDES[NZ][1], z_places[1], ztab, z_past, row_two(x))
        return c

    def finish_z3(p, c):
        correct(w3, p * 32, SIDES[NZ][2], z_places[2], ztab, z_past, row_three(p))
        return c

    def finish_z1(x, c):
        for t in range(2):
            correct(w1, x * 256 + 128 * t, SIDES[NZ][0], z_places[0], ztab, z_past, row_one(x, t))
        return c

    lax.fori_loop(0, NX // 2, finish_z3, 0, unroll=2)
    lax.fori_loop(0, NX, finish_z2, 0, unroll=4)

    def sums_two(g, c):
        rows = [w2[pl.ds(x * 64 + 8 * g, 8), :] for x in range(NX)]
        for f in range(N_TWO):
            x23sl[pl.ds(f * 64 + 8 * g, 8), :] = fir(X_TWO_LEFT[f], rows)
            x23sr[pl.ds(f * 64 + 8 * g, 8), :] = fir(X_TWO_RIGHT[f], rows)
        return c

    def send_three(g, c):
        rows = [w3[pl.ds(p * 32 + 8 * g, 8), :] for p in range(NX // 2)]
        for ref, block, at in ((x23sr, 1, N_TWO * 64), (x23sl, 3, N_TWO * 64), (x3sr, 0, 0), (x3sl, 4, 0)):
            for h, value in enumerate(sums_three(X_THREE[block], rows)):
                ref[pl.ds(at + 32 * h + 8 * g, 8), :] = value
        return c

    lax.fori_loop(0, 8, sums_two, 0)
    lax.fori_loop(0, 4, send_three, 0, unroll=2)
    x23_left = remote(10, x23sl, x23rr, "xl")
    x23_right = remote(11, x23sr, x23rl, "xr")
    x3_left = remote(12, x3sl, x3rr, "xll")
    x3_right = remote(13, x3sr, x3rl, "xrr")
    for copy in (x23_left, x23_right, x3_left, x3_right):
        copy.start()
    lax.fori_loop(0, NX, spread_one, 0, unroll=4)
    lax.fori_loop(0, NX, finish_z1, 0)
    for copy in (x1_left, x1_right, xe_left, xe_right):
        copy.wait()
    for side, ends in enumerate((xerl, xerr)):
        for xf in range(2):
            for h in range(4):
                eg[pl.ds(NX * h + 2 * side + xf, 1), :] = ends[pl.ds(16 + 4 * xf + h, 1), :]
    arrays = slots(1, eg[...].T, None)
    for side, ref in enumerate((x1rl, x1rr)):
        for xf in range(2):
            value = expand(1, arrays, (lanes_of((128, 128)) & 15) == 2 * side + xf, spread1)
            for t in range(2):
                at = pl.ds(xf * 256 + 128 * t, 128)
                ref[at, :] = ref[at, :] + value[:, 128 * t : 128 * t + 128]
    for xf in range(2):
        for t in range(2):
            for ref, ends in ((x1rl, xerl), (x1rr, xerr)):
                at = (xf * 2 + t) * 4
                refs = {"from_left": ends.at[pl.ds(at, 2)], "from_right": ends.at[pl.ds(at + 2, 2)]}
                correct(ref, xf * 256 + 128 * t, SIDES[NZ][0], z_places[0], ztab, refs, lambda f: f)
    for hy in range(2):
        for hz in range(2):

            def out_one(g, c, hy=hy, hz=hz):
                row = 128 * hy + 64 * hz + 8 * g
                rows = [w1[pl.ds(x * 256 + row, 8), :] for x in range(NX)]
                left = [x1rl[pl.ds(f * 256 + row, 8), :] for f in range(2)]
                right = [x1rr[pl.ds(f * 256 + row, 8), :] for f in range(2)]
                for i, value in enumerate(lift_major(rows)):
                    hx = i // 8
                    band = 4 * hx + 2 * hy + hz
                    if not band:
                        continue
                    value = fir([1.0] + X_ONE_FROM_LEFT[i] + X_ONE_FROM_RIGHT[i], [value] + left + right)
                    value = value * (SCALES[0][hx] * SCALES[0][hy] * SCALES[0][hz])
                    o1[pl.ds((band - 1) * 512 + (i % 8) * 64 + 8 * g, 8), :] = value
                return c

            lax.fori_loop(0, 8, out_one, 0, unroll=2)
    for copy in (x23_left, x23_right, x3_left, x3_right):
        copy.wait()
    lane = lanes_of((8, 128))
    low_lanes = lane < 64

    def out_two(g, hz):
        rows = [w2[pl.ds(x * 64 + 8 * g, 8), :] for x in range(NX)]
        left = [x23rl[pl.ds(f * 64 + 8 * g, 8), :] for f in range(N_TWO)]
        right = [x23rr[pl.ds(f * 64 + 8 * g, 8), :] for f in range(N_TWO)]
        for i in range(8):
            hx = i // 4
            value = fir(X_TWO_OWN[i] + X_TWO_FROM_LEFT[i] + X_TWO_FROM_RIGHT[i], rows + left + right)
            scale = SCALES[1][hx] * SCALES[1][hz]
            value = value * jnp.where(low_lanes, scale * SCALES[1][0], scale * SCALES[1][1])
            for hy in range(2):
                band = 4 * hx + 2 * hy + hz
                if band:
                    at = (band - 1) * 128 + (i % 4) * 32 + 8 * (g % 4)
                    o2[pl.ds(at, 8), :] = value[:, 64 * hy : 64 * hy + 64]

    for g in range(8):
        out_two(g, g // 4)

    def out_three(g, hz):
        rows = [w3[pl.ds(p * 32 + 8 * g, 8), :] for p in range(NX // 2)]
        own = sums_three(X_THREE[2], rows)
        high_y = (lane & 63) >= 32
        for hx in range(2):
            value = own[hx]
            for ref, at in ((x23rl, N_TWO * 64), (x23rr, N_TWO * 64), (x3rl, 0), (x3rr, 0)):
                value = value + ref[pl.ds(at + 32 * hx + 8 * g, 8), :]
            scale = SCALES[2][hx] * SCALES[2][hz]
            value = value * jnp.where(high_y, scale * SCALES[2][1], scale * SCALES[2][0])
            for q in range(4):
                i, hy = divmod(q, 2)
                band = 4 * hx + 2 * hy + hz
                row = 16 * i + 8 * (g % 2)
                piece = value[:, 32 * q : 32 * q + 32]
                if band:
                    o3[pl.ds((band - 1) * 32 + row, 8), :] = piece
                else:
                    o4[pl.ds(row, 8), :] = piece

    for g in range(4):
        out_three(g, g // 2)


def paired(weights, rows):
    low_lanes = lanes_of((8, 128)) < 64
    total = jnp.zeros((8, 128), F32)
    for p in range(NX // 2):
        if weights[2 * p] == 0.0 and weights[2 * p + 1] == 0.0:
            continue
        total = total + jnp.where(low_lanes, weights[2 * p], weights[2 * p + 1]) * rows[p]
    return total + pltpu.roll(total, 64, 1)


def sums_three(matrix, rows):
    low_lanes = lanes_of((8, 128)) < 64
    return [jnp.where(low_lanes, paired(matrix[2 * h], rows), paired(matrix[2 * h + 1], rows)) for h in range(2)]


def write(o1, o2, o3, o4, out1, out2, out3, out4, sems):
    copies = []
    for src, dst, parts in ((o1, out1, 7), (o2, out2, 1), (o3, out3, 1), (o4, out4, 1)):
        rows = src.shape[0] // parts
        for i in range(parts):
            at = pl.ds(i * rows, rows)
            copies.append(pltpu.make_async_copy(src.at[at], dst.at[at], sems.at[len(copies)]))
            copies[-1].start()
    for copy in copies:
        copy.wait()


def shards(velocity):
    vmem, hbm = pl.BlockSpec(memory_space=pltpu.VMEM), pl.BlockSpec(memory_space=pltpu.HBM)
    wide = lambda rows: pltpu.VMEM((rows, 128), F32)
    shapes = [(7 * 8 * 64, 128), (7 * 4 * 32, 64), (7 * 2 * 16, 32), (2 * 16, 32)]
    scratch = [32 * NZ, 16 * 64, 8 * 32, 512, 512, X23_ROWS, X23_ROWS, 64, 64, 128]
    scratch += [16 * NY, 16 * NY, 16 * NY // 2, 16 * NY // 4]
    scratch += [32 * NZ, 16 * NZ, 8 * NZ]
    scratch += [16 * 64, 8 * 64, 8 * 32]
    scratch += [table_rows(SIDES[NY]), table_rows(SIDES[NZ])]
    scratch += [Y_ROWS] * 2 + [128] * 2 + [Z_ROWS] * 6
    scratch += [128, 128, 256, 128, 64, 128, 64, 3 * 128, 6 * 64, 12 * 32] + [16] * 6
    scratch += [512] * 2 + [X23_ROWS] * 2 + [64] * 2 + [24] * 4
    operands = [velocity.reshape(NX * NY, NZ), *[jnp.asarray(matrix) for matrix in SPREADS], jnp.asarray(Z_SENDS)]
    got = pl.pallas_call(
        kernel,
        out_shape=[jax.ShapeDtypeStruct(shape, F32) for shape in shapes],
        in_specs=[hbm] * 5,
        out_specs=[vmem] * 4,
        scratch_shapes=[wide(rows) for rows in scratch]
        + [pltpu.VMEM(matrix.shape, jnp.bfloat16) for matrix in SPREADS]
        + [wide(40)]
        + [pltpu.SemaphoreType.DMA((5,)), pltpu.SemaphoreType.DMA((16,)), pltpu.SemaphoreType.DMA((16,))],
        compiler_params=pltpu.CompilerParams(collective_id=0, has_side_effects=True, vmem_limit_bytes=28 * 2**20),
    )(*[pltpu.with_memory_space_constraint(a, pltpu.HBM) for a in operands])
    out1, out2, out3, out4 = pl.pallas_call(
        write,
        out_shape=[jax.ShapeDtypeStruct(shape, F32) for shape in shapes],
        in_specs=[vmem] * 4,
        out_specs=[hbm] * 4,
        scratch_shapes=[pltpu.SemaphoreType.DMA((10,))],
        compiler_params=pltpu.CompilerParams(vmem_limit_bytes=16 * 2**20),
    )(*got)
    return (
        out1.reshape(7, 8, 64, 128).transpose(0, 1, 3, 2),
        out2.reshape(7, 4, 32, 64).transpose(0, 1, 3, 2),
        out3.reshape(7, 2, 16, 32).transpose(0, 1, 3, 2),
        out4.reshape(2, 16, 32).transpose(0, 2, 1),
    )


def solution(mesh):
    return jax.shard_map(
        shards,
        mesh=mesh,
        in_specs=(P("gx", "gy", "gz"),),
        out_specs=(
            P(None, "gx", "gy", "gz"),
            P(None, "gx", "gy", "gz"),
            P(None, "gx", "gy", "gz"),
            P("gx", "gy", "gz"),
        ),
        check_vma=False,
    )
```

```python
import math

import jax
import jax.numpy as jnp
import ml_dtypes
import numpy as np
from jax import lax
from jax.experimental import pallas as pl
from jax.experimental.pallas import tpu as pltpu
from jax.sharding import PartitionSpec as P

ALPHA = -1.586134342059924
BETA = -0.052980118572961
GAMMA = 0.882911075530934
DELTA = 0.443506852043971
SCALE_LOW = math.sqrt(2.0) / 1.230174104914001
SCALE_HIGH = 1.230174104914001 / math.sqrt(2.0)


def lift_matrix(rows, edges):
    s, d = rows[0::2], rows[1::2]
    none = np.zeros_like(s[:1])
    if edges == "periodic":
        d = d + ALPHA * (s + np.roll(s, -1, 0))
        s = s + BETA * (np.roll(d, 1, 0) + d)
        d = d + GAMMA * (s + np.roll(s, -1, 0))
        s = s + DELTA * (np.roll(d, 1, 0) + d)
        return s, d
    start, end = edges
    up = lambda v, last: np.concatenate([v[1:], last])
    down = lambda v, first: np.concatenate([first, v[:-1]])
    d1 = d + ALPHA * (s + up(s, s[-1:] if end else none))
    before1 = d1[:1] if start else ALPHA * s[:1]
    s1 = s + BETA * (down(d1, before1) + d1)
    d2 = d1 + GAMMA * (s1 + up(s1, s1[-1:] if end else BETA * d1[-1:]))
    before2 = d2[:1] if start else before1 + GAMMA * (BETA * before1 + s1[:1])
    return s1 + DELTA * (down(d2, before2) + d2), d2


def path_matrix(rows, level, edges):
    for _ in range(level):
        rows, high = lift_matrix(rows, edges)
    return np.concatenate([rows, high])


def outgoing(n):
    rows, left, right = np.eye(n), [], []
    for _ in range(3):
        s, d = rows[0::2], rows[1::2]
        left += [s[0], s[0] + BETA * (d[0] + ALPHA * (s[0] + s[1]))]
        right += [d[-1] + ALPHA * s[-1], s[-1] + BETA * (d[-2] + ALPHA * (s[-2] + s[-1]))]
        rows = lift_matrix(rows, (False, False))[0]
    return np.stack(left), np.stack(right)


def line_blocks(n, level):
    m = n >> level
    rows = np.eye(5 * n)
    for _ in range(level):
        rows, high = lift_matrix(rows, "periodic")
    whole = np.concatenate([rows[2 * m : 3 * m], high[2 * m : 3 * m]])
    return [whole[:, k * n : (k + 1) * n] for k in range(5)]


def solved(target, basis):
    u = np.linalg.lstsq(basis.T, target.T, rcond=None)[0].T
    assert np.abs(u @ basis - target).max() < 1e-9
    return np.where(np.abs(u) < 1e-10, 0.0, u)


def block_plan(n, level):
    left, right = outgoing(n)
    left, right = left[: 2 * level], right[: 2 * level]
    blocks = line_blocks(n, level)
    alone = path_matrix(np.eye(n), level, (False, False))
    from_left = solved(blocks[1], right)
    from_right = solved(blocks[3], left)
    own = solved(blocks[2] - alone, np.concatenate([left, right]))
    return dict(left=left, right=right, alone=alone, from_left=from_left, from_right=from_right, own_left=own[:, : 2 * level], own_right=own[:, 2 * level :])


def mirror_plan(n, plans):
    out = []
    for start in (True, False):
        uses, rests = [], []
        for level, plan in enumerate(plans, 1):
            m = n >> level
            rows = np.eye(4 * n)
            for _ in range(level):
                rows, high = lift_matrix(rows, (True, True))
            at = 0 if start else 3
            whole = np.concatenate([rows[at * m : (at + 1) * m], high[at * m : (at + 1) * m]])
            whole = whole[:, at * n : (at + 1) * n]
            rests.append(whole - plan["alone"] - plan["own_left"] @ plan["left"] - plan["own_right"] @ plan["right"])
            u = plan["from_left"] if start else plan["from_right"]
            uses.append(np.pad(u, ((0, 0), (0, 6 - u.shape[1]))))
        use, rest = np.concatenate(uses), np.concatenate(rests)
        g = np.linalg.lstsq(use, rest, rcond=None)[0]
        assert np.abs(use @ g - rest).max() < 1e-9
        out.append(np.where(np.abs(g) < 1e-10, 0.0, g))
    return out


MESH = pl.DeviceIdType.MESH
SIZES = {"gx": 8, "gy": 4, "gz": 4}
NX, NY, NZ = 16, 256, 128
F32 = jnp.float32


def rounded(matrix):
    return [[float(np.float32(c)) if abs(c) > 1e-10 else 0.0 for c in row] for row in matrix]


def fir(weights, rows):
    total = None
    for weight, row in zip(weights, rows):
        if weight == 0.0:
            continue
        term = row() if callable(row) else row
        term = term if weight == 1.0 else weight * term
        total = term if total is None else total + term
    return total


def lift_list(s, d, up, down, first, last):
    before1 = ALPHA * first(s)
    d1 = [b + ALPHA * (a + c) for a, b, c in zip(s, d, up(s, None))]
    s1 = [a + BETA * (b + c) for a, b, c in zip(s, d1, down(d1, before1))]
    d2 = [b + GAMMA * (a + c) for a, b, c in zip(s1, d1, up(s1, BETA * last(d1)))]
    before2 = before1 + GAMMA * (BETA * before1 + first(s1))
    s2 = [a + DELTA * (b + c) for a, b, c in zip(s1, d2, down(d2, before2))]
    return s2, d2


def lift_rows(src, base, n, dst, to, keep_high=True):
    k = n // 16
    s = [src[pl.ds(base + 16 * i, 8, stride=2), :] for i in range(k)]
    d = [src[pl.ds(base + 16 * i + 1, 8, stride=2), :] for i in range(k)]
    sub = lax.broadcasted_iota(jnp.int32, (8, 128), 0)
    top, bottom = sub == 0, sub == 7

    def up(v, fill):
        r = [pltpu.roll(x, 7, 0) for x in v]
        fill = jnp.zeros((8, 128), F32) if fill is None else fill
        return [jnp.where(bottom, r[i + 1] if i + 1 < k else fill, r[i]) for i in range(k)]

    def down(v, fill):
        r = [pltpu.roll(x, 1, 0) for x in v]
        return [jnp.where(top, r[i - 1] if i else fill, r[i]) for i in range(k)]

    low, high = lift_list(s, d, up, down, lambda v: v[0], lambda v: v[-1])
    for i in range(k):
        dst[pl.ds(to + 8 * i, 8), :] = low[i]
        if keep_high:
            dst[pl.ds(to + 8 * (k + i), 8), :] = high[i]


def lift_major(rows):
    low, high = lift_list(
        rows[0::2],
        rows[1::2],
        lambda v, fill: v[1:] + [jnp.zeros_like(v[0]) if fill is None else fill],
        lambda v, fill: [fill] + v[:-1],
        lambda v: v[0],
        lambda v: v[-1],
    )
    return low + high


class Side:
    def __init__(self, plan):
        self.groups = {}
        for source in ("from_left", "from_right", "own_left", "own_right"):
            u = plan[source]
            for g in range(u.shape[0] // 8):
                for f in range(u.shape[1]):
                    column = u[8 * g : 8 * g + 8, f]
                    if np.abs(column).max() > 1e-10:
                        self.groups.setdefault(g, []).append((source, f, column))


PLANS = {n: [block_plan(n, level) for level in (1, 2, 3)] for n in (NY, NZ)}
SIDES = {n: [Side(plan) for plan in PLANS[n]] for n in (NY, NZ)}
MIRRORS = mirror_plan(NZ, PLANS[NZ])
SEND_LEFT = {n: rounded(PLANS[n][2]["left"]) for n in (NY, NZ)}
SEND_RIGHT = {n: rounded(PLANS[n][2]["right"]) for n in (NY, NZ)}
SCALES = [(SCALE_LOW**level, SCALE_LOW ** (level - 1) * SCALE_HIGH) for level in (1, 2, 3)]


def factored(matrix):
    u, size, v = np.linalg.svd(matrix, full_matrices=False)
    rank = int((size > 1e-9).sum())
    return rounded(u[:, :rank] * size[:rank]), rounded(v[:rank])


X_ONE = block_plan(NX, 1)
X_ONE_LEFT, X_ONE_RIGHT = rounded(X_ONE["left"]), rounded(X_ONE["right"])
X_ONE_FROM_LEFT, X_ONE_FROM_RIGHT = rounded(X_ONE["from_left"]), rounded(X_ONE["from_right"])
X_TWO_BLOCKS = line_blocks(NX, 2)
X_TWO_FROM_LEFT, X_TWO_RIGHT = factored(X_TWO_BLOCKS[1])
X_TWO_FROM_RIGHT, X_TWO_LEFT = factored(X_TWO_BLOCKS[3])
X_TWO_OWN = rounded(X_TWO_BLOCKS[2])
X_THREE = [rounded(block) for block in line_blocks(NX, 3)]
N_TWO = len(X_TWO_RIGHT)

Y_ROWS = 6 * NX
Z_TWO, Z_THREE, Z_ROWS = 4 * NX, 8 * NX, 8 * NX + 6 * (NX // 2)
X23_ROWS = N_TWO * 64 + 64


def neighbour(axis, step):
    size = SIZES[axis]
    place = {name: lax.axis_index(name) for name in SIZES}
    place[axis] = lax.rem(place[axis] + (step + size), size)
    return tuple(place[name] for name in ("gx", "gy", "gz"))


def build_table(table, sides):
    sub = lax.broadcasted_iota(jnp.int32, (8, 128), 0)
    found = []
    at = 0
    for side in sides:
        places = {}
        for g, terms in side.groups.items():
            for source, f, column in terms:
                value = jnp.zeros((8, 128), F32)
                for i in range(8):
                    if abs(column[i]) > 1e-10:
                        value = jnp.where(sub == i, float(np.float32(column[i])), value)
                table[pl.ds(at, 8), :] = value
                places[g, source, f] = at
                at += 8
        found.append(places)
    return found


def table_rows(sides):
    return 8 * sum(len(terms) for side in sides for terms in side.groups.values())


def correct(ref, base, side, places, table, refs, row):
    for g, terms in side.groups.items():
        terms = [(source, f) for source, f, _ in terms if source in refs]
        if not terms:
            continue
        value = ref[pl.ds(base + 8 * g, 8), :]
        for source, f in terms:
            value = value + table[pl.ds(places[g, source, f], 8), :] * refs[source][pl.ds(row(f), 1), :]
        ref[pl.ds(base + 8 * g, 8), :] = value


def parts_of(value):
    rest, parts = np.asarray(value, np.float32), []
    for _ in range(2):
        part = rest.astype(ml_dtypes.bfloat16)
        parts.append(part)
        rest = rest - part.astype(np.float32)
    return parts


def spread(level):
    plan = PLANS[NY][level - 1]
    left, right = plan["from_left"].T, plan["from_right"].T
    if level == 3:
        blocks = []
        for u in (left, right):
            block = np.zeros((8, NX, 128))
            block[:6, 0::2, :64] = u[:, None, :]
            block[:6, 1::2, 64:] = u[:, None, :]
            blocks.append(block.reshape(128, 128))
        matrix = np.concatenate(blocks)
    else:
        matrix = np.repeat(np.concatenate([left, right]), NX, axis=0)
    one, two = parts_of(matrix)
    return np.concatenate([one, two, one, two])


SPREADS = [spread(level) for level in (1, 2, 3)]
Z_SENDS = np.zeros((40, NZ), np.float32)
for _at, _rows in enumerate((PLANS[NZ][2]["left"], PLANS[NZ][2]["right"], *MIRRORS)):
    Z_SENDS[8 * _at : 8 * _at + 6] = _rows
for _at, _rows in enumerate((X_ONE["left"], X_ONE["right"])):
    for _xf in range(2):
        for _f in range(2):
            Z_SENDS[32 + 4 * _at + 2 * _xf + _f, _f * NX : (_f + 1) * NX] = _rows[_xf]

def split(value):
    one = value.astype(jnp.bfloat16).astype(F32)
    return one, value - one


def lanes_of(shape):
    return lax.broadcasted_iota(jnp.int32, shape, 1)


def slots(level, left, right):
    lane = lanes_of(left.shape)
    turn = lambda value, by: pltpu.roll(value, by, 1)
    if level == 1:
        base = left if right is None else jnp.where(lane < 32, left, jnp.where(lane < 64, turn(right, 32), 0.0))
        one, two = split(base)
        return [one + turn(one, 64), two + turn(two, 64)]
    if level == 2:
        one, two = split(jnp.where(lane < 64, left, turn(right, 64)))
        return [one, one, two, two]
    one, two = zip(split(left), split(right))
    return [*one, *one, *two, *two]


def expand(level, arrays, keep, spread_ref):
    factor = jnp.concatenate([jnp.where(keep, a, 0.0).astype(jnp.bfloat16) for a in arrays], axis=1)
    return jnp.dot(factor, spread_ref[...], preferred_element_type=F32)


def kernel(
    vel, spread1_hbm, spread2_hbm, spread3_hbm, sends_hbm,
    o1, o2, o3, o4,
    w1, w2, w3, x1rl, x1rr, x23rl, x23rr, x3rl, x3rr, eg,
    v, y1, y2, y3, z1, z2, z3, t2, t3, t4, ytab, ztab,
    ysl, ysr, yrl, yrr, zsl, zsr, zrl, zrr, zml, zmr,
    htl, htr, g1, g2, g3, u2, u3, p1, p2, p3, csl, csr, zlsl, zlsr, zlml, zlmr,
    x1sl, x1sr, x23sl, x23sr, x3sl, x3sr, xesl, xesr, xerl, xerr,
    spread1, spread2, spread3, sends, zc, zf, q2, q3,
    load_sems, send_sems, recv_sems,
):
    loads = [
        pltpu.make_async_copy(src, dst, load_sems.at[i])
        for i, (src, dst) in enumerate(
            ((vel, v), (sends_hbm, sends), (spread1_hbm, spread1), (spread2_hbm, spread2), (spread3_hbm, spread3))
        )
    ]
    for load in loads:
        load.start()
    near = {
        "yl": neighbour("gy", -1), "yr": neighbour("gy", 1), "zl": neighbour("gz", -1), "zr": neighbour("gz", 1),
        "xl": neighbour("gx", -1), "xr": neighbour("gx", 1), "xll": neighbour("gx", -2), "xrr": neighbour("gx", 2),
    }
    barrier = pltpu.get_barrier_semaphore()
    for device in near.values():
        pl.semaphore_signal(barrier, inc=1, device_id=device, device_id_type=MESH)
    y_places = build_table(ytab, SIDES[NY])
    z_places = build_table(ztab, SIDES[NZ])
    for ref in (yrl, yrr, ysl, ysr):
        ref[pl.ds(Y_ROWS, 32), :] = jnp.zeros((32, 128), F32)
    eg[...] = jnp.zeros((128, 128), F32)

    def remote(index, src, dst, to):
        return pltpu.make_async_remote_copy(
            src_ref=src,
            dst_ref=dst,
            send_sem=send_sems.at[index],
            recv_sem=recv_sems.at[index],
            device_id=near[to],
            device_id_type=MESH,
        )

    loads[0].wait()

    for h in range(2):
        head = [v[pl.ds(h * 8 * NY + k, 8, stride=NY), :] for k in range(21)]
        tail = [v[pl.ds(h * 8 * NY + k, 8, stride=NY), :] for k in range(NY - 28, NY)]
        for f in range(6):
            ysl[pl.ds(f * NX + 8 * h, 8), :] = fir(SEND_LEFT[NY][f][:21], head)
            ysr[pl.ds(f * NX + 8 * h, 8), :] = fir(SEND_RIGHT[NY][f][-28:], tail)

    loads[1].wait()
    for at, ref in enumerate((ysl, ysr)):
        sums = jnp.dot(
            sends[pl.ds(0, 16), :], ref[...].T, precision=lax.Precision.HIGHEST, preferred_element_type=F32
        )
        csl[pl.ds(8 * at, 8), :] = sums[:8]
        csr[pl.ds(8 * at, 8), :] = sums[8:]
    corners = []
    for at in range(2):
        corners.append(remote(4 + at, csl.at[pl.ds(8 * at, 8)], zc.at[pl.ds(16 * at, 8)], "zl"))
        corners.append(remote(16 + at, csr.at[pl.ds(8 * at, 8)], zc.at[pl.ds(16 * at + 8, 8)], "zr"))
    pl.semaphore_wait(barrier, len(near))
    for copy in corners:
        copy.start()
    y_left = remote(0, ysl.at[pl.ds(0, Y_ROWS)], yrr.at[pl.ds(0, Y_ROWS)], "yl")
    y_right = remote(1, ysr.at[pl.ds(0, Y_ROWS)], yrl.at[pl.ds(0, Y_ROWS)], "yr")
    y_left.start()
    y_right.start()

    def lift_y(x, c):
        lift_rows(v, x * NY, NY, y1, x * NY)
        lift_rows(y1, x * NY, NY // 2, y2, x * (NY // 2))
        lift_rows(y2, x * (NY // 2), NY // 4, y3, x * (NY // 4))
        own = {"own_left": ysl, "own_right": ysr}
        for level, ref in ((1, y2), (2, y3)):
            correct(ref, x * (NY >> level), SIDES[NY][level], y_places[level], ytab, own, lambda f: f * NX + x)
        return c

    lax.fori_loop(0, NX, lift_y, 0, unroll=2)
    def turn_one(x, c):
        for t in range(2):
            z1[pl.ds(x * 256 + 128 * t, 128), :] = y1[pl.ds(x * NY + 128 * t, 128), :].T
        return c

    def turn_two(x, c):
        z2[pl.ds(x * 128, 128), :] = y2[pl.ds(x * 128, 128), :].T
        return c

    def turn_three(p, c):
        z3[pl.ds(p * 128, 128), :] = y3[pl.ds(p * 128, 128), :].T
        return c

    def z_sums(level, load_row, store):
        rows = {}

        def row(k):
            if k not in rows:
                rows[k] = load_row(k)
            return rows[k]

        for f in range(2 * level):
            for at, ref in enumerate((zsl, zsr, zml, zmr)):
                weights = [float(c) for c in Z_SENDS[8 * at + f]]
                ks = [k for k in range(NZ) if weights[k] != 0.0]
                store(ref, f, fir([weights[k] for k in ks], [row(k) for k in ks]))

    lax.fori_loop(0, NX // 2, turn_three, 0, unroll=8)
    lax.fori_loop(0, NX, turn_two, 0, unroll=8)

    def store_three(ref, f, value):
        ref[pl.ds(Z_THREE + f * (NX // 2), 8), :] = value

    z_sums(3, lambda k: z3[pl.ds(k, 8, stride=128), :], store_three)
    for h in range(2):

        def store_two(ref, f, value, h=h):
            ref[pl.ds(Z_TWO + f * NX + 8 * h, 8), :] = value

        z_sums(2, lambda k, h=h: z2[pl.ds(h * 8 * 128 + k, 8, stride=128), :], store_two)
    deep = pl.ds(Z_TWO, Z_ROWS - Z_TWO)
    z_left = remote(2, zsl.at[deep], zrr.at[deep], "zl")
    z_right = remote(3, zsr.at[deep], zrl.at[deep], "zr")
    z_left.start()
    z_right.start()

    def lift_z1(i, c):
        lift_rows(z1, i * NZ, NZ, w1, i * NZ)
        return c

    lax.fori_loop(0, NX, turn_one, 0, unroll=4)
    for copy in corners:
        copy.wait()
    zf_left = remote(18, zc.at[pl.ds(0, 16)], zf.at[pl.ds(0, 16)], "yl")
    zf_right = remote(19, zc.at[pl.ds(16, 16)], zf.at[pl.ds(16, 16)], "yr")
    zf_left.start()
    zf_right.start()
    lax.fori_loop(0, 2 * NX, lift_z1, 0, unroll=4)

    def sums_one(g, c):
        rows = [w1[pl.ds(x * 256 + 8 * g, 8), :] for x in (0, 1, 2, 12, 13, 14, 15)]
        for f in range(2):
            x1sl[pl.ds(f * 256 + 8 * g, 8), :] = fir(X_ONE_LEFT[f][:3], rows[:3])
            x1sr[pl.ds(f * 256 + 8 * g, 8), :] = fir(X_ONE_RIGHT[f][12:], rows[3:])
        return c

    lax.fori_loop(0, 32, sums_one, 0, unroll=4)
    x1_left = remote(6, x1sl, x1rr, "xl")
    x1_right = remote(7, x1sr, x1rl, "xr")
    x1_left.start()
    x1_right.start()
    for h in range(2):
        for t in range(2):

            def store_one(ref, f, value, h=h, t=t):
                ref[pl.ds((f * 2 + t) * NX + 8 * h, 8), :] = value

            z_sums(1, lambda k, h=h, t=t: z1[pl.ds(h * 8 * 256 + t * 128 + k, 8, stride=256), :], store_one)
    first = pl.ds(0, Z_TWO)
    z1_left = remote(14, zsl.at[first], zrr.at[first], "zl")
    z1_right = remote(15, zsr.at[first], zrl.at[first], "zr")
    z1_left.start()
    z1_right.start()

    row_one = lambda x, t: lambda f: (f * 2 + t) * NX + x
    row_two = lambda x: lambda f: Z_TWO + f * NX + x
    row_three = lambda p: lambda f: Z_THREE + f * (NX // 2) + p
    z_own = {"own_left": zsl, "own_right": zsr}

    def lift_z2(x, c):
        lift_rows(z2, x * NZ, NZ, t2, x * 64, keep_high=False)
        lift_rows(t2, x * 64, 64, w2, x * 64)
        correct(w2, x * 64, SIDES[NZ][1], z_places[1], ztab, z_own, row_two(x))
        return c

    def lift_z3(p, c):
        lift_rows(z3, p * NZ, NZ, t3, p * 64, keep_high=False)
        lift_rows(t3, p * 64, 64, t4, p * 32, keep_high=False)
        lift_rows(t4, p * 32, 32, w3, p * 32)
        correct(w3, p * 32, SIDES[NZ][2], z_places[2], ztab, z_own, row_three(p))
        return c

    lax.fori_loop(0, NX // 2, lift_z3, 0, unroll=4)
    lax.fori_loop(0, NX, lift_z2, 0, unroll=4)

    y_left.wait()
    y_right.wait()
    for load in loads[2:]:
        load.wait()
    htl[...] = yrl[...].T
    htr[...] = yrr[...].T
    for at, ref in ((0, htl), (8, htr)):
        sums = jnp.dot(sends[pl.ds(0, 32), :], ref[...], precision=lax.Precision.HIGHEST, preferred_element_type=F32)
        for i, out in enumerate((zlsl, zlsr, zlml, zlmr)):
            out[pl.ds(at, 8), :] = sums[8 * i : 8 * i + 8]
    for i, ref in enumerate((htl, htr)):
        lift_rows(ref, 0, 128, g1, 128 * i)
        lift_rows(g1, 128 * i, 64, u2, 64 * i)
        lift_rows(u2, 64 * i, 32, u3, 32 * i)
    for i in range(2):
        own = {"own_left": zlsl, "own_right": zlsr}
        g2[pl.ds(64 * i, 64), :] = u2[pl.ds(64 * i, 64), :]
        g3[pl.ds(32 * i, 32), :] = u3[pl.ds(32 * i, 32), :]
        correct(g2, 64 * i, SIDES[NZ][1], z_places[1], ztab, own, lambda f, i=i: 8 * i + f)
        correct(g3, 32 * i, SIDES[NZ][2], z_places[2], ztab, own, lambda f, i=i: 8 * i + f)
    for level, g, p, n in ((1, g1, p1, 128), (2, g2, p2, 64), (3, g3, p3, 32)):
        for i, value in enumerate(slots(level, g[pl.ds(0, n), :], g[pl.ds(n, n), :])):
            p[pl.ds(n * i, n), :] = value

    sums = lax.dot_general(
        sends[pl.ds(32, 8), :],
        g1[...],
        (((1,), (1,)), ((), ())),
        precision=lax.Precision.HIGHEST,
        preferred_element_type=F32,
    )
    for way, ref in enumerate((xesl, xesr)):
        for xf in range(2):
            for side in range(2):
                at = 4 * way + 2 * xf
                ref[pl.ds(16 + 4 * xf + 2 * side, 2), :] = sums[at : at + 2, 128 * side : 128 * side + 128]
    xg_left = remote(20, xesl.at[pl.ds(16, 8)], xerr.at[pl.ds(16, 8)], "xl")
    xg_right = remote(21, xesr.at[pl.ds(16, 8)], xerl.at[pl.ds(16, 8)], "xr")
    xg_left.start()
    xg_right.start()

    def spread_one(x, c):
        keep = (lanes_of((128, 128)) & 15) == x
        value = expand(1, [p1[pl.ds(128 * i, 128), :] for i in range(2)], keep, spread1)
        for t in range(2):
            at = pl.ds(x * 256 + 128 * t, 128)
            w1[at, :] = w1[at, :] + value[:, 128 * t : 128 * t + 128]
        return c

    def spread_two(x, c):
        keep = (lanes_of((64, 128)) & 15) == x
        at = pl.ds(x * 64, 64)
        w2[at, :] = w2[at, :] + expand(2, [p2[pl.ds(64 * i, 64), :] for i in range(4)], keep, spread2)
        return c

    def spread_three(p, c):
        keep = ((lanes_of((32, 128)) & 15) >> 1) == p
        at = pl.ds(p * 32, 32)
        w3[at, :] = w3[at, :] + expand(3, [p3[pl.ds(32 * i, 32), :] for i in range(8)], keep, spread3)
        return c

    lax.fori_loop(0, NX // 2, spread_three, 0, unroll=8)
    lax.fori_loop(0, NX, spread_two, 0, unroll=8)

    for copy in (z_left, z_right, zf_left, zf_right):
        copy.wait()
    gz = lax.axis_index("gz")

    @pl.when(gz == 0)
    def _():
        zrl[deep, :] = zml[deep, :]
        zf[pl.ds(24, 8), :] = zlml[pl.ds(0, 8), :]
        zf[pl.ds(8, 8), :] = zlml[pl.ds(8, 8), :]

    @pl.when(gz == SIZES["gz"] - 1)
    def _():
        zrr[deep, :] = zmr[deep, :]
        zf[pl.ds(16, 8), :] = zlmr[pl.ds(0, 8), :]
        zf[pl.ds(0, 8), :] = zlmr[pl.ds(8, 8), :]

    def complete(level):
        lane, sub = lanes_of((16, 128)), lax.broadcasted_iota(jnp.int32, (16, 128), 0)
        count = NX // 2 if level == 3 else NX
        keep = ((lane[:8] & 15) >> 1) == sub[:8] if level == 3 else (lane & 15) == sub
        tall = []
        for at in (8, 0):
            arrays = slots(level, zf[pl.ds(16 + at, 8), :], zf[pl.ds(at, 8), :])
            tall.append([
                jnp.concatenate([jnp.where(keep, a[f : f + 1], 0.0) for f in range(2 * level)], axis=0) for a in arrays
            ])
        both = [jnp.concatenate(pair, axis=0) for pair in zip(*tall)]
        value = expand(level, both, jnp.full(both[0].shape, True), (spread1, spread2, spread3)[level - 1])
        for side, ref in enumerate((zrl, zrr)):
            for f in range(2 * level):
                first_row = (side * 2 * level + f) * count
                piece = value[first_row : first_row + count]
                if level == 1:
                    for t in range(2):
                        at = pl.ds((f * 2 + t) * NX, NX)
                        ref[at, :] = ref[at, :] + piece[:, 128 * t : 128 * t + 128]
                else:
                    at = pl.ds((Z_TWO if level == 2 else Z_THREE) + f * count, count)
                    ref[at, :] = ref[at, :] + piece

    complete(3)
    complete(2)

    for copy in (z1_left, z1_right):
        copy.wait()

    @pl.when(gz == 0)
    def _():
        zrl[first, :] = zml[first, :]

    @pl.when(gz == SIZES["gz"] - 1)
    def _():
        zrr[first, :] = zmr[first, :]

    complete(1)

    for side, ref in enumerate((zrl, zrr)):
        for f in range(2):
            for t in range(2):
                rows = [ref[pl.ds((f * 2 + t) * NX + x, 1), :] for x in (0, 1, 2, 12, 13, 14, 15)]
                for xf in range(2):
                    at = pl.ds((xf * 2 + t) * 4 + side * 2 + f, 1)
                    xesl[at, :] = fir(X_ONE_LEFT[xf][:3], rows[:3])
                    xesr[at, :] = fir(X_ONE_RIGHT[xf][12:], rows[3:])
    xe_left = remote(8, xesl.at[pl.ds(0, 16)], xerr.at[pl.ds(0, 16)], "xl")
    xe_right = remote(9, xesr.at[pl.ds(0, 16)], xerl.at[pl.ds(0, 16)], "xr")
    xe_left.start()
    xe_right.start()

    z_past = {"from_left": zrl, "from_right": zrr}

    def finish_z2(x, c):
        correct(w2, x * 64, SIDES[NZ][1], z_places[1], ztab, z_past, row_two(x))
        return c

    def finish_z3(p, c):
        correct(w3, p * 32, SIDES[NZ][2], z_places[2], ztab, z_past, row_three(p))
        return c

    lax.fori_loop(0, NX // 2, finish_z3, 0, unroll=4)
    lax.fori_loop(0, NX, finish_z2, 0, unroll=4)

    three_to = ((x23sr, N_TWO * 64), (x23sl, N_TWO * 64), (x3sr, 0), (x3sl, 0))

    def sums_two(g, c):
        rows = [w2[pl.ds(x * 64 + 8 * g, 8), :] for x in range(NX)]
        for f in range(N_TWO):
            x23sl[pl.ds(f * 64 + 8 * g, 8), :] = fir(X_TWO_LEFT[f], rows)
            x23sr[pl.ds(f * 64 + 8 * g, 8), :] = fir(X_TWO_RIGHT[f], rows)
        return c

    def send_three(g, c):
        rows = [w3[pl.ds(p * 32 + 8 * g, 8), :] for p in range(NX // 2)]
        for (ref, at), block in zip(three_to, (1, 3, 0, 4)):
            for h, value in enumerate(sums_three(X_THREE[block], rows)):
                ref[pl.ds(at + 32 * h + 8 * g, 8), :] = value
        return c

    lax.fori_loop(0, 8, sums_two, 0, unroll=2)
    lax.fori_loop(0, 4, send_three, 0, unroll=2)
    x23_left = remote(10, x23sl, x23rr, "xl")
    x23_right = remote(11, x23sr, x23rl, "xr")
    x3_left = remote(12, x3sl, x3rr, "xll")
    x3_right = remote(13, x3sr, x3rl, "xrr")
    for copy in (x23_left, x23_right, x3_left, x3_right):
        copy.start()

    def finish_z1(x, c):
        for t in range(2):
            correct(w1, x * 256 + 128 * t, SIDES[NZ][0], z_places[0], ztab, z_past, row_one(x, t))
        return c

    lax.fori_loop(0, NX, spread_one, 0, unroll=4)
    lax.fori_loop(0, NX, finish_z1, 0)
    def own_two(g, c):
        rows = [w2[pl.ds(x * 64 + 8 * g, 8), :] for x in range(NX)]
        for i in range(8):
            q2[pl.ds(i * 64 + 8 * g, 8), :] = fir(X_TWO_OWN[i], rows)
        return c

    def own_three(g, c):
        rows = [w3[pl.ds(p * 32 + 8 * g, 8), :] for p in range(NX // 2)]
        for h, value in enumerate(sums_three(X_THREE[2], rows)):
            q3[pl.ds(32 * h + 8 * g, 8), :] = value
        return c

    lax.fori_loop(0, 8, own_two, 0, unroll=2)
    lax.fori_loop(0, 4, own_three, 0, unroll=2)
    for copy in (x1_left, x1_right, xg_left, xg_right, xe_left, xe_right):
        copy.wait()
    for side, ends in enumerate((xerl, xerr)):
        for xf in range(2):
            for h in range(4):
                eg[pl.ds(NX * h + 2 * side + xf, 1), :] = ends[pl.ds(16 + 4 * xf + h, 1), :]
    arrays = slots(1, eg[...].T, None)
    for side, ref in enumerate((x1rl, x1rr)):
        for xf in range(2):
            value = expand(1, arrays, (lanes_of((128, 128)) & 15) == 2 * side + xf, spread1)
            for t in range(2):
                at = pl.ds(xf * 256 + 128 * t, 128)
                ref[at, :] = ref[at, :] + value[:, 128 * t : 128 * t + 128]
    for xf in range(2):
        for t in range(2):
            for ref, ends in ((x1rl, xerl), (x1rr, xerr)):
                at = (xf * 2 + t) * 4
                refs = {"from_left": ends.at[pl.ds(at, 2)], "from_right": ends.at[pl.ds(at + 2, 2)]}
                correct(ref, xf * 256 + 128 * t, SIDES[NZ][0], z_places[0], ztab, refs, lambda f: f)
    for hy in range(2):
        for hz in range(2):

            def out_one(g, c, hy=hy, hz=hz):
                row = 128 * hy + 64 * hz + 8 * g
                rows = [w1[pl.ds(x * 256 + row, 8), :] for x in range(NX)]
                left = [x1rl[pl.ds(f * 256 + row, 8), :] for f in range(2)]
                right = [x1rr[pl.ds(f * 256 + row, 8), :] for f in range(2)]
                for i, value in enumerate(lift_major(rows)):
                    hx = i // 8
                    band = 4 * hx + 2 * hy + hz
                    if not band:
                        continue
                    value = fir([1.0] + X_ONE_FROM_LEFT[i] + X_ONE_FROM_RIGHT[i], [value] + left + right)
                    value = value * (SCALES[0][hx] * SCALES[0][hy] * SCALES[0][hz])
                    o1[pl.ds((band - 1) * 512 + (i % 8) * 64 + 8 * g, 8), :] = value
                return c

            lax.fori_loop(0, 8, out_one, 0, unroll=2)
    for copy in (x23_left, x23_right, x3_left, x3_right):
        copy.wait()
    lane = lanes_of((8, 128))
    low_lanes = lane < 64

    def out_two(g, hz):
        left = [x23rl[pl.ds(f * 64 + 8 * g, 8), :] for f in range(N_TWO)]
        right = [x23rr[pl.ds(f * 64 + 8 * g, 8), :] for f in range(N_TWO)]
        for i in range(8):
            hx = i // 4
            own = q2[pl.ds(i * 64 + 8 * g, 8), :]
            value = fir([1.0] + X_TWO_FROM_LEFT[i] + X_TWO_FROM_RIGHT[i], [own] + left + right)
            scale = SCALES[1][hx] * SCALES[1][hz]
            value = value * jnp.where(low_lanes, scale * SCALES[1][0], scale * SCALES[1][1])
            for hy in range(2):
                band = 4 * hx + 2 * hy + hz
                if band:
                    at = (band - 1) * 128 + (i % 4) * 32 + 8 * (g % 4)
                    o2[pl.ds(at, 8), :] = value[:, 64 * hy : 64 * hy + 64]

    for g in range(8):
        out_two(g, g // 4)

    def out_three(g, hz):
        high_y = (lane & 63) >= 32
        for hx in range(2):
            value = q3[pl.ds(32 * hx + 8 * g, 8), :]
            for ref, at in ((x23rl, N_TWO * 64), (x23rr, N_TWO * 64), (x3rl, 0), (x3rr, 0)):
                value = value + ref[pl.ds(at + 32 * hx + 8 * g, 8), :]
            scale = SCALES[2][hx] * SCALES[2][hz]
            value = value * jnp.where(high_y, scale * SCALES[2][1], scale * SCALES[2][0])
            for q in range(4):
                i, hy = divmod(q, 2)
                band = 4 * hx + 2 * hy + hz
                row = 16 * i + 8 * (g % 2)
                piece = value[:, 32 * q : 32 * q + 32]
                if band:
                    o3[pl.ds((band - 1) * 32 + row, 8), :] = piece
                else:
                    o4[pl.ds(row, 8), :] = piece

    for g in range(4):
        out_three(g, g // 2)


def paired(weights, rows):
    low_lanes = lanes_of((8, 128)) < 64
    total = jnp.zeros((8, 128), F32)
    for p in range(NX // 2):
        if weights[2 * p] == 0.0 and weights[2 * p + 1] == 0.0:
            continue
        total = total + jnp.where(low_lanes, weights[2 * p], weights[2 * p + 1]) * rows[p]
    return total + pltpu.roll(total, 64, 1)


def sums_three(matrix, rows):
    low_lanes = lanes_of((8, 128)) < 64
    return [jnp.where(low_lanes, paired(matrix[2 * h], rows), paired(matrix[2 * h + 1], rows)) for h in range(2)]


def write(o1, o2, o3, o4, out1, out2, out3, out4, sems):
    copies = []
    for src, dst, parts in ((o1, out1, 7), (o2, out2, 1), (o3, out3, 1), (o4, out4, 1)):
        rows = src.shape[0] // parts
        for i in range(parts):
            at = pl.ds(i * rows, rows)
            copies.append(pltpu.make_async_copy(src.at[at], dst.at[at], sems.at[len(copies)]))
            copies[-1].start()
    for copy in copies:
        copy.wait()


def shards(velocity):
    vmem, hbm = pl.BlockSpec(memory_space=pltpu.VMEM), pl.BlockSpec(memory_space=pltpu.HBM)
    wide = lambda rows: pltpu.VMEM((rows, 128), F32)
    shapes = [(7 * 8 * 64, 128), (7 * 4 * 32, 64), (7 * 2 * 16, 32), (2 * 16, 32)]
    scratch = [32 * NZ, 16 * 64, 8 * 32, 512, 512, X23_ROWS, X23_ROWS, 64, 64, 128]
    scratch += [16 * NY, 16 * NY, 16 * NY // 2, 16 * NY // 4]
    scratch += [32 * NZ, 16 * NZ, 8 * NZ]
    scratch += [16 * 64, 8 * 64, 8 * 32]
    scratch += [table_rows(SIDES[NY]), table_rows(SIDES[NZ])]
    scratch += [128] * 4 + [Z_ROWS] * 6
    scratch += [128, 128, 256, 128, 64, 128, 64, 2 * 128, 4 * 64, 8 * 32] + [16] * 6
    scratch += [512] * 2 + [X23_ROWS] * 2 + [64] * 2 + [24] * 4
    operands = [velocity.reshape(NX * NY, NZ), *[jnp.asarray(matrix) for matrix in SPREADS], jnp.asarray(Z_SENDS)]
    got = pl.pallas_call(
        kernel,
        out_shape=[jax.ShapeDtypeStruct(shape, F32) for shape in shapes],
        in_specs=[hbm] * 5,
        out_specs=[vmem] * 4,
        scratch_shapes=[wide(rows) for rows in scratch]
        + [pltpu.VMEM(matrix.shape, jnp.bfloat16) for matrix in SPREADS]
        + [wide(rows) for rows in (40, 32, 32, 512, 64)]
        + [pltpu.SemaphoreType.DMA((5,)), pltpu.SemaphoreType.DMA((22,)), pltpu.SemaphoreType.DMA((22,))],
        compiler_params=pltpu.CompilerParams(collective_id=0, has_side_effects=True, vmem_limit_bytes=28 * 2**20),
    )(*[pltpu.with_memory_space_constraint(a, pltpu.HBM) for a in operands])
    out1, out2, out3, out4 = pl.pallas_call(
        write,
        out_shape=[jax.ShapeDtypeStruct(shape, F32) for shape in shapes],
        in_specs=[vmem] * 4,
        out_specs=[hbm] * 4,
        scratch_shapes=[pltpu.SemaphoreType.DMA((10,))],
        compiler_params=pltpu.CompilerParams(vmem_limit_bytes=16 * 2**20),
    )(*got)
    return (
        out1.reshape(7, 8, 64, 128).transpose(0, 1, 3, 2),
        out2.reshape(7, 4, 32, 64).transpose(0, 1, 3, 2),
        out3.reshape(7, 2, 16, 32).transpose(0, 1, 3, 2),
        out4.reshape(2, 16, 32).transpose(0, 2, 1),
    )


def solution(mesh):
    return jax.shard_map(
        shards,
        mesh=mesh,
        in_specs=(P("gx", "gy", "gz"),),
        out_specs=(
            P(None, "gx", "gy", "gz"),
            P(None, "gx", "gy", "gz"),
            P(None, "gx", "gy", "gz"),
            P("gx", "gy", "gz"),
        ),
        check_vma=False,
    )
```

```python
import math

import jax
import jax.numpy as jnp
import ml_dtypes
import numpy as np
from jax import lax
from jax.experimental import pallas as pl
from jax.experimental.pallas import tpu as pltpu
from jax.sharding import PartitionSpec as P

ALPHA = -1.586134342059924
BETA = -0.052980118572961
GAMMA = 0.882911075530934
DELTA = 0.443506852043971
SCALE_LOW = math.sqrt(2.0) / 1.230174104914001
SCALE_HIGH = 1.230174104914001 / math.sqrt(2.0)


def lift_matrix(rows, edges):
    s, d = rows[0::2], rows[1::2]
    none = np.zeros_like(s[:1])
    if edges == "periodic":
        d = d + ALPHA * (s + np.roll(s, -1, 0))
        s = s + BETA * (np.roll(d, 1, 0) + d)
        d = d + GAMMA * (s + np.roll(s, -1, 0))
        s = s + DELTA * (np.roll(d, 1, 0) + d)
        return s, d
    start, end = edges
    up = lambda v, last: np.concatenate([v[1:], last])
    down = lambda v, first: np.concatenate([first, v[:-1]])
    d1 = d + ALPHA * (s + up(s, s[-1:] if end else none))
    before1 = d1[:1] if start else ALPHA * s[:1]
    s1 = s + BETA * (down(d1, before1) + d1)
    d2 = d1 + GAMMA * (s1 + up(s1, s1[-1:] if end else BETA * d1[-1:]))
    before2 = d2[:1] if start else before1 + GAMMA * (BETA * before1 + s1[:1])
    return s1 + DELTA * (down(d2, before2) + d2), d2


def path_matrix(rows, level, edges):
    for _ in range(level):
        rows, high = lift_matrix(rows, edges)
    return np.concatenate([rows, high])


def outgoing(n):
    rows, left, right = np.eye(n), [], []
    for _ in range(3):
        s, d = rows[0::2], rows[1::2]
        left += [s[0], s[0] + BETA * (d[0] + ALPHA * (s[0] + s[1]))]
        right += [d[-1] + ALPHA * s[-1], s[-1] + BETA * (d[-2] + ALPHA * (s[-2] + s[-1]))]
        rows = lift_matrix(rows, (False, False))[0]
    return np.stack(left), np.stack(right)


def line_blocks(n, level):
    m = n >> level
    rows = np.eye(5 * n)
    for _ in range(level):
        rows, high = lift_matrix(rows, "periodic")
    whole = np.concatenate([rows[2 * m : 3 * m], high[2 * m : 3 * m]])
    return [whole[:, k * n : (k + 1) * n] for k in range(5)]


def solved(target, basis):
    u = np.linalg.lstsq(basis.T, target.T, rcond=None)[0].T
    assert np.abs(u @ basis - target).max() < 1e-9
    return np.where(np.abs(u) < 1e-10, 0.0, u)


def block_plan(n, level):
    left, right = outgoing(n)
    left, right = left[: 2 * level], right[: 2 * level]
    blocks = line_blocks(n, level)
    alone = path_matrix(np.eye(n), level, (False, False))
    from_left = solved(blocks[1], right)
    from_right = solved(blocks[3], left)
    own = solved(blocks[2] - alone, np.concatenate([left, right]))
    return dict(left=left, right=right, alone=alone, from_left=from_left, from_right=from_right, own_left=own[:, : 2 * level], own_right=own[:, 2 * level :])


def mirror_plan(n, plans):
    out = []
    for start in (True, False):
        uses, rests = [], []
        for level, plan in enumerate(plans, 1):
            m = n >> level
            rows = np.eye(4 * n)
            for _ in range(level):
                rows, high = lift_matrix(rows, (True, True))
            at = 0 if start else 3
            whole = np.concatenate([rows[at * m : (at + 1) * m], high[at * m : (at + 1) * m]])
            whole = whole[:, at * n : (at + 1) * n]
            rests.append(whole - plan["alone"] - plan["own_left"] @ plan["left"] - plan["own_right"] @ plan["right"])
            u = plan["from_left"] if start else plan["from_right"]
            uses.append(np.pad(u, ((0, 0), (0, 6 - u.shape[1]))))
        use, rest = np.concatenate(uses), np.concatenate(rests)
        g = np.linalg.lstsq(use, rest, rcond=None)[0]
        assert np.abs(use @ g - rest).max() < 1e-9
        out.append(np.where(np.abs(g) < 1e-10, 0.0, g))
    return out


MESH = pl.DeviceIdType.MESH
SIZES = {"gx": 8, "gy": 4, "gz": 4}
NX, NY, NZ = 16, 256, 128
F32 = jnp.float32


def rounded(matrix):
    return [[float(np.float32(c)) if abs(c) > 1e-10 else 0.0 for c in row] for row in matrix]


def fir(weights, rows):
    total = None
    for weight, row in zip(weights, rows):
        if weight == 0.0:
            continue
        term = row() if callable(row) else row
        term = term if weight == 1.0 else weight * term
        total = term if total is None else total + term
    return total


def lift_list(s, d, up, down, first, last):
    before1 = ALPHA * first(s)
    d1 = [b + ALPHA * (a + c) for a, b, c in zip(s, d, up(s, None))]
    s1 = [a + BETA * (b + c) for a, b, c in zip(s, d1, down(d1, before1))]
    d2 = [b + GAMMA * (a + c) for a, b, c in zip(s1, d1, up(s1, BETA * last(d1)))]
    before2 = before1 + GAMMA * (BETA * before1 + first(s1))
    s2 = [a + DELTA * (b + c) for a, b, c in zip(s1, d2, down(d2, before2))]
    return s2, d2


def lift_rows(src, base, n, dst, to, keep_high=True):
    k = n // 16
    s = [src[pl.ds(base + 16 * i, 8, stride=2), :] for i in range(k)]
    d = [src[pl.ds(base + 16 * i + 1, 8, stride=2), :] for i in range(k)]
    sub = lax.broadcasted_iota(jnp.int32, (8, 128), 0)
    top, bottom = sub == 0, sub == 7

    def up(v, fill):
        r = [pltpu.roll(x, 7, 0) for x in v]
        fill = jnp.zeros((8, 128), F32) if fill is None else fill
        return [jnp.where(bottom, r[i + 1] if i + 1 < k else fill, r[i]) for i in range(k)]

    def down(v, fill):
        r = [pltpu.roll(x, 1, 0) for x in v]
        return [jnp.where(top, r[i - 1] if i else fill, r[i]) for i in range(k)]

    low, high = lift_list(s, d, up, down, lambda v: v[0], lambda v: v[-1])
    for i in range(k):
        dst[pl.ds(to + 8 * i, 8), :] = low[i]
        if keep_high:
            dst[pl.ds(to + 8 * (k + i), 8), :] = high[i]


def lift_major(rows):
    low, high = lift_list(
        rows[0::2],
        rows[1::2],
        lambda v, fill: v[1:] + [jnp.zeros_like(v[0]) if fill is None else fill],
        lambda v, fill: [fill] + v[:-1],
        lambda v: v[0],
        lambda v: v[-1],
    )
    return low + high


class Side:
    def __init__(self, plan):
        self.groups = {}
        for source in ("from_left", "from_right", "own_left", "own_right"):
            u = plan[source]
            for g in range(u.shape[0] // 8):
                for f in range(u.shape[1]):
                    column = u[8 * g : 8 * g + 8, f]
                    if np.abs(column).max() > 1e-10:
                        self.groups.setdefault(g, []).append((source, f, column))


PLANS = {n: [block_plan(n, level) for level in (1, 2, 3)] for n in (NY, NZ)}
SIDES = {n: [Side(plan) for plan in PLANS[n]] for n in (NY, NZ)}
MIRRORS = mirror_plan(NZ, PLANS[NZ])
SEND_LEFT = {n: rounded(PLANS[n][2]["left"]) for n in (NY, NZ)}
SEND_RIGHT = {n: rounded(PLANS[n][2]["right"]) for n in (NY, NZ)}
SCALES = [(SCALE_LOW**level, SCALE_LOW ** (level - 1) * SCALE_HIGH) for level in (1, 2, 3)]


def factored(matrix):
    u, size, v = np.linalg.svd(matrix, full_matrices=False)
    rank = int((size > 1e-9).sum())
    return rounded(u[:, :rank] * size[:rank]), rounded(v[:rank])


X_ONE = block_plan(NX, 1)
X_ONE_LEFT, X_ONE_RIGHT = rounded(X_ONE["left"]), rounded(X_ONE["right"])
X_ONE_FROM_LEFT, X_ONE_FROM_RIGHT = rounded(X_ONE["from_left"]), rounded(X_ONE["from_right"])
X_TWO_BLOCKS = line_blocks(NX, 2)
X_TWO_FROM_LEFT, X_TWO_RIGHT = factored(X_TWO_BLOCKS[1])
X_TWO_FROM_RIGHT, X_TWO_LEFT = factored(X_TWO_BLOCKS[3])
X_TWO_OWN = rounded(X_TWO_BLOCKS[2])
X_THREE = [rounded(block) for block in line_blocks(NX, 3)]
N_TWO = len(X_TWO_RIGHT)

Y_ROWS = 6 * NX
Z_TWO, Z_THREE, Z_ROWS = 4 * NX, 8 * NX, 8 * NX + 6 * (NX // 2)
X23_ROWS = N_TWO * 64 + 64


def neighbour(axis, step):
    size = SIZES[axis]
    place = {name: lax.axis_index(name) for name in SIZES}
    place[axis] = lax.rem(place[axis] + (step + size), size)
    return tuple(place[name] for name in ("gx", "gy", "gz"))


def build_table(table, sides):
    sub = lax.broadcasted_iota(jnp.int32, (8, 128), 0)
    found = []
    at = 0
    for side in sides:
        places = {}
        for g, terms in side.groups.items():
            for source, f, column in terms:
                value = jnp.zeros((8, 128), F32)
                for i in range(8):
                    if abs(column[i]) > 1e-10:
                        value = jnp.where(sub == i, float(np.float32(column[i])), value)
                table[pl.ds(at, 8), :] = value
                places[g, source, f] = at
                at += 8
        found.append(places)
    return found


def table_rows(sides):
    return 8 * sum(len(terms) for side in sides for terms in side.groups.values())


def correct(ref, base, side, places, table, refs, row):
    for g, terms in side.groups.items():
        terms = [(source, f) for source, f, _ in terms if source in refs]
        if not terms:
            continue
        value = ref[pl.ds(base + 8 * g, 8), :]
        for source, f in terms:
            value = value + table[pl.ds(places[g, source, f], 8), :] * refs[source][pl.ds(row(f), 1), :]
        ref[pl.ds(base + 8 * g, 8), :] = value


def parts_of(value):
    rest, parts = np.asarray(value, np.float32), []
    for _ in range(2):
        part = rest.astype(ml_dtypes.bfloat16)
        parts.append(part)
        rest = rest - part.astype(np.float32)
    return parts


def spread(level):
    plan = PLANS[NY][level - 1]
    left, right = plan["from_left"].T, plan["from_right"].T
    if level == 3:
        blocks = []
        for u in (left, right):
            block = np.zeros((8, NX, 128))
            block[:6, 0::2, :64] = u[:, None, :]
            block[:6, 1::2, 64:] = u[:, None, :]
            blocks.append(block.reshape(128, 128))
        matrix = np.concatenate(blocks)
    else:
        matrix = np.repeat(np.concatenate([left, right]), NX, axis=0)
    one, two = parts_of(matrix)
    return np.concatenate([one, two, one, two])


SPREADS = [spread(level) for level in (1, 2, 3)]
Z_SENDS = np.zeros((40, NZ), np.float32)
for _at, _rows in enumerate((PLANS[NZ][2]["left"], PLANS[NZ][2]["right"], *MIRRORS)):
    Z_SENDS[8 * _at : 8 * _at + 6] = _rows
for _at, _rows in enumerate((X_ONE["left"], X_ONE["right"])):
    for _xf in range(2):
        for _f in range(2):
            Z_SENDS[32 + 4 * _at + 2 * _xf + _f, _f * NX : (_f + 1) * NX] = _rows[_xf]

def split(value):
    one = value.astype(jnp.bfloat16).astype(F32)
    return one, value - one


def lanes_of(shape):
    return lax.broadcasted_iota(jnp.int32, shape, 1)


def slots(level, left, right):
    lane = lanes_of(left.shape)
    turn = lambda value, by: pltpu.roll(value, by, 1)
    if level == 1:
        base = left if right is None else jnp.where(lane < 32, left, jnp.where(lane < 64, turn(right, 32), 0.0))
        one, two = split(base)
        return [one + turn(one, 64), two + turn(two, 64)]
    if level == 2:
        one, two = split(jnp.where(lane < 64, left, turn(right, 64)))
        return [one, one, two, two]
    one, two = zip(split(left), split(right))
    return [*one, *one, *two, *two]


def expand(level, arrays, keep, spread_ref):
    factor = jnp.concatenate([jnp.where(keep, a, 0.0).astype(jnp.bfloat16) for a in arrays], axis=1)
    return jnp.dot(factor, spread_ref[...], preferred_element_type=F32)


def kernel(
    vel, spread1_hbm, spread2_hbm, spread3_hbm, sends_hbm,
    o1, o2, o3, o4,
    w1, w2, w3, x1rl, x1rr, x23rl, x23rr, x3rl, x3rr, eg,
    v, y1, y2, y3, z1, z2, z3, t2, t3, t4, ytab, ztab,
    ysl, ysr, yrl, yrr, zsl, zsr, zrl, zrr, zml, zmr,
    htl, htr, g1, g2, g3, u2, u3, p1, p2, p3, csl, csr, zlsl, zlsr, zlml, zlmr,
    x1sl, x1sr, x23sl, x23sr, x3sl, x3sr, xesl, xesr, xerl, xerr,
    spread1, spread2, spread3, sends, zc, zf, q2, q3,
    load_sems, send_sems, recv_sems,
):
    loads = [
        pltpu.make_async_copy(src, dst, load_sems.at[i])
        for i, (src, dst) in enumerate(
            ((vel, v), (sends_hbm, sends), (spread1_hbm, spread1), (spread2_hbm, spread2), (spread3_hbm, spread3))
        )
    ]
    for load in loads:
        load.start()
    near = {
        "yl": neighbour("gy", -1), "yr": neighbour("gy", 1), "zl": neighbour("gz", -1), "zr": neighbour("gz", 1),
        "xl": neighbour("gx", -1), "xr": neighbour("gx", 1), "xll": neighbour("gx", -2), "xrr": neighbour("gx", 2),
    }
    barrier = pltpu.get_barrier_semaphore()
    for device in near.values():
        pl.semaphore_signal(barrier, inc=1, device_id=device, device_id_type=MESH)
    y_places = build_table(ytab, SIDES[NY])
    z_places = build_table(ztab, SIDES[NZ])
    for ref in (yrl, yrr, ysl, ysr):
        ref[pl.ds(Y_ROWS, 32), :] = jnp.zeros((32, 128), F32)
    eg[...] = jnp.zeros((128, 128), F32)

    def remote(index, src, dst, to):
        return pltpu.make_async_remote_copy(
            src_ref=src,
            dst_ref=dst,
            send_sem=send_sems.at[index],
            recv_sem=recv_sems.at[index],
            device_id=near[to],
            device_id_type=MESH,
        )

    loads[0].wait()

    for h in range(2):
        head = [v[pl.ds(h * 8 * NY + k, 8, stride=NY), :] for k in range(21)]
        tail = [v[pl.ds(h * 8 * NY + k, 8, stride=NY), :] for k in range(NY - 28, NY)]
        for f in range(6):
            ysl[pl.ds(f * NX + 8 * h, 8), :] = fir(SEND_LEFT[NY][f][:21], head)
            ysr[pl.ds(f * NX + 8 * h, 8), :] = fir(SEND_RIGHT[NY][f][-28:], tail)

    loads[1].wait()
    for at, ref in enumerate((ysl, ysr)):
        sums = jnp.dot(
            sends[pl.ds(0, 16), :], ref[...].T, precision=lax.Precision.HIGHEST, preferred_element_type=F32
        )
        csl[pl.ds(8 * at, 8), :] = sums[:8]
        csr[pl.ds(8 * at, 8), :] = sums[8:]
    corners = []
    for at in range(2):
        corners.append(remote(4 + at, csl.at[pl.ds(8 * at, 8)], zc.at[pl.ds(16 * at, 8)], "zl"))
        corners.append(remote(16 + at, csr.at[pl.ds(8 * at, 8)], zc.at[pl.ds(16 * at + 8, 8)], "zr"))
    pl.semaphore_wait(barrier, len(near))
    for copy in corners:
        copy.start()
    y_left = remote(0, ysl.at[pl.ds(0, Y_ROWS)], yrr.at[pl.ds(0, Y_ROWS)], "yl")
    y_right = remote(1, ysr.at[pl.ds(0, Y_ROWS)], yrl.at[pl.ds(0, Y_ROWS)], "yr")
    y_left.start()
    y_right.start()

    def lift_y(x, c):
        lift_rows(v, x * NY, NY, y1, x * NY)
        lift_rows(y1, x * NY, NY // 2, y2, x * (NY // 2))
        lift_rows(y2, x * (NY // 2), NY // 4, y3, x * (NY // 4))
        own = {"own_left": ysl, "own_right": ysr}
        for level, ref in ((1, y2), (2, y3)):
            correct(ref, x * (NY >> level), SIDES[NY][level], y_places[level], ytab, own, lambda f: f * NX + x)
        return c

    lax.fori_loop(0, NX, lift_y, 0, unroll=2)
    def turn_one(x, c):
        for t in range(2):
            z1[pl.ds(x * 256 + 128 * t, 128), :] = y1[pl.ds(x * NY + 128 * t, 128), :].T
        return c

    def turn_two(x, c):
        z2[pl.ds(x * 128, 128), :] = y2[pl.ds(x * 128, 128), :].T
        return c

    def turn_three(p, c):
        z3[pl.ds(p * 128, 128), :] = y3[pl.ds(p * 128, 128), :].T
        return c

    def z_sums(level, load_row, store):
        rows = {}

        def row(k):
            if k not in rows:
                rows[k] = load_row(k)
            return rows[k]

        for f in range(2 * level):
            for at, ref in enumerate((zsl, zsr, zml, zmr)):
                weights = [float(c) for c in Z_SENDS[8 * at + f]]
                ks = [k for k in range(NZ) if weights[k] != 0.0]
                store(ref, f, fir([weights[k] for k in ks], [row(k) for k in ks]))

    lax.fori_loop(0, NX // 2, turn_three, 0, unroll=8)
    lax.fori_loop(0, NX, turn_two, 0, unroll=16)

    def store_three(ref, f, value):
        ref[pl.ds(Z_THREE + f * (NX // 2), 8), :] = value

    z_sums(3, lambda k: z3[pl.ds(k, 8, stride=128), :], store_three)
    for h in range(2):

        def store_two(ref, f, value, h=h):
            ref[pl.ds(Z_TWO + f * NX + 8 * h, 8), :] = value

        z_sums(2, lambda k, h=h: z2[pl.ds(h * 8 * 128 + k, 8, stride=128), :], store_two)
    deep = pl.ds(Z_TWO, Z_ROWS - Z_TWO)
    z_left = remote(2, zsl.at[deep], zrr.at[deep], "zl")
    z_right = remote(3, zsr.at[deep], zrl.at[deep], "zr")
    z_left.start()
    z_right.start()

    def lift_z1(i, c):
        lift_rows(z1, i * NZ, NZ, w1, i * NZ)
        return c

    lax.fori_loop(0, NX, turn_one, 0, unroll=8)
    for copy in corners:
        copy.wait()
    zf_left = remote(18, zc.at[pl.ds(0, 16)], zf.at[pl.ds(0, 16)], "yl")
    zf_right = remote(19, zc.at[pl.ds(16, 16)], zf.at[pl.ds(16, 16)], "yr")
    zf_left.start()
    zf_right.start()
    lax.fori_loop(0, 6, lift_z1, 0, unroll=6)
    lax.fori_loop(24, 32, lift_z1, 0, unroll=4)

    def sums_one(g, c):
        rows = [w1[pl.ds(x * 256 + 8 * g, 8), :] for x in (0, 1, 2, 12, 13, 14, 15)]
        for f in range(2):
            x1sl[pl.ds(f * 256 + 8 * g, 8), :] = fir(X_ONE_LEFT[f][:3], rows[:3])
            x1sr[pl.ds(f * 256 + 8 * g, 8), :] = fir(X_ONE_RIGHT[f][12:], rows[3:])
        return c

    lax.fori_loop(0, 32, sums_one, 0, unroll=4)
    x1_left = remote(6, x1sl, x1rr, "xl")
    x1_right = remote(7, x1sr, x1rl, "xr")
    x1_left.start()
    x1_right.start()
    for h in range(2):
        for t in range(2):

            def store_one(ref, f, value, h=h, t=t):
                ref[pl.ds((f * 2 + t) * NX + 8 * h, 8), :] = value

            z_sums(1, lambda k, h=h, t=t: z1[pl.ds(h * 8 * 256 + t * 128 + k, 8, stride=256), :], store_one)
    first = pl.ds(0, Z_TWO)
    z1_left = remote(14, zsl.at[first], zrr.at[first], "zl")
    z1_right = remote(15, zsr.at[first], zrl.at[first], "zr")
    z1_left.start()
    z1_right.start()

    row_one = lambda x, t: lambda f: (f * 2 + t) * NX + x
    row_two = lambda x: lambda f: Z_TWO + f * NX + x
    row_three = lambda p: lambda f: Z_THREE + f * (NX // 2) + p
    z_own = {"own_left": zsl, "own_right": zsr}

    def lift_z2(x, c):
        lift_rows(z2, x * NZ, NZ, t2, x * 64, keep_high=False)
        lift_rows(t2, x * 64, 64, w2, x * 64)
        correct(w2, x * 64, SIDES[NZ][1], z_places[1], ztab, z_own, row_two(x))
        return c

    def lift_z3(p, c):
        lift_rows(z3, p * NZ, NZ, t3, p * 64, keep_high=False)
        lift_rows(t3, p * 64, 64, t4, p * 32, keep_high=False)
        lift_rows(t4, p * 32, 32, w3, p * 32)
        correct(w3, p * 32, SIDES[NZ][2], z_places[2], ztab, z_own, row_three(p))
        return c

    lax.fori_loop(0, NX // 2, lift_z3, 0, unroll=4)
    lax.fori_loop(0, NX, lift_z2, 0, unroll=4)

    y_left.wait()
    y_right.wait()
    for load in loads[2:]:
        load.wait()
    htl[...] = yrl[...].T
    htr[...] = yrr[...].T
    for at, ref in ((0, htl), (8, htr)):
        sums = jnp.dot(sends[pl.ds(0, 32), :], ref[...], precision=lax.Precision.HIGHEST, preferred_element_type=F32)
        for i, out in enumerate((zlsl, zlsr, zlml, zlmr)):
            out[pl.ds(at, 8), :] = sums[8 * i : 8 * i + 8]
    for i, ref in enumerate((htl, htr)):
        lift_rows(ref, 0, 128, g1, 128 * i)
        lift_rows(g1, 128 * i, 64, u2, 64 * i)
        lift_rows(u2, 64 * i, 32, u3, 32 * i)
    for i in range(2):
        own = {"own_left": zlsl, "own_right": zlsr}
        g2[pl.ds(64 * i, 64), :] = u2[pl.ds(64 * i, 64), :]
        g3[pl.ds(32 * i, 32), :] = u3[pl.ds(32 * i, 32), :]
        correct(g2, 64 * i, SIDES[NZ][1], z_places[1], ztab, own, lambda f, i=i: 8 * i + f)
        correct(g3, 32 * i, SIDES[NZ][2], z_places[2], ztab, own, lambda f, i=i: 8 * i + f)
    for level, g, p, n in ((1, g1, p1, 128), (2, g2, p2, 64), (3, g3, p3, 32)):
        for i, value in enumerate(slots(level, g[pl.ds(0, n), :], g[pl.ds(n, n), :])):
            p[pl.ds(n * i, n), :] = value

    sums = lax.dot_general(
        sends[pl.ds(32, 8), :],
        g1[...],
        (((1,), (1,)), ((), ())),
        precision=lax.Precision.HIGHEST,
        preferred_element_type=F32,
    )
    for way, ref in enumerate((xesl, xesr)):
        for xf in range(2):
            for side in range(2):
                at = 4 * way + 2 * xf
                ref[pl.ds(16 + 4 * xf + 2 * side, 2), :] = sums[at : at + 2, 128 * side : 128 * side + 128]
    xg_left = remote(20, xesl.at[pl.ds(16, 8)], xerr.at[pl.ds(16, 8)], "xl")
    xg_right = remote(21, xesr.at[pl.ds(16, 8)], xerl.at[pl.ds(16, 8)], "xr")
    xg_left.start()
    xg_right.start()

    def spread_one(x, c):
        keep = (lanes_of((128, 128)) & 15) == x
        value = expand(1, [p1[pl.ds(128 * i, 128), :] for i in range(2)], keep, spread1)
        for t in range(2):
            at = pl.ds(x * 256 + 128 * t, 128)
            w1[at, :] = w1[at, :] + value[:, 128 * t : 128 * t + 128]
        return c

    def spread_two(x, c):
        keep = (lanes_of((64, 128)) & 15) == x
        at = pl.ds(x * 64, 64)
        w2[at, :] = w2[at, :] + expand(2, [p2[pl.ds(64 * i, 64), :] for i in range(4)], keep, spread2)
        return c

    def spread_three(p, c):
        keep = ((lanes_of((32, 128)) & 15) >> 1) == p
        at = pl.ds(p * 32, 32)
        w3[at, :] = w3[at, :] + expand(3, [p3[pl.ds(32 * i, 32), :] for i in range(8)], keep, spread3)
        return c

    lax.fori_loop(0, NX // 2, spread_three, 0, unroll=8)
    lax.fori_loop(0, NX, spread_two, 0, unroll=16)

    for copy in (z_left, z_right, zf_left, zf_right):
        copy.wait()
    gz = lax.axis_index("gz")

    @pl.when(gz == 0)
    def _():
        zrl[deep, :] = zml[deep, :]
        zf[pl.ds(24, 8), :] = zlml[pl.ds(0, 8), :]
        zf[pl.ds(8, 8), :] = zlml[pl.ds(8, 8), :]

    @pl.when(gz == SIZES["gz"] - 1)
    def _():
        zrr[deep, :] = zmr[deep, :]
        zf[pl.ds(16, 8), :] = zlmr[pl.ds(0, 8), :]
        zf[pl.ds(0, 8), :] = zlmr[pl.ds(8, 8), :]

    def complete(level):
        lane, sub = lanes_of((16, 128)), lax.broadcasted_iota(jnp.int32, (16, 128), 0)
        count = NX // 2 if level == 3 else NX
        keep = ((lane[:8] & 15) >> 1) == sub[:8] if level == 3 else (lane & 15) == sub
        tall = []
        for at in (8, 0):
            arrays = slots(level, zf[pl.ds(16 + at, 8), :], zf[pl.ds(at, 8), :])
            tall.append([
                jnp.concatenate([jnp.where(keep, a[f : f + 1], 0.0) for f in range(2 * level)], axis=0) for a in arrays
            ])
        both = [jnp.concatenate(pair, axis=0) for pair in zip(*tall)]
        value = expand(level, both, jnp.full(both[0].shape, True), (spread1, spread2, spread3)[level - 1])
        for side, ref in enumerate((zrl, zrr)):
            for f in range(2 * level):
                first_row = (side * 2 * level + f) * count
                piece = value[first_row : first_row + count]
                if level == 1:
                    for t in range(2):
                        at = pl.ds((f * 2 + t) * NX, NX)
                        ref[at, :] = ref[at, :] + piece[:, 128 * t : 128 * t + 128]
                else:
                    at = pl.ds((Z_TWO if level == 2 else Z_THREE) + f * count, count)
                    ref[at, :] = ref[at, :] + piece

    complete(3)
    complete(2)

    for copy in (z1_left, z1_right):
        copy.wait()

    @pl.when(gz == 0)
    def _():
        zrl[first, :] = zml[first, :]

    @pl.when(gz == SIZES["gz"] - 1)
    def _():
        zrr[first, :] = zmr[first, :]

    complete(1)

    for side, ref in enumerate((zrl, zrr)):
        for f in range(2):
            for t in range(2):
                rows = [ref[pl.ds((f * 2 + t) * NX + x, 1), :] for x in (0, 1, 2, 12, 13, 14, 15)]
                for xf in range(2):
                    at = pl.ds((xf * 2 + t) * 4 + side * 2 + f, 1)
                    xesl[at, :] = fir(X_ONE_LEFT[xf][:3], rows[:3])
                    xesr[at, :] = fir(X_ONE_RIGHT[xf][12:], rows[3:])
    xe_left = remote(8, xesl.at[pl.ds(0, 16)], xerr.at[pl.ds(0, 16)], "xl")
    xe_right = remote(9, xesr.at[pl.ds(0, 16)], xerl.at[pl.ds(0, 16)], "xr")
    xe_left.start()
    xe_right.start()

    z_past = {"from_left": zrl, "from_right": zrr}

    def finish_z2(x, c):
        correct(w2, x * 64, SIDES[NZ][1], z_places[1], ztab, z_past, row_two(x))
        return c

    def finish_z3(p, c):
        correct(w3, p * 32, SIDES[NZ][2], z_places[2], ztab, z_past, row_three(p))
        return c

    lax.fori_loop(0, NX // 2, finish_z3, 0, unroll=8)
    lax.fori_loop(0, NX, finish_z2, 0, unroll=16)

    three_to = ((x23sr, N_TWO * 64), (x23sl, N_TWO * 64), (x3sr, 0), (x3sl, 0))

    def sums_two(g, c):
        rows = [w2[pl.ds(x * 64 + 8 * g, 8), :] for x in range(NX)]
        for f in range(N_TWO):
            x23sl[pl.ds(f * 64 + 8 * g, 8), :] = fir(X_TWO_LEFT[f], rows)
            x23sr[pl.ds(f * 64 + 8 * g, 8), :] = fir(X_TWO_RIGHT[f], rows)
        return c

    def send_three(g, c):
        rows = [w3[pl.ds(p * 32 + 8 * g, 8), :] for p in range(NX // 2)]
        for (ref, at), block in zip(three_to, (1, 3, 0, 4)):
            for h, value in enumerate(sums_three(X_THREE[block], rows)):
                ref[pl.ds(at + 32 * h + 8 * g, 8), :] = value
        return c

    lax.fori_loop(0, 8, sums_two, 0, unroll=8)
    lax.fori_loop(0, 4, send_three, 0, unroll=4)
    x23_left = remote(10, x23sl, x23rr, "xl")
    x23_right = remote(11, x23sr, x23rl, "xr")
    x3_left = remote(12, x3sl, x3rr, "xll")
    x3_right = remote(13, x3sr, x3rl, "xrr")
    for copy in (x23_left, x23_right, x3_left, x3_right):
        copy.start()

    def finish_z1(x, c):
        for t in range(2):
            correct(w1, x * 256 + 128 * t, SIDES[NZ][0], z_places[0], ztab, z_past, row_one(x, t))
        return c

    lax.fori_loop(6, 24, lift_z1, 0, unroll=6)
    lax.fori_loop(0, NX, spread_one, 0, unroll=4)
    lax.fori_loop(0, NX, finish_z1, 0)
    def own_two(g, c):
        rows = [w2[pl.ds(x * 64 + 8 * g, 8), :] for x in range(NX)]
        for i in range(8):
            q2[pl.ds(i * 64 + 8 * g, 8), :] = fir(X_TWO_OWN[i], rows)
        return c

    def own_three(g, c):
        rows = [w3[pl.ds(p * 32 + 8 * g, 8), :] for p in range(NX // 2)]
        for h, value in enumerate(sums_three(X_THREE[2], rows)):
            q3[pl.ds(32 * h + 8 * g, 8), :] = value
        return c

    lax.fori_loop(0, 8, own_two, 0, unroll=2)
    lax.fori_loop(0, 4, own_three, 0, unroll=2)
    for copy in (x1_left, x1_right, xg_left, xg_right, xe_left, xe_right):
        copy.wait()
    for side, ends in enumerate((xerl, xerr)):
        for xf in range(2):
            for h in range(4):
                eg[pl.ds(NX * h + 2 * side + xf, 1), :] = ends[pl.ds(16 + 4 * xf + h, 1), :]
    arrays = slots(1, eg[...].T, None)
    for side, ref in enumerate((x1rl, x1rr)):
        for xf in range(2):
            value = expand(1, arrays, (lanes_of((128, 128)) & 15) == 2 * side + xf, spread1)
            for t in range(2):
                at = pl.ds(xf * 256 + 128 * t, 128)
                ref[at, :] = ref[at, :] + value[:, 128 * t : 128 * t + 128]
    for xf in range(2):
        for t in range(2):
            for ref, ends in ((x1rl, xerl), (x1rr, xerr)):
                at = (xf * 2 + t) * 4
                refs = {"from_left": ends.at[pl.ds(at, 2)], "from_right": ends.at[pl.ds(at + 2, 2)]}
                correct(ref, xf * 256 + 128 * t, SIDES[NZ][0], z_places[0], ztab, refs, lambda f: f)
    for hy in range(2):
        for hz in range(2):

            def out_one(g, c, hy=hy, hz=hz):
                row = 128 * hy + 64 * hz + 8 * g
                rows = [w1[pl.ds(x * 256 + row, 8), :] for x in range(NX)]
                left = [x1rl[pl.ds(f * 256 + row, 8), :] for f in range(2)]
                right = [x1rr[pl.ds(f * 256 + row, 8), :] for f in range(2)]
                for i, value in enumerate(lift_major(rows)):
                    hx = i // 8
                    band = 4 * hx + 2 * hy + hz
                    if not band:
                        continue
                    value = fir([1.0] + X_ONE_FROM_LEFT[i] + X_ONE_FROM_RIGHT[i], [value] + left + right)
                    value = value * (SCALES[0][hx] * SCALES[0][hy] * SCALES[0][hz])
                    o1[pl.ds((band - 1) * 512 + (i % 8) * 64 + 8 * g, 8), :] = value
                return c

            lax.fori_loop(0, 8, out_one, 0, unroll=2)
    for copy in (x23_left, x23_right, x3_left, x3_right):
        copy.wait()
    lane = lanes_of((8, 128))
    low_lanes = lane < 64

    def out_two(g, hz):
        left = [x23rl[pl.ds(f * 64 + 8 * g, 8), :] for f in range(N_TWO)]
        right = [x23rr[pl.ds(f * 64 + 8 * g, 8), :] for f in range(N_TWO)]
        for i in range(8):
            hx = i // 4
            own = q2[pl.ds(i * 64 + 8 * g, 8), :]
            value = fir([1.0] + X_TWO_FROM_LEFT[i] + X_TWO_FROM_RIGHT[i], [own] + left + right)
            scale = SCALES[1][hx] * SCALES[1][hz]
            value = value * jnp.where(low_lanes, scale * SCALES[1][0], scale * SCALES[1][1])
            for hy in range(2):
                band = 4 * hx + 2 * hy + hz
                if band:
                    at = (band - 1) * 128 + (i % 4) * 32 + 8 * (g % 4)
                    o2[pl.ds(at, 8), :] = value[:, 64 * hy : 64 * hy + 64]

    for g in range(8):
        out_two(g, g // 4)

    def out_three(g, hz):
        high_y = (lane & 63) >= 32
        for hx in range(2):
            value = q3[pl.ds(32 * hx + 8 * g, 8), :]
            for ref, at in ((x23rl, N_TWO * 64), (x23rr, N_TWO * 64), (x3rl, 0), (x3rr, 0)):
                value = value + ref[pl.ds(at + 32 * hx + 8 * g, 8), :]
            scale = SCALES[2][hx] * SCALES[2][hz]
            value = value * jnp.where(high_y, scale * SCALES[2][1], scale * SCALES[2][0])
            for q in range(4):
                i, hy = divmod(q, 2)
                band = 4 * hx + 2 * hy + hz
                row = 16 * i + 8 * (g % 2)
                piece = value[:, 32 * q : 32 * q + 32]
                if band:
                    o3[pl.ds((band - 1) * 32 + row, 8), :] = piece
                else:
                    o4[pl.ds(row, 8), :] = piece

    for g in range(4):
        out_three(g, g // 2)


def paired(weights, rows):
    low_lanes = lanes_of((8, 128)) < 64
    total = jnp.zeros((8, 128), F32)
    for p in range(NX // 2):
        if weights[2 * p] == 0.0 and weights[2 * p + 1] == 0.0:
            continue
        total = total + jnp.where(low_lanes, weights[2 * p], weights[2 * p + 1]) * rows[p]
    return total + pltpu.roll(total, 64, 1)


def sums_three(matrix, rows):
    low_lanes = lanes_of((8, 128)) < 64
    return [jnp.where(low_lanes, paired(matrix[2 * h], rows), paired(matrix[2 * h + 1], rows)) for h in range(2)]


def write(o1, o2, o3, o4, out1, out2, out3, out4, sems):
    copies = []
    for src, dst, parts in ((o1, out1, 7), (o2, out2, 1), (o3, out3, 1), (o4, out4, 1)):
        rows = src.shape[0] // parts
        for i in range(parts):
            at = pl.ds(i * rows, rows)
            copies.append(pltpu.make_async_copy(src.at[at], dst.at[at], sems.at[len(copies)]))
            copies[-1].start()
    for copy in copies:
        copy.wait()


def shards(velocity):
    vmem, hbm = pl.BlockSpec(memory_space=pltpu.VMEM), pl.BlockSpec(memory_space=pltpu.HBM)
    wide = lambda rows: pltpu.VMEM((rows, 128), F32)
    shapes = [(7 * 8 * 64, 128), (7 * 4 * 32, 64), (7 * 2 * 16, 32), (2 * 16, 32)]
    scratch = [32 * NZ, 16 * 64, 8 * 32, 512, 512, X23_ROWS, X23_ROWS, 64, 64, 128]
    scratch += [16 * NY, 16 * NY, 16 * NY // 2, 16 * NY // 4]
    scratch += [32 * NZ, 16 * NZ, 8 * NZ]
    scratch += [16 * 64, 8 * 64, 8 * 32]
    scratch += [table_rows(SIDES[NY]), table_rows(SIDES[NZ])]
    scratch += [128] * 4 + [Z_ROWS] * 6
    scratch += [128, 128, 256, 128, 64, 128, 64, 2 * 128, 4 * 64, 8 * 32] + [16] * 6
    scratch += [512] * 2 + [X23_ROWS] * 2 + [64] * 2 + [24] * 4
    operands = [velocity.reshape(NX * NY, NZ), *[jnp.asarray(matrix) for matrix in SPREADS], jnp.asarray(Z_SENDS)]
    got = pl.pallas_call(
        kernel,
        out_shape=[jax.ShapeDtypeStruct(shape, F32) for shape in shapes],
        in_specs=[hbm] * 5,
        out_specs=[vmem] * 4,
        scratch_shapes=[wide(rows) for rows in scratch]
        + [pltpu.VMEM(matrix.shape, jnp.bfloat16) for matrix in SPREADS]
        + [wide(rows) for rows in (40, 32, 32, 512, 64)]
        + [pltpu.SemaphoreType.DMA((5,)), pltpu.SemaphoreType.DMA((22,)), pltpu.SemaphoreType.DMA((22,))],
        compiler_params=pltpu.CompilerParams(collective_id=0, has_side_effects=True, vmem_limit_bytes=28 * 2**20),
    )(*[pltpu.with_memory_space_constraint(a, pltpu.HBM) for a in operands])
    out1, out2, out3, out4 = pl.pallas_call(
        write,
        out_shape=[jax.ShapeDtypeStruct(shape, F32) for shape in shapes],
        in_specs=[vmem] * 4,
        out_specs=[hbm] * 4,
        scratch_shapes=[pltpu.SemaphoreType.DMA((10,))],
        compiler_params=pltpu.CompilerParams(vmem_limit_bytes=16 * 2**20),
    )(*got)
    return (
        out1.reshape(7, 8, 64, 128).transpose(0, 1, 3, 2),
        out2.reshape(7, 4, 32, 64).transpose(0, 1, 3, 2),
        out3.reshape(7, 2, 16, 32).transpose(0, 1, 3, 2),
        out4.reshape(2, 16, 32).transpose(0, 2, 1),
    )


def solution(mesh):
    return jax.shard_map(
        shards,
        mesh=mesh,
        in_specs=(P("gx", "gy", "gz"),),
        out_specs=(
            P(None, "gx", "gy", "gz"),
            P(None, "gx", "gy", "gz"),
            P(None, "gx", "gy", "gz"),
            P("gx", "gy", "gz"),
        ),
        check_vma=False,
    )
```

```python
import math

import jax
import jax.numpy as jnp
import ml_dtypes
import numpy as np
from jax import lax
from jax.experimental import pallas as pl
from jax.experimental.pallas import tpu as pltpu
from jax.sharding import PartitionSpec as P

ALPHA = -1.586134342059924
BETA = -0.052980118572961
GAMMA = 0.882911075530934
DELTA = 0.443506852043971
SCALE_LOW = math.sqrt(2.0) / 1.230174104914001
SCALE_HIGH = 1.230174104914001 / math.sqrt(2.0)


def lift_matrix(rows, edges):
    s, d = rows[0::2], rows[1::2]
    none = np.zeros_like(s[:1])
    if edges == "periodic":
        d = d + ALPHA * (s + np.roll(s, -1, 0))
        s = s + BETA * (np.roll(d, 1, 0) + d)
        d = d + GAMMA * (s + np.roll(s, -1, 0))
        s = s + DELTA * (np.roll(d, 1, 0) + d)
        return s, d
    start, end = edges
    up = lambda v, last: np.concatenate([v[1:], last])
    down = lambda v, first: np.concatenate([first, v[:-1]])
    d1 = d + ALPHA * (s + up(s, s[-1:] if end else none))
    before1 = d1[:1] if start else ALPHA * s[:1]
    s1 = s + BETA * (down(d1, before1) + d1)
    d2 = d1 + GAMMA * (s1 + up(s1, s1[-1:] if end else BETA * d1[-1:]))
    before2 = d2[:1] if start else before1 + GAMMA * (BETA * before1 + s1[:1])
    return s1 + DELTA * (down(d2, before2) + d2), d2


def path_matrix(rows, level, edges):
    for _ in range(level):
        rows, high = lift_matrix(rows, edges)
    return np.concatenate([rows, high])


def outgoing(n):
    rows, left, right = np.eye(n), [], []
    for _ in range(3):
        s, d = rows[0::2], rows[1::2]
        left += [s[0], s[0] + BETA * (d[0] + ALPHA * (s[0] + s[1]))]
        right += [d[-1] + ALPHA * s[-1], s[-1] + BETA * (d[-2] + ALPHA * (s[-2] + s[-1]))]
        rows = lift_matrix(rows, (False, False))[0]
    return np.stack(left), np.stack(right)


def line_blocks(n, level):
    m = n >> level
    rows = np.eye(5 * n)
    for _ in range(level):
        rows, high = lift_matrix(rows, "periodic")
    whole = np.concatenate([rows[2 * m : 3 * m], high[2 * m : 3 * m]])
    return [whole[:, k * n : (k + 1) * n] for k in range(5)]


def solved(target, basis):
    u = np.linalg.lstsq(basis.T, target.T, rcond=None)[0].T
    assert np.abs(u @ basis - target).max() < 1e-9
    return np.where(np.abs(u) < 1e-10, 0.0, u)


def block_plan(n, level):
    left, right = outgoing(n)
    left, right = left[: 2 * level], right[: 2 * level]
    blocks = line_blocks(n, level)
    alone = path_matrix(np.eye(n), level, (False, False))
    from_left = solved(blocks[1], right)
    from_right = solved(blocks[3], left)
    own = solved(blocks[2] - alone, np.concatenate([left, right]))
    return dict(left=left, right=right, alone=alone, from_left=from_left, from_right=from_right, own_left=own[:, : 2 * level], own_right=own[:, 2 * level :])


def mirror_plan(n, plans):
    out = []
    for start in (True, False):
        uses, rests = [], []
        for level, plan in enumerate(plans, 1):
            m = n >> level
            rows = np.eye(4 * n)
            for _ in range(level):
                rows, high = lift_matrix(rows, (True, True))
            at = 0 if start else 3
            whole = np.concatenate([rows[at * m : (at + 1) * m], high[at * m : (at + 1) * m]])
            whole = whole[:, at * n : (at + 1) * n]
            rests.append(whole - plan["alone"] - plan["own_left"] @ plan["left"] - plan["own_right"] @ plan["right"])
            u = plan["from_left"] if start else plan["from_right"]
            uses.append(np.pad(u, ((0, 0), (0, 6 - u.shape[1]))))
        use, rest = np.concatenate(uses), np.concatenate(rests)
        g = np.linalg.lstsq(use, rest, rcond=None)[0]
        assert np.abs(use @ g - rest).max() < 1e-9
        out.append(np.where(np.abs(g) < 1e-10, 0.0, g))
    return out


MESH = pl.DeviceIdType.MESH
SIZES = {"gx": 8, "gy": 4, "gz": 4}
NX, NY, NZ = 16, 256, 128
F32 = jnp.float32


def rounded(matrix):
    return [[float(np.float32(c)) if abs(c) > 1e-10 else 0.0 for c in row] for row in matrix]


def fir(weights, rows):
    total = None
    for weight, row in zip(weights, rows):
        if weight == 0.0:
            continue
        term = row() if callable(row) else row
        term = term if weight == 1.0 else weight * term
        total = term if total is None else total + term
    return total


def lift_list(s, d, up, down, first, last):
    before1 = ALPHA * first(s)
    d1 = [b + ALPHA * (a + c) for a, b, c in zip(s, d, up(s, None))]
    s1 = [a + BETA * (b + c) for a, b, c in zip(s, d1, down(d1, before1))]
    d2 = [b + GAMMA * (a + c) for a, b, c in zip(s1, d1, up(s1, BETA * last(d1)))]
    before2 = before1 + GAMMA * (BETA * before1 + first(s1))
    s2 = [a + DELTA * (b + c) for a, b, c in zip(s1, d2, down(d2, before2))]
    return s2, d2


def lift_rows(src, base, n, dst, to, keep_high=True):
    k = n // 16
    s = [src[pl.ds(base + 16 * i, 8, stride=2), :] for i in range(k)]
    d = [src[pl.ds(base + 16 * i + 1, 8, stride=2), :] for i in range(k)]
    sub = lax.broadcasted_iota(jnp.int32, (8, 128), 0)
    top, bottom = sub == 0, sub == 7

    def up(v, fill):
        r = [pltpu.roll(x, 7, 0) for x in v]
        fill = jnp.zeros((8, 128), F32) if fill is None else fill
        return [jnp.where(bottom, r[i + 1] if i + 1 < k else fill, r[i]) for i in range(k)]

    def down(v, fill):
        r = [pltpu.roll(x, 1, 0) for x in v]
        return [jnp.where(top, r[i - 1] if i else fill, r[i]) for i in range(k)]

    low, high = lift_list(s, d, up, down, lambda v: v[0], lambda v: v[-1])
    for i in range(k):
        dst[pl.ds(to + 8 * i, 8), :] = low[i]
        if keep_high:
            dst[pl.ds(to + 8 * (k + i), 8), :] = high[i]


def lift_major(rows):
    low, high = lift_list(
        rows[0::2],
        rows[1::2],
        lambda v, fill: v[1:] + [jnp.zeros_like(v[0]) if fill is None else fill],
        lambda v, fill: [fill] + v[:-1],
        lambda v: v[0],
        lambda v: v[-1],
    )
    return low + high


class Side:
    def __init__(self, plan):
        self.groups = {}
        for source in ("from_left", "from_right", "own_left", "own_right"):
            u = plan[source]
            for g in range(u.shape[0] // 8):
                for f in range(u.shape[1]):
                    column = u[8 * g : 8 * g + 8, f]
                    if np.abs(column).max() > 1e-10:
                        self.groups.setdefault(g, []).append((source, f, column))


PLANS = {n: [block_plan(n, level) for level in (1, 2, 3)] for n in (NY, NZ)}
SIDES = {n: [Side(plan) for plan in PLANS[n]] for n in (NY, NZ)}
MIRRORS = mirror_plan(NZ, PLANS[NZ])
SEND_LEFT = {n: rounded(PLANS[n][2]["left"]) for n in (NY, NZ)}
SEND_RIGHT = {n: rounded(PLANS[n][2]["right"]) for n in (NY, NZ)}
SCALES = [(SCALE_LOW**level, SCALE_LOW ** (level - 1) * SCALE_HIGH) for level in (1, 2, 3)]


def factored(matrix):
    u, size, v = np.linalg.svd(matrix, full_matrices=False)
    rank = int((size > 1e-9).sum())
    return rounded(u[:, :rank] * size[:rank]), rounded(v[:rank])


X_ONE = block_plan(NX, 1)
X_ONE_LEFT, X_ONE_RIGHT = rounded(X_ONE["left"]), rounded(X_ONE["right"])
X_ONE_FROM_LEFT, X_ONE_FROM_RIGHT = rounded(X_ONE["from_left"]), rounded(X_ONE["from_right"])
X_TWO_BLOCKS = line_blocks(NX, 2)
X_TWO_FROM_LEFT, X_TWO_RIGHT = factored(X_TWO_BLOCKS[1])
X_TWO_FROM_RIGHT, X_TWO_LEFT = factored(X_TWO_BLOCKS[3])
X_TWO_OWN = rounded(X_TWO_BLOCKS[2])
X_THREE = [rounded(block) for block in line_blocks(NX, 3)]
N_TWO = len(X_TWO_RIGHT)

Y_ROWS = 6 * NX
Z_TWO, Z_THREE, Z_ROWS = 4 * NX, 8 * NX, 8 * NX + 6 * (NX // 2)
X23_ROWS = N_TWO * 64 + 64


def neighbour(axis, step):
    size = SIZES[axis]
    place = {name: lax.axis_index(name) for name in SIZES}
    place[axis] = lax.rem(place[axis] + (step + size), size)
    return tuple(place[name] for name in ("gx", "gy", "gz"))


def build_table(table, sides):
    sub = lax.broadcasted_iota(jnp.int32, (8, 128), 0)
    found = []
    at = 0
    for side in sides:
        places = {}
        for g, terms in side.groups.items():
            for source, f, column in terms:
                value = jnp.zeros((8, 128), F32)
                for i in range(8):
                    if abs(column[i]) > 1e-10:
                        value = jnp.where(sub == i, float(np.float32(column[i])), value)
                table[pl.ds(at, 8), :] = value
                places[g, source, f] = at
                at += 8
        found.append(places)
    return found


def table_rows(sides):
    return 8 * sum(len(terms) for side in sides for terms in side.groups.values())


def correct(ref, base, side, places, table, refs, row):
    for g, terms in side.groups.items():
        terms = [(source, f) for source, f, _ in terms if source in refs]
        if not terms:
            continue
        value = ref[pl.ds(base + 8 * g, 8), :]
        for source, f in terms:
            value = value + table[pl.ds(places[g, source, f], 8), :] * refs[source][pl.ds(row(f), 1), :]
        ref[pl.ds(base + 8 * g, 8), :] = value


def parts_of(value):
    rest, parts = np.asarray(value, np.float32), []
    for _ in range(2):
        part = rest.astype(ml_dtypes.bfloat16)
        parts.append(part)
        rest = rest - part.astype(np.float32)
    return parts


def spread(level):
    plan = PLANS[NY][level - 1]
    left, right = plan["from_left"].T, plan["from_right"].T
    if level == 3:
        blocks = []
        for u in (left, right):
            block = np.zeros((8, NX, 128))
            block[:6, 0::2, :64] = u[:, None, :]
            block[:6, 1::2, 64:] = u[:, None, :]
            blocks.append(block.reshape(128, 128))
        matrix = np.concatenate(blocks)
    else:
        matrix = np.repeat(np.concatenate([left, right]), NX, axis=0)
    one, two = parts_of(matrix)
    return np.concatenate([one, two, one, two])


SPREADS = [spread(level) for level in (1, 2, 3)]
Z_SENDS = np.zeros((40, NZ), np.float32)
for _at, _rows in enumerate((PLANS[NZ][2]["left"], PLANS[NZ][2]["right"], *MIRRORS)):
    Z_SENDS[8 * _at : 8 * _at + 6] = _rows
for _at, _rows in enumerate((X_ONE["left"], X_ONE["right"])):
    for _xf in range(2):
        for _f in range(2):
            Z_SENDS[32 + 4 * _at + 2 * _xf + _f, _f * NX : (_f + 1) * NX] = _rows[_xf]

def split(value):
    one = value.astype(jnp.bfloat16).astype(F32)
    return one, value - one


def lanes_of(shape):
    return lax.broadcasted_iota(jnp.int32, shape, 1)


def slots(level, left, right):
    lane = lanes_of(left.shape)
    turn = lambda value, by: pltpu.roll(value, by, 1)
    if level == 1:
        base = left if right is None else jnp.where(lane < 32, left, jnp.where(lane < 64, turn(right, 32), 0.0))
        one, two = split(base)
        return [one + turn(one, 64), two + turn(two, 64)]
    if level == 2:
        one, two = split(jnp.where(lane < 64, left, turn(right, 64)))
        return [one, one, two, two]
    one, two = zip(split(left), split(right))
    return [*one, *one, *two, *two]


def expand(level, arrays, keep, spread_ref):
    factor = jnp.concatenate([jnp.where(keep, a, 0.0).astype(jnp.bfloat16) for a in arrays], axis=1)
    return jnp.dot(factor, spread_ref[...], preferred_element_type=F32)


def kernel(
    vel, spread1_hbm, spread2_hbm, spread3_hbm, sends_hbm,
    o1, q2, q3, x23rl, x23rr, x3rl, x3rr,
    w1, w2, w3, x1rl, x1rr, eg,
    v, y1, y2, y3, z1, z2, z3, t2, t3, t4, ytab, ztab,
    ysl, ysr, yrl, yrr, zsl, zsr, zrl, zrr, zml, zmr,
    htl, htr, g1, g2, g3, u2, u3, p1, p2, p3, csl, csr, zlsl, zlsr, zlml, zlmr,
    x1sl, x1sr, x23sl, x23sr, x3sl, x3sr, xesl, xesr, xerl, xerr,
    spread1, spread2, spread3, sends, zc, zf,
    load_sems, send_sems, recv_sems,
):
    loads = [
        pltpu.make_async_copy(src, dst, load_sems.at[i])
        for i, (src, dst) in enumerate(
            ((vel, v), (sends_hbm, sends), (spread1_hbm, spread1), (spread2_hbm, spread2), (spread3_hbm, spread3))
        )
    ]
    for load in loads:
        load.start()
    near = {
        "yl": neighbour("gy", -1), "yr": neighbour("gy", 1), "zl": neighbour("gz", -1), "zr": neighbour("gz", 1),
        "xl": neighbour("gx", -1), "xr": neighbour("gx", 1), "xll": neighbour("gx", -2), "xrr": neighbour("gx", 2),
    }
    barrier = pltpu.get_barrier_semaphore()
    for device in near.values():
        pl.semaphore_signal(barrier, inc=1, device_id=device, device_id_type=MESH)
    y_places = build_table(ytab, SIDES[NY])
    z_places = build_table(ztab, SIDES[NZ])
    for ref in (yrl, yrr, ysl, ysr):
        ref[pl.ds(Y_ROWS, 32), :] = jnp.zeros((32, 128), F32)
    eg[...] = jnp.zeros((128, 128), F32)

    def remote(index, src, dst, to):
        return pltpu.make_async_remote_copy(
            src_ref=src,
            dst_ref=dst,
            send_sem=send_sems.at[index],
            recv_sem=recv_sems.at[index],
            device_id=near[to],
            device_id_type=MESH,
        )

    loads[0].wait()

    for h in range(2):
        head = [v[pl.ds(h * 8 * NY + k, 8, stride=NY), :] for k in range(21)]
        tail = [v[pl.ds(h * 8 * NY + k, 8, stride=NY), :] for k in range(NY - 28, NY)]
        for f in range(6):
            ysl[pl.ds(f * NX + 8 * h, 8), :] = fir(SEND_LEFT[NY][f][:21], head)
            ysr[pl.ds(f * NX + 8 * h, 8), :] = fir(SEND_RIGHT[NY][f][-28:], tail)

    loads[1].wait()
    for at, ref in enumerate((ysl, ysr)):
        sums = jnp.dot(
            sends[pl.ds(0, 16), :], ref[...].T, precision=lax.Precision.HIGHEST, preferred_element_type=F32
        )
        csl[pl.ds(8 * at, 8), :] = sums[:8]
        csr[pl.ds(8 * at, 8), :] = sums[8:]
    corners = []
    for at in range(2):
        corners.append(remote(4 + at, csl.at[pl.ds(8 * at, 8)], zc.at[pl.ds(16 * at, 8)], "zl"))
        corners.append(remote(16 + at, csr.at[pl.ds(8 * at, 8)], zc.at[pl.ds(16 * at + 8, 8)], "zr"))
    pl.semaphore_wait(barrier, len(near))
    for copy in corners:
        copy.start()
    y_left = remote(0, ysl.at[pl.ds(0, Y_ROWS)], yrr.at[pl.ds(0, Y_ROWS)], "yl")
    y_right = remote(1, ysr.at[pl.ds(0, Y_ROWS)], yrl.at[pl.ds(0, Y_ROWS)], "yr")
    y_left.start()
    y_right.start()

    def lift_y(x, c):
        lift_rows(v, x * NY, NY, y1, x * NY)
        lift_rows(y1, x * NY, NY // 2, y2, x * (NY // 2))
        lift_rows(y2, x * (NY // 2), NY // 4, y3, x * (NY // 4))
        own = {"own_left": ysl, "own_right": ysr}
        for level, ref in ((1, y2), (2, y3)):
            correct(ref, x * (NY >> level), SIDES[NY][level], y_places[level], ytab, own, lambda f: f * NX + x)
        return c

    lax.fori_loop(0, NX, lift_y, 0, unroll=2)
    def turn_one(x, c):
        for t in range(2):
            z1[pl.ds(x * 256 + 128 * t, 128), :] = y1[pl.ds(x * NY + 128 * t, 128), :].T
        return c

    def turn_two(x, c):
        z2[pl.ds(x * 128, 128), :] = y2[pl.ds(x * 128, 128), :].T
        return c

    def turn_three(p, c):
        z3[pl.ds(p * 128, 128), :] = y3[pl.ds(p * 128, 128), :].T
        return c

    def z_sums(level, load_row, store):
        rows = {}

        def row(k):
            if k not in rows:
                rows[k] = load_row(k)
            return rows[k]

        for f in range(2 * level):
            for at, ref in enumerate((zsl, zsr, zml, zmr)):
                weights = [float(c) for c in Z_SENDS[8 * at + f]]
                ks = [k for k in range(NZ) if weights[k] != 0.0]
                store(ref, f, fir([weights[k] for k in ks], [row(k) for k in ks]))

    lax.fori_loop(0, NX // 2, turn_three, 0, unroll=8)
    lax.fori_loop(0, NX, turn_two, 0, unroll=16)

    def store_three(ref, f, value):
        ref[pl.ds(Z_THREE + f * (NX // 2), 8), :] = value

    z_sums(3, lambda k: z3[pl.ds(k, 8, stride=128), :], store_three)
    for h in range(2):

        def store_two(ref, f, value, h=h):
            ref[pl.ds(Z_TWO + f * NX + 8 * h, 8), :] = value

        z_sums(2, lambda k, h=h: z2[pl.ds(h * 8 * 128 + k, 8, stride=128), :], store_two)
    deep = pl.ds(Z_TWO, Z_ROWS - Z_TWO)
    z_left = remote(2, zsl.at[deep], zrr.at[deep], "zl")
    z_right = remote(3, zsr.at[deep], zrl.at[deep], "zr")
    z_left.start()
    z_right.start()

    def lift_z1(i, c):
        lift_rows(z1, i * NZ, NZ, w1, i * NZ)
        return c

    lax.fori_loop(0, NX, turn_one, 0, unroll=8)
    for copy in corners:
        copy.wait()
    zf_left = remote(18, zc.at[pl.ds(0, 16)], zf.at[pl.ds(0, 16)], "yl")
    zf_right = remote(19, zc.at[pl.ds(16, 16)], zf.at[pl.ds(16, 16)], "yr")
    zf_left.start()
    zf_right.start()
    lax.fori_loop(0, 6, lift_z1, 0, unroll=6)
    lax.fori_loop(24, 32, lift_z1, 0, unroll=4)

    def sums_one(g, c):
        rows = [w1[pl.ds(x * 256 + 8 * g, 8), :] for x in (0, 1, 2, 12, 13, 14, 15)]
        for f in range(2):
            x1sl[pl.ds(f * 256 + 8 * g, 8), :] = fir(X_ONE_LEFT[f][:3], rows[:3])
            x1sr[pl.ds(f * 256 + 8 * g, 8), :] = fir(X_ONE_RIGHT[f][12:], rows[3:])
        return c

    lax.fori_loop(0, 32, sums_one, 0, unroll=4)
    x1_left = remote(6, x1sl, x1rr, "xl")
    x1_right = remote(7, x1sr, x1rl, "xr")
    x1_left.start()
    x1_right.start()
    for h in range(2):
        for t in range(2):

            def store_one(ref, f, value, h=h, t=t):
                ref[pl.ds((f * 2 + t) * NX + 8 * h, 8), :] = value

            z_sums(1, lambda k, h=h, t=t: z1[pl.ds(h * 8 * 256 + t * 128 + k, 8, stride=256), :], store_one)
    first = pl.ds(0, Z_TWO)
    z1_left = remote(14, zsl.at[first], zrr.at[first], "zl")
    z1_right = remote(15, zsr.at[first], zrl.at[first], "zr")
    z1_left.start()
    z1_right.start()

    row_one = lambda x, t: lambda f: (f * 2 + t) * NX + x
    row_two = lambda x: lambda f: Z_TWO + f * NX + x
    row_three = lambda p: lambda f: Z_THREE + f * (NX // 2) + p
    z_own = {"own_left": zsl, "own_right": zsr}

    def lift_z2(x, c):
        lift_rows(z2, x * NZ, NZ, t2, x * 64, keep_high=False)
        lift_rows(t2, x * 64, 64, w2, x * 64)
        correct(w2, x * 64, SIDES[NZ][1], z_places[1], ztab, z_own, row_two(x))
        return c

    def lift_z3(p, c):
        lift_rows(z3, p * NZ, NZ, t3, p * 64, keep_high=False)
        lift_rows(t3, p * 64, 64, t4, p * 32, keep_high=False)
        lift_rows(t4, p * 32, 32, w3, p * 32)
        correct(w3, p * 32, SIDES[NZ][2], z_places[2], ztab, z_own, row_three(p))
        return c

    lax.fori_loop(0, NX // 2, lift_z3, 0, unroll=4)
    lax.fori_loop(0, NX, lift_z2, 0, unroll=4)

    y_left.wait()
    y_right.wait()
    for load in loads[2:]:
        load.wait()
    htl[...] = yrl[...].T
    htr[...] = yrr[...].T
    for at, ref in ((0, htl), (8, htr)):
        sums = jnp.dot(sends[pl.ds(0, 32), :], ref[...], precision=lax.Precision.HIGHEST, preferred_element_type=F32)
        for i, out in enumerate((zlsl, zlsr, zlml, zlmr)):
            out[pl.ds(at, 8), :] = sums[8 * i : 8 * i + 8]
    for i, ref in enumerate((htl, htr)):
        lift_rows(ref, 0, 128, g1, 128 * i)
        lift_rows(g1, 128 * i, 64, u2, 64 * i)
        lift_rows(u2, 64 * i, 32, u3, 32 * i)
    for i in range(2):
        own = {"own_left": zlsl, "own_right": zlsr}
        g2[pl.ds(64 * i, 64), :] = u2[pl.ds(64 * i, 64), :]
        g3[pl.ds(32 * i, 32), :] = u3[pl.ds(32 * i, 32), :]
        correct(g2, 64 * i, SIDES[NZ][1], z_places[1], ztab, own, lambda f, i=i: 8 * i + f)
        correct(g3, 32 * i, SIDES[NZ][2], z_places[2], ztab, own, lambda f, i=i: 8 * i + f)
    for level, g, p, n in ((1, g1, p1, 128), (2, g2, p2, 64), (3, g3, p3, 32)):
        for i, value in enumerate(slots(level, g[pl.ds(0, n), :], g[pl.ds(n, n), :])):
            p[pl.ds(n * i, n), :] = value

    sums = lax.dot_general(
        sends[pl.ds(32, 8), :],
        g1[...],
        (((1,), (1,)), ((), ())),
        precision=lax.Precision.HIGHEST,
        preferred_element_type=F32,
    )
    for way, ref in enumerate((xesl, xesr)):
        for xf in range(2):
            for side in range(2):
                at = 4 * way + 2 * xf
                ref[pl.ds(16 + 4 * xf + 2 * side, 2), :] = sums[at : at + 2, 128 * side : 128 * side + 128]
    xg_left = remote(20, xesl.at[pl.ds(16, 8)], xerr.at[pl.ds(16, 8)], "xl")
    xg_right = remote(21, xesr.at[pl.ds(16, 8)], xerl.at[pl.ds(16, 8)], "xr")
    xg_left.start()
    xg_right.start()

    def spread_one(x, c):
        keep = (lanes_of((128, 128)) & 15) == x
        value = expand(1, [p1[pl.ds(128 * i, 128), :] for i in range(2)], keep, spread1)
        for t in range(2):
            at = pl.ds(x * 256 + 128 * t, 128)
            w1[at, :] = w1[at, :] + value[:, 128 * t : 128 * t + 128]
        return c

    def spread_two(x, c):
        keep = (lanes_of((64, 128)) & 15) == x
        at = pl.ds(x * 64, 64)
        w2[at, :] = w2[at, :] + expand(2, [p2[pl.ds(64 * i, 64), :] for i in range(4)], keep, spread2)
        return c

    def spread_three(p, c):
        keep = ((lanes_of((32, 128)) & 15) >> 1) == p
        at = pl.ds(p * 32, 32)
        w3[at, :] = w3[at, :] + expand(3, [p3[pl.ds(32 * i, 32), :] for i in range(8)], keep, spread3)
        return c

    lax.fori_loop(0, NX // 2, spread_three, 0, unroll=8)
    lax.fori_loop(0, NX, spread_two, 0, unroll=16)

    for copy in (z_left, z_right, zf_left, zf_right):
        copy.wait()
    gz = lax.axis_index("gz")

    @pl.when(gz == 0)
    def _():
        zrl[deep, :] = zml[deep, :]
        zf[pl.ds(24, 8), :] = zlml[pl.ds(0, 8), :]
        zf[pl.ds(8, 8), :] = zlml[pl.ds(8, 8), :]

    @pl.when(gz == SIZES["gz"] - 1)
    def _():
        zrr[deep, :] = zmr[deep, :]
        zf[pl.ds(16, 8), :] = zlmr[pl.ds(0, 8), :]
        zf[pl.ds(0, 8), :] = zlmr[pl.ds(8, 8), :]

    def complete(level):
        lane, sub = lanes_of((16, 128)), lax.broadcasted_iota(jnp.int32, (16, 128), 0)
        count = NX // 2 if level == 3 else NX
        keep = ((lane[:8] & 15) >> 1) == sub[:8] if level == 3 else (lane & 15) == sub
        tall = []
        for at in (8, 0):
            arrays = slots(level, zf[pl.ds(16 + at, 8), :], zf[pl.ds(at, 8), :])
            tall.append([
                jnp.concatenate([jnp.where(keep, a[f : f + 1], 0.0) for f in range(2 * level)], axis=0) for a in arrays
            ])
        both = [jnp.concatenate(pair, axis=0) for pair in zip(*tall)]
        value = expand(level, both, jnp.full(both[0].shape, True), (spread1, spread2, spread3)[level - 1])
        for side, ref in enumerate((zrl, zrr)):
            for f in range(2 * level):
                first_row = (side * 2 * level + f) * count
                piece = value[first_row : first_row + count]
                if level == 1:
                    for t in range(2):
                        at = pl.ds((f * 2 + t) * NX, NX)
                        ref[at, :] = ref[at, :] + piece[:, 128 * t : 128 * t + 128]
                else:
                    at = pl.ds((Z_TWO if level == 2 else Z_THREE) + f * count, count)
                    ref[at, :] = ref[at, :] + piece

    complete(3)
    complete(2)

    for copy in (z1_left, z1_right):
        copy.wait()

    @pl.when(gz == 0)
    def _():
        zrl[first, :] = zml[first, :]

    @pl.when(gz == SIZES["gz"] - 1)
    def _():
        zrr[first, :] = zmr[first, :]

    complete(1)

    for side, ref in enumerate((zrl, zrr)):
        for f in range(2):
            for t in range(2):
                rows = [ref[pl.ds((f * 2 + t) * NX + x, 1), :] for x in (0, 1, 2, 12, 13, 14, 15)]
                for xf in range(2):
                    at = pl.ds((xf * 2 + t) * 4 + side * 2 + f, 1)
                    xesl[at, :] = fir(X_ONE_LEFT[xf][:3], rows[:3])
                    xesr[at, :] = fir(X_ONE_RIGHT[xf][12:], rows[3:])
    xe_left = remote(8, xesl.at[pl.ds(0, 16)], xerr.at[pl.ds(0, 16)], "xl")
    xe_right = remote(9, xesr.at[pl.ds(0, 16)], xerl.at[pl.ds(0, 16)], "xr")
    xe_left.start()
    xe_right.start()

    z_past = {"from_left": zrl, "from_right": zrr}

    def finish_z2(x, c):
        correct(w2, x * 64, SIDES[NZ][1], z_places[1], ztab, z_past, row_two(x))
        return c

    def finish_z3(p, c):
        correct(w3, p * 32, SIDES[NZ][2], z_places[2], ztab, z_past, row_three(p))
        return c

    lax.fori_loop(0, NX // 2, finish_z3, 0, unroll=8)
    lax.fori_loop(0, NX, finish_z2, 0, unroll=16)

    three_to = ((x23sr, N_TWO * 64), (x23sl, N_TWO * 64), (x3sr, 0), (x3sl, 0))

    def sums_two(g, c):
        rows = [w2[pl.ds(x * 64 + 8 * g, 8), :] for x in range(NX)]
        for f in range(N_TWO):
            x23sl[pl.ds(f * 64 + 8 * g, 8), :] = fir(X_TWO_LEFT[f], rows)
            x23sr[pl.ds(f * 64 + 8 * g, 8), :] = fir(X_TWO_RIGHT[f], rows)
        return c

    def send_three(g, c):
        rows = [w3[pl.ds(p * 32 + 8 * g, 8), :] for p in range(NX // 2)]
        for (ref, at), block in zip(three_to, (1, 3, 0, 4)):
            for h, value in enumerate(sums_three(X_THREE[block], rows)):
                ref[pl.ds(at + 32 * h + 8 * g, 8), :] = value
        return c

    lax.fori_loop(0, 8, sums_two, 0, unroll=8)
    lax.fori_loop(0, 4, send_three, 0, unroll=4)
    x23_left = remote(10, x23sl, x23rr, "xl")
    x23_right = remote(11, x23sr, x23rl, "xr")
    x3_left = remote(12, x3sl, x3rr, "xll")
    x3_right = remote(13, x3sr, x3rl, "xrr")
    for copy in (x23_left, x23_right, x3_left, x3_right):
        copy.start()

    def finish_z1(x, c):
        for t in range(2):
            correct(w1, x * 256 + 128 * t, SIDES[NZ][0], z_places[0], ztab, z_past, row_one(x, t))
        return c

    lax.fori_loop(6, 24, lift_z1, 0, unroll=6)
    lax.fori_loop(0, NX, spread_one, 0, unroll=4)
    lax.fori_loop(0, NX, finish_z1, 0)
    def own_two(g, c):
        rows = [w2[pl.ds(x * 64 + 8 * g, 8), :] for x in range(NX)]
        for i in range(8):
            q2[pl.ds(i * 64 + 8 * g, 8), :] = fir(X_TWO_OWN[i], rows)
        return c

    def own_three(g, c):
        rows = [w3[pl.ds(p * 32 + 8 * g, 8), :] for p in range(NX // 2)]
        for h, value in enumerate(sums_three(X_THREE[2], rows)):
            q3[pl.ds(32 * h + 8 * g, 8), :] = value
        return c

    lax.fori_loop(0, 8, own_two, 0, unroll=2)
    lax.fori_loop(0, 4, own_three, 0, unroll=2)
    for copy in (x1_left, x1_right, xg_left, xg_right, xe_left, xe_right):
        copy.wait()
    for side, ends in enumerate((xerl, xerr)):
        for xf in range(2):
            for h in range(4):
                eg[pl.ds(NX * h + 2 * side + xf, 1), :] = ends[pl.ds(16 + 4 * xf + h, 1), :]
    arrays = slots(1, eg[...].T, None)
    for side, ref in enumerate((x1rl, x1rr)):
        for xf in range(2):
            value = expand(1, arrays, (lanes_of((128, 128)) & 15) == 2 * side + xf, spread1)
            for t in range(2):
                at = pl.ds(xf * 256 + 128 * t, 128)
                ref[at, :] = ref[at, :] + value[:, 128 * t : 128 * t + 128]
    for xf in range(2):
        for t in range(2):
            for ref, ends in ((x1rl, xerl), (x1rr, xerr)):
                at = (xf * 2 + t) * 4
                refs = {"from_left": ends.at[pl.ds(at, 2)], "from_right": ends.at[pl.ds(at + 2, 2)]}
                correct(ref, xf * 256 + 128 * t, SIDES[NZ][0], z_places[0], ztab, refs, lambda f: f)
    for hy in range(2):
        for hz in range(2):

            def out_one(g, c, hy=hy, hz=hz):
                row = 128 * hy + 64 * hz + 8 * g
                rows = [w1[pl.ds(x * 256 + row, 8), :] for x in range(NX)]
                left = [x1rl[pl.ds(f * 256 + row, 8), :] for f in range(2)]
                right = [x1rr[pl.ds(f * 256 + row, 8), :] for f in range(2)]
                for i, value in enumerate(lift_major(rows)):
                    hx = i // 8
                    band = 4 * hx + 2 * hy + hz
                    if not band:
                        continue
                    value = fir([1.0] + X_ONE_FROM_LEFT[i] + X_ONE_FROM_RIGHT[i], [value] + left + right)
                    value = value * (SCALES[0][hx] * SCALES[0][hy] * SCALES[0][hz])
                    o1[pl.ds((band - 1) * 512 + (i % 8) * 64 + 8 * g, 8), :] = value
                return c

            lax.fori_loop(0, 8, out_one, 0, unroll=2)
    for copy in (x23_left, x23_right, x3_left, x3_right):
        copy.wait()


def paired(weights, rows):
    low_lanes = lanes_of((8, 128)) < 64
    total = jnp.zeros((8, 128), F32)
    for p in range(NX // 2):
        if weights[2 * p] == 0.0 and weights[2 * p + 1] == 0.0:
            continue
        total = total + jnp.where(low_lanes, weights[2 * p], weights[2 * p + 1]) * rows[p]
    return total + pltpu.roll(total, 64, 1)


def sums_three(matrix, rows):
    low_lanes = lanes_of((8, 128)) < 64
    return [jnp.where(low_lanes, paired(matrix[2 * h], rows), paired(matrix[2 * h + 1], rows)) for h in range(2)]


def write(o1, q2, q3, x23rl, x23rr, x3rl, x3rr, out1, out2, out3, out4, o2, o3, o4, sems):
    copies = []

    def send(src, dst):
        copies.append(pltpu.make_async_copy(src, dst, sems.at[len(copies)]))
        copies[-1].start()

    for band in range(7):
        at = pl.ds(band * 512, 512)
        send(o1.at[at], out1.at[at])
    lane = lanes_of((8, 128))
    low_lanes = lane < 64

    def out_three(g, hz):
        high_y = (lane & 63) >= 32
        for hx in range(2):
            value = q3[pl.ds(32 * hx + 8 * g, 8), :]
            for ref, at in ((x23rl, N_TWO * 64), (x23rr, N_TWO * 64), (x3rl, 0), (x3rr, 0)):
                value = value + ref[pl.ds(at + 32 * hx + 8 * g, 8), :]
            scale = SCALES[2][hx] * SCALES[2][hz]
            value = value * jnp.where(high_y, scale * SCALES[2][1], scale * SCALES[2][0])
            for q in range(4):
                i, hy = divmod(q, 2)
                band = 4 * hx + 2 * hy + hz
                row = 16 * i + 8 * (g % 2)
                piece = value[:, 32 * q : 32 * q + 32]
                if band:
                    o3[pl.ds((band - 1) * 32 + row, 8), :] = piece
                else:
                    o4[pl.ds(row, 8), :] = piece

    for g in range(4):
        out_three(g, g // 2)
    send(o3, out3)
    send(o4, out4)

    def out_two(g, hz):
        left = [x23rl[pl.ds(f * 64 + 8 * g, 8), :] for f in range(N_TWO)]
        right = [x23rr[pl.ds(f * 64 + 8 * g, 8), :] for f in range(N_TWO)]
        for i in range(8):
            hx = i // 4
            own = q2[pl.ds(i * 64 + 8 * g, 8), :]
            value = fir([1.0] + X_TWO_FROM_LEFT[i] + X_TWO_FROM_RIGHT[i], [own] + left + right)
            scale = SCALES[1][hx] * SCALES[1][hz]
            value = value * jnp.where(low_lanes, scale * SCALES[1][0], scale * SCALES[1][1])
            for hy in range(2):
                band = 4 * hx + 2 * hy + hz
                if band:
                    at = (band - 1) * 128 + (i % 4) * 32 + 8 * (g % 4)
                    o2[pl.ds(at, 8), :] = value[:, 64 * hy : 64 * hy + 64]

    for g in range(8):
        out_two(g, g // 4)
    send(o2, out2)
    for copy in copies:
        copy.wait()


def shards(velocity):
    vmem, hbm = pl.BlockSpec(memory_space=pltpu.VMEM), pl.BlockSpec(memory_space=pltpu.HBM)
    wide = lambda rows: pltpu.VMEM((rows, 128), F32)
    shapes = [(7 * 8 * 64, 128), (7 * 4 * 32, 64), (7 * 2 * 16, 32), (2 * 16, 32)]
    results = [7 * 8 * 64, 512, 64, X23_ROWS, X23_ROWS, 64, 64]
    scratch = [32 * NZ, 16 * 64, 8 * 32, 512, 512, 128]
    scratch += [16 * NY, 16 * NY, 16 * NY // 2, 16 * NY // 4]
    scratch += [32 * NZ, 16 * NZ, 8 * NZ]
    scratch += [16 * 64, 8 * 64, 8 * 32]
    scratch += [table_rows(SIDES[NY]), table_rows(SIDES[NZ])]
    scratch += [128] * 4 + [Z_ROWS] * 6
    scratch += [128, 128, 256, 128, 64, 128, 64, 2 * 128, 4 * 64, 8 * 32] + [16] * 6
    scratch += [512] * 2 + [X23_ROWS] * 2 + [64] * 2 + [24] * 4
    operands = [velocity.reshape(NX * NY, NZ), *[jnp.asarray(matrix) for matrix in SPREADS], jnp.asarray(Z_SENDS)]
    got = pl.pallas_call(
        kernel,
        out_shape=[jax.ShapeDtypeStruct((rows, 128), F32) for rows in results],
        in_specs=[hbm] * 5,
        out_specs=[vmem] * len(results),
        scratch_shapes=[wide(rows) for rows in scratch]
        + [pltpu.VMEM(matrix.shape, jnp.bfloat16) for matrix in SPREADS]
        + [wide(rows) for rows in (40, 32, 32)]
        + [pltpu.SemaphoreType.DMA((5,)), pltpu.SemaphoreType.DMA((22,)), pltpu.SemaphoreType.DMA((22,))],
        compiler_params=pltpu.CompilerParams(collective_id=0, has_side_effects=True, vmem_limit_bytes=28 * 2**20),
    )(*[pltpu.with_memory_space_constraint(a, pltpu.HBM) for a in operands])
    out1, out2, out3, out4 = pl.pallas_call(
        write,
        out_shape=[jax.ShapeDtypeStruct(shape, F32) for shape in shapes],
        in_specs=[vmem] * len(results),
        out_specs=[hbm] * 4,
        scratch_shapes=[pltpu.VMEM(shape, F32) for shape in shapes[1:]] + [pltpu.SemaphoreType.DMA((10,))],
        compiler_params=pltpu.CompilerParams(vmem_limit_bytes=16 * 2**20),
    )(*got)
    return (
        out1.reshape(7, 8, 64, 128).transpose(0, 1, 3, 2),
        out2.reshape(7, 4, 32, 64).transpose(0, 1, 3, 2),
        out3.reshape(7, 2, 16, 32).transpose(0, 1, 3, 2),
        out4.reshape(2, 16, 32).transpose(0, 2, 1),
    )


def solution(mesh):
    return jax.shard_map(
        shards,
        mesh=mesh,
        in_specs=(P("gx", "gy", "gz"),),
        out_specs=(
            P(None, "gx", "gy", "gz"),
            P(None, "gx", "gy", "gz"),
            P(None, "gx", "gy", "gz"),
            P("gx", "gy", "gz"),
        ),
        check_vma=False,
    )
```

```python
import math

import jax
import jax.numpy as jnp
import ml_dtypes
import numpy as np
from jax import lax
from jax.experimental import pallas as pl
from jax.experimental.pallas import tpu as pltpu
from jax.sharding import PartitionSpec as P

ALPHA = -1.586134342059924
BETA = -0.052980118572961
GAMMA = 0.882911075530934
DELTA = 0.443506852043971
SCALE_LOW = math.sqrt(2.0) / 1.230174104914001
SCALE_HIGH = 1.230174104914001 / math.sqrt(2.0)


def lift_matrix(rows, edges):
    s, d = rows[0::2], rows[1::2]
    none = np.zeros_like(s[:1])
    if edges == "periodic":
        d = d + ALPHA * (s + np.roll(s, -1, 0))
        s = s + BETA * (np.roll(d, 1, 0) + d)
        d = d + GAMMA * (s + np.roll(s, -1, 0))
        s = s + DELTA * (np.roll(d, 1, 0) + d)
        return s, d
    start, end = edges
    up = lambda v, last: np.concatenate([v[1:], last])
    down = lambda v, first: np.concatenate([first, v[:-1]])
    d1 = d + ALPHA * (s + up(s, s[-1:] if end else none))
    before1 = d1[:1] if start else ALPHA * s[:1]
    s1 = s + BETA * (down(d1, before1) + d1)
    d2 = d1 + GAMMA * (s1 + up(s1, s1[-1:] if end else BETA * d1[-1:]))
    before2 = d2[:1] if start else before1 + GAMMA * (BETA * before1 + s1[:1])
    return s1 + DELTA * (down(d2, before2) + d2), d2


def path_matrix(rows, level, edges):
    for _ in range(level):
        rows, high = lift_matrix(rows, edges)
    return np.concatenate([rows, high])


def outgoing(n):
    rows, left, right = np.eye(n), [], []
    for _ in range(3):
        s, d = rows[0::2], rows[1::2]
        left += [s[0], s[0] + BETA * (d[0] + ALPHA * (s[0] + s[1]))]
        right += [d[-1] + ALPHA * s[-1], s[-1] + BETA * (d[-2] + ALPHA * (s[-2] + s[-1]))]
        rows = lift_matrix(rows, (False, False))[0]
    return np.stack(left), np.stack(right)


def line_blocks(n, level):
    m = n >> level
    rows = np.eye(5 * n)
    for _ in range(level):
        rows, high = lift_matrix(rows, "periodic")
    whole = np.concatenate([rows[2 * m : 3 * m], high[2 * m : 3 * m]])
    return [whole[:, k * n : (k + 1) * n] for k in range(5)]


def solved(target, basis):
    u = np.linalg.lstsq(basis.T, target.T, rcond=None)[0].T
    assert np.abs(u @ basis - target).max() < 1e-9
    return np.where(np.abs(u) < 1e-10, 0.0, u)


def block_plan(n, level):
    left, right = outgoing(n)
    left, right = left[: 2 * level], right[: 2 * level]
    blocks = line_blocks(n, level)
    alone = path_matrix(np.eye(n), level, (False, False))
    from_left = solved(blocks[1], right)
    from_right = solved(blocks[3], left)
    own = solved(blocks[2] - alone, np.concatenate([left, right]))
    return dict(left=left, right=right, alone=alone, from_left=from_left, from_right=from_right, own_left=own[:, : 2 * level], own_right=own[:, 2 * level :])


def mirror_plan(n, plans):
    out = []
    for start in (True, False):
        uses, rests = [], []
        for level, plan in enumerate(plans, 1):
            m = n >> level
            rows = np.eye(4 * n)
            for _ in range(level):
                rows, high = lift_matrix(rows, (True, True))
            at = 0 if start else 3
            whole = np.concatenate([rows[at * m : (at + 1) * m], high[at * m : (at + 1) * m]])
            whole = whole[:, at * n : (at + 1) * n]
            rests.append(whole - plan["alone"] - plan["own_left"] @ plan["left"] - plan["own_right"] @ plan["right"])
            u = plan["from_left"] if start else plan["from_right"]
            uses.append(np.pad(u, ((0, 0), (0, 6 - u.shape[1]))))
        use, rest = np.concatenate(uses), np.concatenate(rests)
        g = np.linalg.lstsq(use, rest, rcond=None)[0]
        assert np.abs(use @ g - rest).max() < 1e-9
        out.append(np.where(np.abs(g) < 1e-10, 0.0, g))
    return out


MESH = pl.DeviceIdType.MESH
SIZES = {"gx": 8, "gy": 4, "gz": 4}
NX, NY, NZ = 16, 256, 128
F32 = jnp.float32


def rounded(matrix):
    return [[float(np.float32(c)) if abs(c) > 1e-10 else 0.0 for c in row] for row in matrix]


def fir(weights, rows):
    total = None
    for weight, row in zip(weights, rows):
        if weight == 0.0:
            continue
        term = row() if callable(row) else row
        term = term if weight == 1.0 else weight * term
        total = term if total is None else total + term
    return total


def lift_list(s, d, up, down, first, last):
    before1 = ALPHA * first(s)
    d1 = [b + ALPHA * (a + c) for a, b, c in zip(s, d, up(s, None))]
    s1 = [a + BETA * (b + c) for a, b, c in zip(s, d1, down(d1, before1))]
    d2 = [b + GAMMA * (a + c) for a, b, c in zip(s1, d1, up(s1, BETA * last(d1)))]
    before2 = before1 + GAMMA * (BETA * before1 + first(s1))
    s2 = [a + DELTA * (b + c) for a, b, c in zip(s1, d2, down(d2, before2))]
    return s2, d2


def lift_rows(src, base, n, dst, to, keep_high=True):
    k = n // 16
    s = [src[pl.ds(base + 16 * i, 8, stride=2), :] for i in range(k)]
    d = [src[pl.ds(base + 16 * i + 1, 8, stride=2), :] for i in range(k)]
    sub = lax.broadcasted_iota(jnp.int32, (8, 128), 0)
    top, bottom = sub == 0, sub == 7

    def up(v, fill):
        r = [pltpu.roll(x, 7, 0) for x in v]
        fill = jnp.zeros((8, 128), F32) if fill is None else fill
        return [jnp.where(bottom, r[i + 1] if i + 1 < k else fill, r[i]) for i in range(k)]

    def down(v, fill):
        r = [pltpu.roll(x, 1, 0) for x in v]
        return [jnp.where(top, r[i - 1] if i else fill, r[i]) for i in range(k)]

    low, high = lift_list(s, d, up, down, lambda v: v[0], lambda v: v[-1])
    for i in range(k):
        dst[pl.ds(to + 8 * i, 8), :] = low[i]
        if keep_high:
            dst[pl.ds(to + 8 * (k + i), 8), :] = high[i]


def lift_major(rows):
    low, high = lift_list(
        rows[0::2],
        rows[1::2],
        lambda v, fill: v[1:] + [jnp.zeros_like(v[0]) if fill is None else fill],
        lambda v, fill: [fill] + v[:-1],
        lambda v: v[0],
        lambda v: v[-1],
    )
    return low + high


class Side:
    def __init__(self, plan):
        self.groups = {}
        for source in ("from_left", "from_right", "own_left", "own_right"):
            u = plan[source]
            for g in range(u.shape[0] // 8):
                for f in range(u.shape[1]):
                    column = u[8 * g : 8 * g + 8, f]
                    if np.abs(column).max() > 1e-10:
                        self.groups.setdefault(g, []).append((source, f, column))


PLANS = {n: [block_plan(n, level) for level in (1, 2, 3)] for n in (NY, NZ)}
SIDES = {n: [Side(plan) for plan in PLANS[n]] for n in (NY, NZ)}
MIRRORS = mirror_plan(NZ, PLANS[NZ])
SEND_LEFT = {n: rounded(PLANS[n][2]["left"]) for n in (NY, NZ)}
SEND_RIGHT = {n: rounded(PLANS[n][2]["right"]) for n in (NY, NZ)}
SCALES = [(SCALE_LOW**level, SCALE_LOW ** (level - 1) * SCALE_HIGH) for level in (1, 2, 3)]


def factored(matrix):
    u, size, v = np.linalg.svd(matrix, full_matrices=False)
    rank = int((size > 1e-9).sum())
    return rounded(u[:, :rank] * size[:rank]), rounded(v[:rank])


X_ONE = block_plan(NX, 1)
X_ONE_LEFT, X_ONE_RIGHT = rounded(X_ONE["left"]), rounded(X_ONE["right"])
X_ONE_FROM_LEFT, X_ONE_FROM_RIGHT = rounded(X_ONE["from_left"]), rounded(X_ONE["from_right"])
X_TWO_BLOCKS = line_blocks(NX, 2)
X_TWO_FROM_LEFT, X_TWO_RIGHT = factored(X_TWO_BLOCKS[1])
X_TWO_FROM_RIGHT, X_TWO_LEFT = factored(X_TWO_BLOCKS[3])
X_TWO_OWN = rounded(X_TWO_BLOCKS[2])
X_THREE = [rounded(block) for block in line_blocks(NX, 3)]
X_FAR_FROM_LEFT, X_FAR_RIGHT = factored(line_blocks(NX, 3)[0])
X_FAR_FROM_RIGHT, X_FAR_LEFT = factored(line_blocks(NX, 3)[4])
N_TWO = len(X_TWO_RIGHT)

Y_ROWS = 6 * NX
Z_TWO, Z_THREE, Z_ROWS = 4 * NX, 8 * NX, 8 * NX + 6 * (NX // 2)
X23_ROWS = N_TWO * 64 + 64


def neighbour(axis, step):
    size = SIZES[axis]
    place = {name: lax.axis_index(name) for name in SIZES}
    place[axis] = lax.rem(place[axis] + (step + size), size)
    return tuple(place[name] for name in ("gx", "gy", "gz"))


def build_table(table, sides):
    sub = lax.broadcasted_iota(jnp.int32, (8, 128), 0)
    found = []
    at = 0
    for side in sides:
        places = {}
        for g, terms in side.groups.items():
            for source, f, column in terms:
                value = jnp.zeros((8, 128), F32)
                for i in range(8):
                    if abs(column[i]) > 1e-10:
                        value = jnp.where(sub == i, float(np.float32(column[i])), value)
                table[pl.ds(at, 8), :] = value
                places[g, source, f] = at
                at += 8
        found.append(places)
    return found


def table_rows(sides):
    return 8 * sum(len(terms) for side in sides for terms in side.groups.values())


def correct(ref, base, side, places, table, refs, row):
    for g, terms in side.groups.items():
        terms = [(source, f) for source, f, _ in terms if source in refs]
        if not terms:
            continue
        value = ref[pl.ds(base + 8 * g, 8), :]
        for source, f in terms:
            value = value + table[pl.ds(places[g, source, f], 8), :] * refs[source][pl.ds(row(f), 1), :]
        ref[pl.ds(base + 8 * g, 8), :] = value


def parts_of(value):
    rest, parts = np.asarray(value, np.float32), []
    for _ in range(2):
        part = rest.astype(ml_dtypes.bfloat16)
        parts.append(part)
        rest = rest - part.astype(np.float32)
    return parts


def spread(level):
    plan = PLANS[NY][level - 1]
    left, right = plan["from_left"].T, plan["from_right"].T
    if level == 3:
        blocks = []
        for u in (left, right):
            block = np.zeros((8, NX, 128))
            block[:6, 0::2, :64] = u[:, None, :]
            block[:6, 1::2, 64:] = u[:, None, :]
            blocks.append(block.reshape(128, 128))
        matrix = np.concatenate(blocks)
    else:
        matrix = np.repeat(np.concatenate([left, right]), NX, axis=0)
    one, two = parts_of(matrix)
    return np.concatenate([one, two, one, two])


SPREADS = [spread(level) for level in (1, 2, 3)]
Z_SENDS = np.zeros((40, NZ), np.float32)
for _at, _rows in enumerate((PLANS[NZ][2]["left"], PLANS[NZ][2]["right"], *MIRRORS)):
    Z_SENDS[8 * _at : 8 * _at + 6] = _rows
for _at, _rows in enumerate((X_ONE["left"], X_ONE["right"])):
    for _xf in range(2):
        for _f in range(2):
            Z_SENDS[32 + 4 * _at + 2 * _xf + _f, _f * NX : (_f + 1) * NX] = _rows[_xf]

def split(value):
    one = value.astype(jnp.bfloat16).astype(F32)
    return one, value - one


def lanes_of(shape):
    return lax.broadcasted_iota(jnp.int32, shape, 1)


def slots(level, left, right):
    lane = lanes_of(left.shape)
    turn = lambda value, by: pltpu.roll(value, by, 1)
    if level == 1:
        base = left if right is None else jnp.where(lane < 32, left, jnp.where(lane < 64, turn(right, 32), 0.0))
        one, two = split(base)
        return [one + turn(one, 64), two + turn(two, 64)]
    if level == 2:
        one, two = split(jnp.where(lane < 64, left, turn(right, 64)))
        return [one, one, two, two]
    one, two = zip(split(left), split(right))
    return [*one, *one, *two, *two]


def expand(level, arrays, keep, spread_ref):
    factor = jnp.concatenate([jnp.where(keep, a, 0.0).astype(jnp.bfloat16) for a in arrays], axis=1)
    return jnp.dot(factor, spread_ref[...], preferred_element_type=F32)


def kernel(
    vel, spread1_hbm, spread2_hbm, spread3_hbm, sends_hbm,
    o1, q2, q3, x23rl, x23rr, x3rl, x3rr,
    w1, w2, w3, x1rl, x1rr, eg,
    v, y1, y2, y3, z1, z2, z3, t2, t3, t4, ytab, ztab,
    ysl, ysr, yrl, yrr, zsl, zsr, zrl, zrr, zml, zmr,
    htl, htr, g1, g2, g3, u2, u3, p1, p2, p3, csl, csr, zlsl, zlsr, zlml, zlmr,
    x1sl, x1sr, x23sl, x23sr, x3sl, x3sr, xesl, xesr, xerl, xerr,
    spread1, spread2, spread3, sends, zc, zf,
    load_sems, send_sems, recv_sems,
):
    loads = [
        pltpu.make_async_copy(src, dst, load_sems.at[i])
        for i, (src, dst) in enumerate(
            ((vel, v), (sends_hbm, sends), (spread1_hbm, spread1), (spread2_hbm, spread2), (spread3_hbm, spread3))
        )
    ]
    for load in loads:
        load.start()
    near = {
        "yl": neighbour("gy", -1), "yr": neighbour("gy", 1), "zl": neighbour("gz", -1), "zr": neighbour("gz", 1),
        "xl": neighbour("gx", -1), "xr": neighbour("gx", 1), "xll": neighbour("gx", -2), "xrr": neighbour("gx", 2),
    }
    barrier = pltpu.get_barrier_semaphore()
    for device in near.values():
        pl.semaphore_signal(barrier, inc=1, device_id=device, device_id_type=MESH)
    y_places = build_table(ytab, SIDES[NY])
    z_places = build_table(ztab, SIDES[NZ])
    for ref in (yrl, yrr, ysl, ysr):
        ref[pl.ds(Y_ROWS, 32), :] = jnp.zeros((32, 128), F32)
    eg[...] = jnp.zeros((128, 128), F32)

    def remote(index, src, dst, to):
        return pltpu.make_async_remote_copy(
            src_ref=src,
            dst_ref=dst,
            send_sem=send_sems.at[index],
            recv_sem=recv_sems.at[index],
            device_id=near[to],
            device_id_type=MESH,
        )

    loads[0].wait()

    for h in range(2):
        head = [v[pl.ds(h * 8 * NY + k, 8, stride=NY), :] for k in range(21)]
        tail = [v[pl.ds(h * 8 * NY + k, 8, stride=NY), :] for k in range(NY - 28, NY)]
        for f in range(6):
            ysl[pl.ds(f * NX + 8 * h, 8), :] = fir(SEND_LEFT[NY][f][:21], head)
            ysr[pl.ds(f * NX + 8 * h, 8), :] = fir(SEND_RIGHT[NY][f][-28:], tail)

    loads[1].wait()
    for at, ref in enumerate((ysl, ysr)):
        sums = jnp.dot(
            sends[pl.ds(0, 16), :], ref[...].T, precision=lax.Precision.HIGHEST, preferred_element_type=F32
        )
        csl[pl.ds(8 * at, 8), :] = sums[:8]
        csr[pl.ds(8 * at, 8), :] = sums[8:]
    corners = []
    for at in range(2):
        corners.append(remote(4 + at, csl.at[pl.ds(8 * at, 8)], zc.at[pl.ds(16 * at, 8)], "zl"))
        corners.append(remote(16 + at, csr.at[pl.ds(8 * at, 8)], zc.at[pl.ds(16 * at + 8, 8)], "zr"))
    pl.semaphore_wait(barrier, len(near))
    for copy in corners:
        copy.start()
    y_left = remote(0, ysl.at[pl.ds(0, Y_ROWS)], yrr.at[pl.ds(0, Y_ROWS)], "yl")
    y_right = remote(1, ysr.at[pl.ds(0, Y_ROWS)], yrl.at[pl.ds(0, Y_ROWS)], "yr")
    y_left.start()
    y_right.start()

    def lift_y(x, c):
        lift_rows(v, x * NY, NY, y1, x * NY)
        lift_rows(y1, x * NY, NY // 2, y2, x * (NY // 2))
        lift_rows(y2, x * (NY // 2), NY // 4, y3, x * (NY // 4))
        own = {"own_left": ysl, "own_right": ysr}
        for level, ref in ((1, y2), (2, y3)):
            correct(ref, x * (NY >> level), SIDES[NY][level], y_places[level], ytab, own, lambda f: f * NX + x)
        return c

    lax.fori_loop(0, NX, lift_y, 0, unroll=2)
    def turn_one(x, c):
        for t in range(2):
            z1[pl.ds(x * 256 + 128 * t, 128), :] = y1[pl.ds(x * NY + 128 * t, 128), :].T
        return c

    def turn_two(x, c):
        z2[pl.ds(x * 128, 128), :] = y2[pl.ds(x * 128, 128), :].T
        return c

    def turn_three(p, c):
        z3[pl.ds(p * 128, 128), :] = y3[pl.ds(p * 128, 128), :].T
        return c

    def z_sums(level, load_row, store):
        rows = {}

        def row(k):
            if k not in rows:
                rows[k] = load_row(k)
            return rows[k]

        for f in range(2 * level):
            for at, ref in enumerate((zsl, zsr, zml, zmr)):
                weights = [float(c) for c in Z_SENDS[8 * at + f]]
                ks = [k for k in range(NZ) if weights[k] != 0.0]
                store(ref, f, fir([weights[k] for k in ks], [row(k) for k in ks]))

    lax.fori_loop(0, NX // 2, turn_three, 0, unroll=8)
    lax.fori_loop(0, NX, turn_two, 0, unroll=16)

    def store_three(ref, f, value):
        ref[pl.ds(Z_THREE + f * (NX // 2), 8), :] = value

    z_sums(3, lambda k: z3[pl.ds(k, 8, stride=128), :], store_three)
    for h in range(2):

        def store_two(ref, f, value, h=h):
            ref[pl.ds(Z_TWO + f * NX + 8 * h, 8), :] = value

        z_sums(2, lambda k, h=h: z2[pl.ds(h * 8 * 128 + k, 8, stride=128), :], store_two)
    deep = pl.ds(Z_TWO, Z_ROWS - Z_TWO)
    z_left = remote(2, zsl.at[deep], zrr.at[deep], "zl")
    z_right = remote(3, zsr.at[deep], zrl.at[deep], "zr")
    z_left.start()
    z_right.start()

    def lift_z1(i, c):
        lift_rows(z1, i * NZ, NZ, w1, i * NZ)
        return c

    lax.fori_loop(0, NX, turn_one, 0, unroll=8)
    for copy in corners:
        copy.wait()
    zf_left = remote(18, zc.at[pl.ds(0, 16)], zf.at[pl.ds(0, 16)], "yl")
    zf_right = remote(19, zc.at[pl.ds(16, 16)], zf.at[pl.ds(16, 16)], "yr")
    zf_left.start()
    zf_right.start()
    lax.fori_loop(0, 6, lift_z1, 0, unroll=6)
    lax.fori_loop(24, 32, lift_z1, 0, unroll=4)

    def sums_one(g, c):
        rows = [w1[pl.ds(x * 256 + 8 * g, 8), :] for x in (0, 1, 2, 12, 13, 14, 15)]
        for f in range(2):
            x1sl[pl.ds(f * 256 + 8 * g, 8), :] = fir(X_ONE_LEFT[f][:3], rows[:3])
            x1sr[pl.ds(f * 256 + 8 * g, 8), :] = fir(X_ONE_RIGHT[f][12:], rows[3:])
        return c

    lax.fori_loop(0, 32, sums_one, 0, unroll=4)
    x1_left = remote(6, x1sl, x1rr, "xl")
    x1_right = remote(7, x1sr, x1rl, "xr")
    x1_left.start()
    x1_right.start()
    for h in range(2):
        for t in range(2):

            def store_one(ref, f, value, h=h, t=t):
                ref[pl.ds((f * 2 + t) * NX + 8 * h, 8), :] = value

            z_sums(1, lambda k, h=h, t=t: z1[pl.ds(h * 8 * 256 + t * 128 + k, 8, stride=256), :], store_one)
    first = pl.ds(0, Z_TWO)
    z1_left = remote(14, zsl.at[first], zrr.at[first], "zl")
    z1_right = remote(15, zsr.at[first], zrl.at[first], "zr")
    z1_left.start()
    z1_right.start()

    row_one = lambda x, t: lambda f: (f * 2 + t) * NX + x
    row_two = lambda x: lambda f: Z_TWO + f * NX + x
    row_three = lambda p: lambda f: Z_THREE + f * (NX // 2) + p
    z_own = {"own_left": zsl, "own_right": zsr}

    def lift_z2(x, c):
        lift_rows(z2, x * NZ, NZ, t2, x * 64, keep_high=False)
        lift_rows(t2, x * 64, 64, w2, x * 64)
        correct(w2, x * 64, SIDES[NZ][1], z_places[1], ztab, z_own, row_two(x))
        return c

    def lift_z3(p, c):
        lift_rows(z3, p * NZ, NZ, t3, p * 64, keep_high=False)
        lift_rows(t3, p * 64, 64, t4, p * 32, keep_high=False)
        lift_rows(t4, p * 32, 32, w3, p * 32)
        correct(w3, p * 32, SIDES[NZ][2], z_places[2], ztab, z_own, row_three(p))
        return c

    lax.fori_loop(0, NX // 2, lift_z3, 0, unroll=4)
    lax.fori_loop(0, NX, lift_z2, 0, unroll=4)

    y_left.wait()
    y_right.wait()
    for load in loads[2:]:
        load.wait()
    htl[...] = yrl[...].T
    htr[...] = yrr[...].T
    for at, ref in ((0, htl), (8, htr)):
        sums = jnp.dot(sends[pl.ds(0, 32), :], ref[...], precision=lax.Precision.HIGHEST, preferred_element_type=F32)
        for i, out in enumerate((zlsl, zlsr, zlml, zlmr)):
            out[pl.ds(at, 8), :] = sums[8 * i : 8 * i + 8]
    for i, ref in enumerate((htl, htr)):
        lift_rows(ref, 0, 128, g1, 128 * i)
        lift_rows(g1, 128 * i, 64, u2, 64 * i)
        lift_rows(u2, 64 * i, 32, u3, 32 * i)
    for i in range(2):
        own = {"own_left": zlsl, "own_right": zlsr}
        g2[pl.ds(64 * i, 64), :] = u2[pl.ds(64 * i, 64), :]
        g3[pl.ds(32 * i, 32), :] = u3[pl.ds(32 * i, 32), :]
        correct(g2, 64 * i, SIDES[NZ][1], z_places[1], ztab, own, lambda f, i=i: 8 * i + f)
        correct(g3, 32 * i, SIDES[NZ][2], z_places[2], ztab, own, lambda f, i=i: 8 * i + f)
    for level, g, p, n in ((1, g1, p1, 128), (2, g2, p2, 64), (3, g3, p3, 32)):
        for i, value in enumerate(slots(level, g[pl.ds(0, n), :], g[pl.ds(n, n), :])):
            p[pl.ds(n * i, n), :] = value

    sums = lax.dot_general(
        sends[pl.ds(32, 8), :],
        g1[...],
        (((1,), (1,)), ((), ())),
        precision=lax.Precision.HIGHEST,
        preferred_element_type=F32,
    )
    for way, ref in enumerate((xesl, xesr)):
        for xf in range(2):
            for side in range(2):
                at = 4 * way + 2 * xf
                ref[pl.ds(16 + 4 * xf + 2 * side, 2), :] = sums[at : at + 2, 128 * side : 128 * side + 128]
    xg_left = remote(20, xesl.at[pl.ds(16, 8)], xerr.at[pl.ds(16, 8)], "xl")
    xg_right = remote(21, xesr.at[pl.ds(16, 8)], xerl.at[pl.ds(16, 8)], "xr")
    xg_left.start()
    xg_right.start()

    def spread_one(x, c):
        keep = (lanes_of((128, 128)) & 15) == x
        value = expand(1, [p1[pl.ds(128 * i, 128), :] for i in range(2)], keep, spread1)
        for t in range(2):
            at = pl.ds(x * 256 + 128 * t, 128)
            w1[at, :] = w1[at, :] + value[:, 128 * t : 128 * t + 128]
        return c

    def spread_two(x, c):
        keep = (lanes_of((64, 128)) & 15) == x
        at = pl.ds(x * 64, 64)
        w2[at, :] = w2[at, :] + expand(2, [p2[pl.ds(64 * i, 64), :] for i in range(4)], keep, spread2)
        return c

    def spread_three(p, c):
        keep = ((lanes_of((32, 128)) & 15) >> 1) == p
        at = pl.ds(p * 32, 32)
        w3[at, :] = w3[at, :] + expand(3, [p3[pl.ds(32 * i, 32), :] for i in range(8)], keep, spread3)
        return c

    lax.fori_loop(0, NX // 2, spread_three, 0, unroll=8)
    lax.fori_loop(0, NX, spread_two, 0, unroll=16)

    for copy in (z_left, z_right, zf_left, zf_right):
        copy.wait()
    gz = lax.axis_index("gz")

    @pl.when(gz == 0)
    def _():
        zrl[deep, :] = zml[deep, :]
        zf[pl.ds(24, 8), :] = zlml[pl.ds(0, 8), :]
        zf[pl.ds(8, 8), :] = zlml[pl.ds(8, 8), :]

    @pl.when(gz == SIZES["gz"] - 1)
    def _():
        zrr[deep, :] = zmr[deep, :]
        zf[pl.ds(16, 8), :] = zlmr[pl.ds(0, 8), :]
        zf[pl.ds(0, 8), :] = zlmr[pl.ds(8, 8), :]

    def complete(level):
        lane, sub = lanes_of((16, 128)), lax.broadcasted_iota(jnp.int32, (16, 128), 0)
        count = NX // 2 if level == 3 else NX
        keep = ((lane[:8] & 15) >> 1) == sub[:8] if level == 3 else (lane & 15) == sub
        tall = []
        for at in (8, 0):
            arrays = slots(level, zf[pl.ds(16 + at, 8), :], zf[pl.ds(at, 8), :])
            tall.append([
                jnp.concatenate([jnp.where(keep, a[f : f + 1], 0.0) for f in range(2 * level)], axis=0) for a in arrays
            ])
        both = [jnp.concatenate(pair, axis=0) for pair in zip(*tall)]
        value = expand(level, both, jnp.full(both[0].shape, True), (spread1, spread2, spread3)[level - 1])
        for side, ref in enumerate((zrl, zrr)):
            for f in range(2 * level):
                first_row = (side * 2 * level + f) * count
                piece = value[first_row : first_row + count]
                if level == 1:
                    for t in range(2):
                        at = pl.ds((f * 2 + t) * NX, NX)
                        ref[at, :] = ref[at, :] + piece[:, 128 * t : 128 * t + 128]
                else:
                    at = pl.ds((Z_TWO if level == 2 else Z_THREE) + f * count, count)
                    ref[at, :] = ref[at, :] + piece

    complete(3)
    complete(2)

    for copy in (z1_left, z1_right):
        copy.wait()

    @pl.when(gz == 0)
    def _():
        zrl[first, :] = zml[first, :]

    @pl.when(gz == SIZES["gz"] - 1)
    def _():
        zrr[first, :] = zmr[first, :]

    complete(1)

    for side, ref in enumerate((zrl, zrr)):
        for f in range(2):
            for t in range(2):
                rows = [ref[pl.ds((f * 2 + t) * NX + x, 1), :] for x in (0, 1, 2, 12, 13, 14, 15)]
                for xf in range(2):
                    at = pl.ds((xf * 2 + t) * 4 + side * 2 + f, 1)
                    xesl[at, :] = fir(X_ONE_LEFT[xf][:3], rows[:3])
                    xesr[at, :] = fir(X_ONE_RIGHT[xf][12:], rows[3:])
    xe_left = remote(8, xesl.at[pl.ds(0, 16)], xerr.at[pl.ds(0, 16)], "xl")
    xe_right = remote(9, xesr.at[pl.ds(0, 16)], xerl.at[pl.ds(0, 16)], "xr")
    xe_left.start()
    xe_right.start()

    z_past = {"from_left": zrl, "from_right": zrr}

    def finish_z2(x, c):
        correct(w2, x * 64, SIDES[NZ][1], z_places[1], ztab, z_past, row_two(x))
        return c

    def finish_z3(p, c):
        correct(w3, p * 32, SIDES[NZ][2], z_places[2], ztab, z_past, row_three(p))
        return c

    lax.fori_loop(0, NX // 2, finish_z3, 0, unroll=8)
    lax.fori_loop(0, NX, finish_z2, 0, unroll=16)

    three_to = ((x23sr, N_TWO * 64), (x23sl, N_TWO * 64))

    def sums_two(g, c):
        rows = [w2[pl.ds(x * 64 + 8 * g, 8), :] for x in range(NX)]
        for f in range(N_TWO):
            x23sl[pl.ds(f * 64 + 8 * g, 8), :] = fir(X_TWO_LEFT[f], rows)
            x23sr[pl.ds(f * 64 + 8 * g, 8), :] = fir(X_TWO_RIGHT[f], rows)
        return c

    def send_three(g, c):
        rows = [w3[pl.ds(p * 32 + 8 * g, 8), :] for p in range(NX // 2)]
        for (ref, at), block in zip(three_to, (1, 3)):
            for h, value in enumerate(sums_three(X_THREE[block], rows)):
                ref[pl.ds(at + 32 * h + 8 * g, 8), :] = value
        low_lanes = lanes_of((8, 128)) < 64
        for ref, sums in ((x3sr, X_FAR_RIGHT), (x3sl, X_FAR_LEFT)):
            ref[pl.ds(8 * g, 8), :] = jnp.where(low_lanes, paired(sums[0], rows), paired(sums[-1], rows))
        return c

    lax.fori_loop(0, 8, sums_two, 0, unroll=8)
    lax.fori_loop(0, 4, send_three, 0, unroll=4)
    x23_left = remote(10, x23sl, x23rr, "xl")
    x23_right = remote(11, x23sr, x23rl, "xr")
    x3_left = remote(12, x3sl, x3rr, "xll")
    x3_right = remote(13, x3sr, x3rl, "xrr")
    for copy in (x23_left, x23_right, x3_left, x3_right):
        copy.start()

    def finish_z1(x, c):
        for t in range(2):
            correct(w1, x * 256 + 128 * t, SIDES[NZ][0], z_places[0], ztab, z_past, row_one(x, t))
        return c

    lax.fori_loop(6, 24, lift_z1, 0, unroll=6)
    lax.fori_loop(0, NX, spread_one, 0, unroll=4)
    lax.fori_loop(0, NX, finish_z1, 0)
    def own_two(g, c):
        rows = [w2[pl.ds(x * 64 + 8 * g, 8), :] for x in range(NX)]
        for i in range(8):
            q2[pl.ds(i * 64 + 8 * g, 8), :] = fir(X_TWO_OWN[i], rows)
        return c

    def own_three(g, c):
        rows = [w3[pl.ds(p * 32 + 8 * g, 8), :] for p in range(NX // 2)]
        for h, value in enumerate(sums_three(X_THREE[2], rows)):
            q3[pl.ds(32 * h + 8 * g, 8), :] = value
        return c

    lax.fori_loop(0, 8, own_two, 0, unroll=2)
    lax.fori_loop(0, 4, own_three, 0, unroll=2)
    for copy in (x1_left, x1_right, xg_left, xg_right, xe_left, xe_right):
        copy.wait()
    for side, ends in enumerate((xerl, xerr)):
        for xf in range(2):
            for h in range(4):
                eg[pl.ds(NX * h + 2 * side + xf, 1), :] = ends[pl.ds(16 + 4 * xf + h, 1), :]
    arrays = slots(1, eg[...].T, None)
    for side, ref in enumerate((x1rl, x1rr)):
        for xf in range(2):
            value = expand(1, arrays, (lanes_of((128, 128)) & 15) == 2 * side + xf, spread1)
            for t in range(2):
                at = pl.ds(xf * 256 + 128 * t, 128)
                ref[at, :] = ref[at, :] + value[:, 128 * t : 128 * t + 128]
    for xf in range(2):
        for t in range(2):
            for ref, ends in ((x1rl, xerl), (x1rr, xerr)):
                at = (xf * 2 + t) * 4
                refs = {"from_left": ends.at[pl.ds(at, 2)], "from_right": ends.at[pl.ds(at + 2, 2)]}
                correct(ref, xf * 256 + 128 * t, SIDES[NZ][0], z_places[0], ztab, refs, lambda f: f)
    for hy in range(2):
        for hz in range(2):

            def out_one(g, c, hy=hy, hz=hz):
                row = 128 * hy + 64 * hz + 8 * g
                rows = [w1[pl.ds(x * 256 + row, 8), :] for x in range(NX)]
                left = [x1rl[pl.ds(f * 256 + row, 8), :] for f in range(2)]
                right = [x1rr[pl.ds(f * 256 + row, 8), :] for f in range(2)]
                for i, value in enumerate(lift_major(rows)):
                    hx = i // 8
                    band = 4 * hx + 2 * hy + hz
                    if not band:
                        continue
                    value = fir([1.0] + X_ONE_FROM_LEFT[i] + X_ONE_FROM_RIGHT[i], [value] + left + right)
                    value = value * (SCALES[0][hx] * SCALES[0][hy] * SCALES[0][hz])
                    o1[pl.ds((band - 1) * 512 + (i % 8) * 64 + 8 * g, 8), :] = value
                return c

            lax.fori_loop(0, 8, out_one, 0, unroll=2)
    for copy in (x23_left, x23_right, x3_left, x3_right):
        copy.wait()


def paired(weights, rows):
    low_lanes = lanes_of((8, 128)) < 64
    total = jnp.zeros((8, 128), F32)
    for p in range(NX // 2):
        if weights[2 * p] == 0.0 and weights[2 * p + 1] == 0.0:
            continue
        total = total + jnp.where(low_lanes, weights[2 * p], weights[2 * p + 1]) * rows[p]
    return total + pltpu.roll(total, 64, 1)


def sums_three(matrix, rows):
    low_lanes = lanes_of((8, 128)) < 64
    return [jnp.where(low_lanes, paired(matrix[2 * h], rows), paired(matrix[2 * h + 1], rows)) for h in range(2)]


def write(o1, q2, q3, x23rl, x23rr, x3rl, x3rr, out1, out2, out3, out4, o2, o3, o4, sems):
    copies = []

    def send(src, dst):
        copies.append(pltpu.make_async_copy(src, dst, sems.at[len(copies)]))
        copies[-1].start()

    for band in range(7):
        at = pl.ds(band * 512, 512)
        send(o1.at[at], out1.at[at])
    lane = lanes_of((8, 128))
    low_lanes = lane < 64

    def out_three(g, hz):
        high_y = (lane & 63) >= 32
        for hx in range(2):
            value = q3[pl.ds(32 * hx + 8 * g, 8), :]
            for ref in (x23rl, x23rr):
                value = value + ref[pl.ds(N_TWO * 64 + 32 * hx + 8 * g, 8), :]
            for ref, uses in ((x3rl, X_FAR_FROM_LEFT), (x3rr, X_FAR_FROM_RIGHT)):
                far, (low, high) = ref[pl.ds(8 * g, 8), :], uses[2 * hx : 2 * hx + 2]
                value = value + jnp.where(low_lanes, low[0], high[-1]) * far
                if len(low) == 2:
                    value = value + jnp.where(low_lanes, low[1], high[0]) * pltpu.roll(far, 64, 1)
            scale = SCALES[2][hx] * SCALES[2][hz]
            value = value * jnp.where(high_y, scale * SCALES[2][1], scale * SCALES[2][0])
            for q in range(4):
                i, hy = divmod(q, 2)
                band = 4 * hx + 2 * hy + hz
                row = 16 * i + 8 * (g % 2)
                piece = value[:, 32 * q : 32 * q + 32]
                if band:
                    o3[pl.ds((band - 1) * 32 + row, 8), :] = piece
                else:
                    o4[pl.ds(row, 8), :] = piece

    for g in range(4):
        out_three(g, g // 2)
    send(o3, out3)
    send(o4, out4)

    def out_two(g, hz):
        left = [x23rl[pl.ds(f * 64 + 8 * g, 8), :] for f in range(N_TWO)]
        right = [x23rr[pl.ds(f * 64 + 8 * g, 8), :] for f in range(N_TWO)]
        for i in range(8):
            hx = i // 4
            own = q2[pl.ds(i * 64 + 8 * g, 8), :]
            value = fir([1.0] + X_TWO_FROM_LEFT[i] + X_TWO_FROM_RIGHT[i], [own] + left + right)
            scale = SCALES[1][hx] * SCALES[1][hz]
            value = value * jnp.where(low_lanes, scale * SCALES[1][0], scale * SCALES[1][1])
            for hy in range(2):
                band = 4 * hx + 2 * hy + hz
                if band:
                    at = (band - 1) * 128 + (i % 4) * 32 + 8 * (g % 4)
                    o2[pl.ds(at, 8), :] = value[:, 64 * hy : 64 * hy + 64]

    for g in range(8):
        out_two(g, g // 4)
    send(o2, out2)
    for copy in copies:
        copy.wait()


def shards(velocity):
    vmem, hbm = pl.BlockSpec(memory_space=pltpu.VMEM), pl.BlockSpec(memory_space=pltpu.HBM)
    wide = lambda rows: pltpu.VMEM((rows, 128), F32)
    shapes = [(7 * 8 * 64, 128), (7 * 4 * 32, 64), (7 * 2 * 16, 32), (2 * 16, 32)]
    results = [7 * 8 * 64, 512, 64, X23_ROWS, X23_ROWS, 32, 32]
    scratch = [32 * NZ, 16 * 64, 8 * 32, 512, 512, 128]
    scratch += [16 * NY, 16 * NY, 16 * NY // 2, 16 * NY // 4]
    scratch += [32 * NZ, 16 * NZ, 8 * NZ]
    scratch += [16 * 64, 8 * 64, 8 * 32]
    scratch += [table_rows(SIDES[NY]), table_rows(SIDES[NZ])]
    scratch += [128] * 4 + [Z_ROWS] * 6
    scratch += [128, 128, 256, 128, 64, 128, 64, 2 * 128, 4 * 64, 8 * 32] + [16] * 6
    scratch += [512] * 2 + [X23_ROWS] * 2 + [32] * 2 + [24] * 4
    operands = [velocity.reshape(NX * NY, NZ), *[jnp.asarray(matrix) for matrix in SPREADS], jnp.asarray(Z_SENDS)]
    got = pl.pallas_call(
        kernel,
        out_shape=[jax.ShapeDtypeStruct((rows, 128), F32) for rows in results],
        in_specs=[hbm] * 5,
        out_specs=[vmem] * len(results),
        scratch_shapes=[wide(rows) for rows in scratch]
        + [pltpu.VMEM(matrix.shape, jnp.bfloat16) for matrix in SPREADS]
        + [wide(rows) for rows in (40, 32, 32)]
        + [pltpu.SemaphoreType.DMA((5,)), pltpu.SemaphoreType.DMA((22,)), pltpu.SemaphoreType.DMA((22,))],
        compiler_params=pltpu.CompilerParams(collective_id=0, has_side_effects=True, vmem_limit_bytes=28 * 2**20),
    )(*[pltpu.with_memory_space_constraint(a, pltpu.HBM) for a in operands])
    out1, out2, out3, out4 = pl.pallas_call(
        write,
        out_shape=[jax.ShapeDtypeStruct(shape, F32) for shape in shapes],
        in_specs=[vmem] * len(results),
        out_specs=[hbm] * 4,
        scratch_shapes=[pltpu.VMEM(shape, F32) for shape in shapes[1:]] + [pltpu.SemaphoreType.DMA((10,))],
        compiler_params=pltpu.CompilerParams(vmem_limit_bytes=16 * 2**20),
    )(*got)
    return (
        out1.reshape(7, 8, 64, 128).transpose(0, 1, 3, 2),
        out2.reshape(7, 4, 32, 64).transpose(0, 1, 3, 2),
        out3.reshape(7, 2, 16, 32).transpose(0, 1, 3, 2),
        out4.reshape(2, 16, 32).transpose(0, 2, 1),
    )


def solution(mesh):
    return jax.shard_map(
        shards,
        mesh=mesh,
        in_specs=(P("gx", "gy", "gz"),),
        out_specs=(
            P(None, "gx", "gy", "gz"),
            P(None, "gx", "gy", "gz"),
            P(None, "gx", "gy", "gz"),
            P("gx", "gy", "gz"),
        ),
        check_vma=False,
    )
```
